256 devices in a mesh: panel: 2 (over x_hi), lat: 8 (over z), lon: 16 (over x_lo, y, core).
Axes of the slice: x: 4 (x_hi: 2, x_lo: 2; x = x_hi * 2 + x_lo), y: 4, z: 8, core: 2. Of those that a mesh axis runs over, the one named last changes fastest.
Arguments:
- state: float32 [2, 128, 256, 8, 128], P('panel', 'lat', 'lon'), may hold values from -6 to 6
- rim_base: int32 [2, 1536, 2], P('panel', ('lat', 'lon')), may hold values from 1 to 253, as said below
- rim_weight: float32 [2, 1536, 16], P('panel', ('lat', 'lon')), may hold values from -0.1 to 0.2
- rim_angle: float32 [2, 1536], P('panel', ('lat', 'lon')), may hold values from -3 to 3
- rim_target: int32 [2, 1536, 2], P('panel'), may hold values from -2 to 257, as said below
Outputs:
- change: float32 [2, 128, 256, 8, 128], P('panel', 'lat', 'lon')
The draws below stay inside these ranges and needn't reach their ends.
Inputs may be any that keep to these rules, and one draw needn't show every extreme that they name: `rim_base`: entry e of panel p names a base cell (row, column) of panel p whose 4 x 4 donor stencil, rows and columns from base - 1 to base + 2, lies inside the panel; the base cell lies in block e // 12 of 16 x 16 cells, blocks numbered row by row with 16 blocks to a row. `rim_target`: the rim of panel q is a loop of 1536 positions: rows -2 and -1 at columns 0 to 256 - 1 (column by column, row -2 first), then columns 256 and 257 at rows 0 to 128 - 1 (row by row), then rows 128 and 129 at columns 255 down to 0, then columns -2 and -1 at rows 127 down to 0. Entry e, with b = e // 12 and i = e % 12, fills loop position (i * 128 + b + o_q) mod 1536, for one offset o_q per panel.
All inputs are finite; a program needn't handle non-finite values.
Results may differ from the reference program's by a relative error of at most 0.00015.
Values sent between devices are 32-bit elements; how exact they have to be, the bound alone decides.
A program may use at most 64 MiB of HBM per device.

```python
import math
import jax
import jax.numpy as jnp
from jax import lax

CT = 16
CP = 16
NR = 128
FIELDS = 8
NTH = 128
NPH = 256
RIM_DEV = 12
NRIM = 1536
N_LAT = 8


def draw_rim_base(key, part):
    lat_blocks = NTH // CT
    lon_blocks = NPH // CP
    entry = jnp.arange(NRIM, dtype=jnp.int32)
    block_id = entry // RIM_DEV
    block_row = block_id // lon_blocks
    block_col = block_id % lon_blocks
    low_row = jnp.where(block_row == 0, 1, 0)
    high_row = jnp.where(block_row == lat_blocks - 1, CT - 2, CT)
    low_col = jnp.where(block_col == 0, 1, 0)
    high_col = jnp.where(block_col == lon_blocks - 1, CP - 2, CP)
    key_row, key_col = jax.random.split(jax.random.fold_in(key, 11))
    row_pick = jax.random.randint(key_row, (2, NRIM), low_row, high_row, dtype=jnp.int32)
    col_pick = jax.random.randint(key_col, (2, NRIM), low_col, high_col, dtype=jnp.int32)
    return jnp.stack([block_row * CT + row_pick, block_col * CP + col_pick], axis=-1).astype(jnp.int32)


def loop_order():
    entry = jnp.arange(NRIM, dtype=jnp.int32)
    block_total = NRIM // RIM_DEV
    return entry % RIM_DEV * block_total + entry // RIM_DEV


def draw_rim_angle(key, part):
    loop_pos = loop_order().astype(jnp.float32)
    key_phase, key_rough = jax.random.split(jax.random.fold_in(key, 31))
    phase = jax.random.uniform(key_phase, (2, 1), jnp.float32, 0.0, 2.0 * math.pi)
    smooth = 2.5 * jnp.sin(2.0 * math.pi * loop_pos[None, :] / NRIM + phase)
    rough = jnp.clip(0.15 * jax.random.normal(key_rough, (2, NRIM), jnp.float32), -0.4, 0.4)
    return (smooth + rough).astype(jnp.float32)


def draw_rim_target(key, part):
    loop_pos = loop_order()
    offset = jax.random.randint(jax.random.fold_in(key, 23), (2, 1), 0, NRIM, dtype=jnp.int32)
    place = (loop_pos[None, :] + offset) % NRIM
    top_band = place < 2 * NPH
    right_ids = place - 2 * NPH
    right_band = (right_ids >= 0) & (right_ids < 2 * NTH)
    bottom_ids = right_ids - 2 * NTH
    bottom_band = (bottom_ids >= 0) & (bottom_ids < 2 * NPH)
    left_ids = bottom_ids - 2 * NPH
    row_ids = jnp.where(top_band, place % 2 - 2, jnp.where(right_band, right_ids // 2, jnp.where(bottom_band, NTH + bottom_ids % 2, NTH - 1 - left_ids // 2)))
    col_ids = jnp.where(top_band, place // 2, jnp.where(right_band, NPH + right_ids % 2, jnp.where(bottom_band, NPH - 1 - bottom_ids // 2, left_ids % 2 - 2)))
    return jnp.stack([row_ids, col_ids], axis=-1).astype(jnp.int32)


def level_of(stream_key, dims, cuts, least, top_value):
    level = 1.0
    for position, shards_of in cuts:
        draws = jax.random.uniform(jax.random.fold_in(jax.random.fold_in(stream_key, 6), position), (shards_of,), jnp.float32, least / len(cuts), top_value / len(cuts))
        level = level * jnp.repeat(jnp.exp(draws), dims[position] // shards_of).reshape((-1,) + (1,) * (len(dims) - 1 - position))
    return level


def gaussian(key, shape, scale, most, pieces=(), kind=jnp.bfloat16):
    gain = level_of(key, shape, pieces, -0.22, 0.18) if pieces else 1.0
    array = jax.random.normal(key, shape, jnp.float32) * scale * gain
    return jnp.minimum(jnp.maximum(array, -most), most).astype(kind)


def setup_inputs(seed: int = 0) -> dict:
    streams_of = jax.random.split(jax.random.key(seed), 6)
    state = gaussian(streams_of[0], (2, NTH, NPH, FIELDS, NR), 1.0, 6.0, ((0, 2), (1, 8), (2, 16)), jnp.float32)
    rim_base = draw_rim_base(jax.random.fold_in(streams_of[5], 71), 0)
    rim_weight = jnp.clip(-0.1 + 0.3 * jax.random.uniform(streams_of[2], (2, NRIM, 16), jnp.float32) ** level_of(streams_of[2], (2, NRIM, 16), ((0, 2), (1, 128)), -0.2, 0.2), -0.1, 0.2)
    rim_angle = draw_rim_angle(jax.random.fold_in(streams_of[5], 71), 0)
    rim_target = draw_rim_target(jax.random.fold_in(streams_of[5], 71), 0)
    return dict(state=state, rim_base=rim_base, rim_weight=rim_weight, rim_angle=rim_angle, rim_target=rim_target)


ETA_COEF = 0.2
NU_COEF = 0.2
KAPPA_COEF = 0.3
SOUND_SQ = 1.0
ARCHIMEDES_LIFT = 0.5
TIME_STEP = 0.2


def grid_geometry(levels, theta_count, phi_count):
    radius_scale = 2.0 * theta_count / math.pi
    radial_step = 0.65 * radius_scale / levels
    radius = 0.35 * radius_scale + (jnp.arange(levels, dtype=jnp.int32).astype(jnp.float32) + 0.5) * radial_step
    return radius, radial_step, math.pi / (2 * theta_count), 1.5 * math.pi / phi_count


def theta_sine(first_row, count, theta_count):
    row_index = first_row + jnp.arange(count, dtype=jnp.int32)
    colatitude = math.pi / 4 + (row_index.astype(jnp.float32) + 0.5) * (math.pi / (2 * theta_count))
    return jnp.sin(colatitude)


def inner_volumes(quantity):
    return quantity[1:-1, 1:-1]


def diff_theta(quantity, spacing):
    return (quantity[2:, 1:-1] - quantity[:-2, 1:-1]) * (0.5 / spacing)


def diff_phi(quantity, spacing):
    return (quantity[1:-1, 2:] - quantity[1:-1, :-2]) * (0.5 / spacing)


def diff_radius(quantity, spacing):
    zero_layer = jnp.zeros(quantity.shape[:-1] + (1,), quantity.dtype)
    upper_part = jnp.concatenate([quantity[..., 1:], zero_layer], axis=-1)
    lower_part = jnp.concatenate([zero_layer, quantity[..., :-1]], axis=-1)
    return (upper_part - lower_part) * (0.5 / spacing)


def curl_of(directional_components, colatitude_factor_list, spherical_layout):
    radius, radial_step, polar_step, azimuth_step = spherical_layout
    radial_part, polar_part, azimuth_part = directional_components
    polar_factor_halfway = colatitude_factor_list[1:-1]
    out_radial = (diff_theta(colatitude_factor_list * azimuth_part, polar_step) - diff_phi(polar_part, azimuth_step)) / (radius * polar_factor_halfway)
    out_polar = (diff_phi(radial_part, azimuth_step) / polar_factor_halfway - diff_radius(inner_volumes(radius * azimuth_part), radial_step)) / radius
    out_azimuth = (diff_radius(inner_volumes(radius * polar_part), radial_step) - diff_theta(radial_part, polar_step)) / radius
    return (out_radial, out_polar, out_azimuth)


def slope_quantity(quantity, colatitude_factor_list, spherical_layout):
    radius, radial_step, polar_step, azimuth_step = spherical_layout
    polar_factor_halfway = colatitude_factor_list[1:-1]
    return (diff_radius(inner_volumes(quantity), radial_step), diff_theta(quantity, polar_step) / radius, diff_phi(quantity, azimuth_step) / (radius * polar_factor_halfway))


def outflow_density(directional_components, colatitude_factor_list, spherical_layout):
    radius, radial_step, polar_step, azimuth_step = spherical_layout
    radial_part, polar_part, azimuth_part = directional_components
    polar_factor_halfway = colatitude_factor_list[1:-1]
    radial_term = diff_radius(inner_volumes(radius * radius * radial_part), radial_step) / (radius * radius)
    return radial_term + (diff_theta(colatitude_factor_list * polar_part, polar_step) + diff_phi(azimuth_part, azimuth_step)) / (radius * polar_factor_halfway)


def cross_product(left, right):
    return (left[1] * right[2] - left[2] * right[1], left[2] * right[0] - left[0] * right[2], left[0] * right[1] - left[1] * right[0])


def dot_product(left, right):
    return left[0] * right[0] + left[1] * right[1] + left[2] * right[2]


def tendency(padded, colatitude_factor_list, spherical_layout):
    directional_components = [padded[:, :, number, :] for number in range(8)]
    velocity = tuple(directional_components[0:3])
    magnetic = tuple(directional_components[3:6])
    warmth_state = directional_components[6]
    pressure = directional_components[7]
    polar_factor_halfway = colatitude_factor_list[1:-1]
    current = curl_of(magnetic, colatitude_factor_list, spherical_layout)
    vorticity = curl_of(velocity, colatitude_factor_list, spherical_layout)
    warmth_slope = slope_quantity(warmth_state, colatitude_factor_list, spherical_layout)
    velocity_mid = tuple(inner_volumes(part) for part in velocity)
    magnetic_mid = tuple(inner_volumes(part) for part in magnetic)
    induced = cross_product(velocity_mid, magnetic_mid)
    electric = tuple(induced[number] - ETA_COEF * current[number] for number in range(3))
    magnetic_rate = curl_of(electric, polar_factor_halfway, spherical_layout)
    vorticity_curl = curl_of(vorticity, polar_factor_halfway, spherical_layout)
    thermal_flux = outflow_density(warmth_slope, polar_factor_halfway, spherical_layout)
    total_head = inner_volumes(pressure) + 0.5 * dot_product(velocity_mid, velocity_mid)
    head_grad = slope_quantity(total_head, polar_factor_halfway, spherical_layout)
    pressure_rate = -SOUND_SQ * outflow_density(velocity_mid, polar_factor_halfway, spherical_layout)
    velocity_in = tuple(inner_volumes(part) for part in velocity_mid)
    magnetic_in = tuple(inner_volumes(part) for part in magnetic_mid)
    current_in = tuple(inner_volumes(part) for part in current)
    vorticity_in = tuple(inner_volumes(part) for part in vorticity)
    slope_heat_entering = tuple(inner_volumes(part) for part in warmth_slope)
    warmth_entering = inner_volumes(inner_volumes(warmth_state))
    lorentz = cross_product(current_in, magnetic_in)
    advect = cross_product(velocity_in, vorticity_in)
    flow_acceleration = [advect[number] + lorentz[number] - head_grad[number] - NU_COEF * vorticity_curl[number] for number in range(3)]
    flow_acceleration[0] = flow_acceleration[0] + ARCHIMEDES_LIFT * warmth_entering
    temp_rate = KAPPA_COEF * thermal_flux - dot_product(velocity_in, slope_heat_entering)
    return jnp.stack(flow_acceleration + list(magnetic_rate) + [temp_rate, pressure_rate], axis=2)


def interpolate(donors, weights, turning):
    mixed = jnp.einsum("ek,ekfr->efr", weights, donors, precision=lax.Precision.HIGHEST)
    cosine = jnp.cos(turning)[:, None]
    sine_turn = jnp.sin(turning)[:, None]
    return jnp.stack([mixed[:, 0], cosine * mixed[:, 1] - sine_turn * mixed[:, 2], sine_turn * mixed[:, 1] + cosine * mixed[:, 2], mixed[:, 3], cosine * mixed[:, 4] - sine_turn * mixed[:, 5], sine_turn * mixed[:, 4] + cosine * mixed[:, 5], mixed[:, 6], mixed[:, 7]], axis=1)


def rim_values(fields, rim_base, rim_weight, rim_angle, donor_panel):
    base_cell = rim_base[donor_panel]
    steps_row = jnp.arange(4, dtype=jnp.int32)
    offsets = ((steps_row[:, None] - 1) * NPH + steps_row[None, :] - 1).reshape(1, 16)
    donor_ids = (base_cell[:, 0] * NPH + base_cell[:, 1])[:, None] + offsets
    flat_cells = fields[donor_panel].reshape(NTH * NPH, fields.shape[3], fields.shape[4])
    return interpolate(flat_cells[donor_ids], rim_weight[donor_panel], rim_angle[donor_panel])


def padded_panel(fields, values, rim_target, panel_id):
    wide_cols = NPH + 4
    frame = jnp.zeros((NTH + 4, wide_cols) + fields.shape[3:], fields.dtype)
    frame = frame.at[2:-2, 2:-2].set(fields[panel_id])
    target = rim_target[panel_id]
    spots = (target[:, 0] + 2) * wide_cols + target[:, 1] + 2
    flat_frame = frame.reshape(((NTH + 4) * wide_cols,) + fields.shape[3:]).at[spots].set(values)
    return flat_frame.reshape((NTH + 4, wide_cols) + fields.shape[3:])


def panel_rate(frame, spherical_layout):
    def one_slab(slab_id):
        first_row = slab_id * CT
        row_slab = lax.dynamic_slice_in_dim(frame, first_row, CT + 4, 0)
        colatitude_factor_list = theta_sine(first_row - 2, CT + 4, NTH)[:, None, None]
        return tendency(row_slab, colatitude_factor_list, spherical_layout)

    slabs = lax.map(one_slab, jnp.arange(N_LAT, dtype=jnp.int32))
    return slabs.reshape((NTH, NPH) + frame.shape[2:])


def rates(fields, rim_base, rim_weight, rim_angle, rim_target, spherical_layout):
    results = []
    for panel_id in range(2):
        values = rim_values(fields, rim_base, rim_weight, rim_angle, 1 - panel_id)
        frame = padded_panel(fields, values, rim_target, panel_id)
        results.append(panel_rate(frame, spherical_layout))
    return jnp.stack(results)


def reference(state, rim_base, rim_weight, rim_angle, rim_target):
    spherical_layout = grid_geometry(NR, NTH, NPH)
    first_rate = rates(state, rim_base, rim_weight, rim_angle, rim_target, spherical_layout)
    middle = state + TIME_STEP * first_rate
    second_rate = rates(middle, rim_base, rim_weight, rim_angle, rim_target, spherical_layout)
    return 0.5 * TIME_STEP * (first_rate + second_rate)
```

```python
import math

import jax
import jax.numpy as jnp
import numpy as np
from jax import lax
from jax.experimental import pallas as pl
from jax.experimental.pallas import tpu as pltpu
from jax.sharding import PartitionSpec as P

NTH, NPH, NR, NF, CB = 128, 256, 128, 8, 16
LAT, LON = NTH // CB, NPH // CB
LOOP = 1536
ENTRIES = 12
ETA = np.float32(0.2)
NU = np.float32(0.2)
KAPPA = np.float32(0.3)
LIFT = np.float32(0.5)
DT = np.float32(0.2)
MESH = pl.DeviceIdType.MESH

DTHETA = math.pi / (2 * NTH)
DPHI = 1.5 * math.pi / NPH
H_THETA = np.float32(0.5 / DTHETA)


def row_table():
    g = np.arange(-4, NTH + 4)
    sine = lambda k: np.sin(math.pi / 4 + (k + 0.5) * DTHETA)
    s = sine(g)
    half = 0.5 / DTHETA
    return np.stack([sine(g + 1) * half / s, sine(g - 1) * half / s, 0.5 / DPHI / s]).astype(
        np.float32
    )


def level_table():
    scale = 2.0 * NTH / math.pi
    dr = 0.65 * scale / NR
    r = 0.35 * scale + (np.arange(NR) + 0.5) * dr
    half = 0.5 / dr
    up = np.where(np.arange(NR) < NR - 1, half, 0.0)
    down = np.where(np.arange(NR) > 0, half, 0.0)
    r_up, r_down = np.roll(r, -1), np.roll(r, 1)
    rows = [
        1 / r,
        up * r_up / r,
        down * r_down / r,
        up,
        down,
        up * r_up**2 / r**2,
        down * r_down**2 / r**2,
        0 * r,
    ]
    return np.stack(rows).astype(np.float32)


def above(x):
    return pltpu.roll(x, NR - 1, 1)


def below(x):
    return pltpu.roll(x, 1, 1)


def cross(a, b):
    return (
        a[1] * b[2] - a[2] * b[1],
        a[2] * b[0] - a[0] * b[2],
        a[0] * b[1] - a[1] * b[0],
    )


def kernel(
    rows, levels, state, base, weight, angle, mine,
    out,
    Y0, Y1, K1, L1, V,
    R00, R01, R10, R11, Q, W00, W01, W10, W11, X00, X01, X10, X11,
    trig, far, off,
    halo_send, halo_recv, a_send, a_recv, b_send, b_recv, x_send, x_recv, misc,
):
    p, a, c = lax.axis_index("panel"), lax.axis_index("lat"), lax.axis_index("lon")
    b = a * LON + c
    Y = (Y0, Y1)
    R = ((R00, R01), (R10, R11))
    W = ((W00, W01), (W10, W11))
    X = ((X00, X01), (X10, X11))

    ri = levels[0:1, :]
    cp, cm = levels[1:2, :], levels[2:3, :]
    dp, dm = levels[3:4, :], levels[4:5, :]
    ep, em = levels[5:6, :], levels[6:7, :]

    steps = [(1, 0), (-1, 0), (0, 1), (0, -1), (1, 1), (1, -1), (-1, 1), (-1, -1)]

    def span(step, extent_src):
        if step == 0:
            return 0, 2, CB
        return (CB - 2, 0, 2) if step > 0 else (0, CB + 2, 2)

    def halo_copy(e, k):
        dr, dc = steps[k]
        r0, rd, rn = span(dr, CB)
        c0, cd, cn = span(dc, CB)
        if e == 0:
            src = state.at[pl.ds(r0, rn), pl.ds(c0, cn)]
        else:
            src = Y[1].at[pl.ds(r0 + 2, rn), pl.ds(c0 + 2, cn)]
        return pltpu.make_async_remote_copy(
            src_ref=src,
            dst_ref=Y[e].at[pl.ds(rd, rn), pl.ds(cd, cn)],
            send_sem=halo_send.at[e, k],
            recv_sem=halo_recv.at[e, k],
            device_id=(p, a + dr, c + dc),
            device_id_type=MESH,
        )

    def exists(dr, dc):
        ok = None
        for pos, d, n in ((a, dr, LAT), (c, dc, LON)):
            if d:
                t = (pos < n - 1) if d > 0 else (pos > 0)
                ok = t if ok is None else jnp.logical_and(ok, t)
        return ok

    def halo_start(e):
        for k, (dr, dc) in enumerate(steps):
            @pl.when(exists(dr, dc))
            def _():
                halo_copy(e, k).start()

    def halo_wait_recv(e):
        for k, (dr, dc) in enumerate(steps):
            @pl.when(exists(-dr, -dc))
            def _():
                halo_copy(e, k).wait_recv()

    def halo_wait_send(e):
        for k, (dr, dc) in enumerate(steps):
            @pl.when(exists(dr, dc))
            def _():
                halo_copy(e, k).wait_send()

    on_top, on_bottom = a == 0, a == LAT - 1
    on_right, on_left = c == LON - 1, c == 0
    active = (jnp.logical_or(on_top, on_bottom), jnp.logical_or(on_right, on_left))
    sign = (jnp.where(on_top, 1, -1), jnp.where(on_right, 1, -1))
    rank = (jnp.where(on_top, c, LON - 1 - c), jnp.where(on_right, a, LAT - 1 - a))
    groups = (LON // 4, LAT // 4)
    member = tuple(lax.rem(u, 4) for u in rank)
    has_next = tuple(u // 4 < n - 1 for u, n in zip(rank, groups))
    has_prev = tuple(u // 4 > 0 for u in rank)

    def along(side, step):
        if side == 0:
            return (p, a, c + sign[0] * step)
        return (p, a + sign[1] * step, c)

    m_src = lax.rem(c, 4)

    def a_copy(e, g):
        if g < 4:
            side, dev = 0, (1 - p, 0, 4 * g + m_src)
        elif g < 6:
            side, dev = 1, (1 - p, 4 * (g - 4) + m_src, LON - 1)
        elif g < 10:
            side, dev = 0, (1 - p, LAT - 1, 39 - 4 * g - m_src)
        else:
            side, dev = 1, (1 - p, 47 - 4 * g - m_src, 0)
        return pltpu.make_async_remote_copy(
            src_ref=V.at[e, g],
            dst_ref=R[e][side].at[4 * a + c // 4],
            send_sem=a_send.at[e],
            recv_sem=a_recv.at[e, side],
            device_id=dev,
            device_id_type=MESH,
        )

    def a_wait_send(e):
        pltpu.make_async_remote_copy(
            src_ref=V.at[e],
            dst_ref=R[e][0].at[pl.ds(0, ENTRIES)],
            send_sem=a_send.at[e],
            recv_sem=a_recv.at[e, 0],
            device_id=(1 - p, a, c),
            device_id_type=MESH,
        ).wait_send()

    def a_wait_recv(e, side):
        pltpu.make_async_remote_copy(
            src_ref=R[e][side],
            dst_ref=R[e][side],
            send_sem=a_send.at[e],
            recv_sem=a_recv.at[e, side],
            device_id=(1 - p, a, c),
            device_id_type=MESH,
        ).wait_recv()

    def b_copy(e, side, s, slot):
        return pltpu.make_async_remote_copy(
            src_ref=Q.at[e, side, pl.ds(8 * s, 10)],
            dst_ref=W[e][side].at[slot],
            send_sem=b_send.at[e, side, s],
            recv_sem=b_recv.at[e, side, slot],
            device_id=along(side, s - member[side]),
            device_id_type=MESH,
        )

    def x_copy(e, side, way):
        return pltpu.make_async_remote_copy(
            src_ref=Q.at[e, side, 32 if way == 0 else 1],
            dst_ref=X[e][side].at[way, member[side]],
            send_sem=x_send.at[e, side, way],
            recv_sem=x_recv.at[e, side, way],
            device_id=along(side, (4 if way == 0 else -1) - member[side]),
            device_id_type=MESH,
        )

    def x_wait_recv(e, side, way):
        pltpu.make_async_remote_copy(
            src_ref=X[e][side].at[way],
            dst_ref=X[e][side].at[way],
            send_sem=x_send.at[e, side, way],
            recv_sem=x_recv.at[e, side, way],
            device_id=along(side, 1),
            device_id_type=MESH,
        ).wait_recv()

    def flat(e):
        return Y[e].reshape(20 * 20 * NF, NR)

    def interpolate(e, o_far):
        turn = (b + o_far) >> 7
        sub = lax.broadcasted_iota(jnp.int32, (NF, NR), 0)
        first = jnp.logical_or(sub == 1, sub == 4)
        second = jnp.logical_or(sub == 2, sub == 5)
        turned = jnp.logical_or(first, second)

        @pl.loop(0, ENTRIES)
        def _(g):
            i = lax.rem(g - turn + 2 * ENTRIES, ENTRIES)
            r0 = jnp.clip(base[i, 0] - a * CB + 1, 1, CB)
            c0 = jnp.clip(base[i, 1] - c * CB + 1, 1, CB)
            parts = []
            for x in range(4):
                acc = None
                for y in range(4):
                    term = weight[i, 4 * x + y] * Y[e][r0 + x, c0 + y]
                    acc = term if acc is None else acc + term
                parts.append(acc)
            m = (parts[0] + parts[1]) + (parts[2] + parts[3])
            cosine = trig[0, pl.ds(i, 1), :]
            sine = trig[1, pl.ds(i, 1), :]
            partner = jnp.where(first, -pltpu.roll(m, NF - 1, 0), pltpu.roll(m, 1, 0))
            V[e, g] = jnp.where(turned, cosine * m + sine * partner, m)

    def side_loop(fn):
        for side in range(2):
            @pl.when(active[side])
            def _():
                fn(side)

    def spread(e, side, o_near):
        shift = (member[side] + o_near) >> 2
        for n in range(34):
            Q[e, side, n] = R[e][side][(n - 1 - shift + LOOP) & 31]
        for s in range(4):
            @pl.when(member[side] != s)
            def _():
                b_copy(e, side, s, member[side]).start()
        for way, has in ((0, has_next), (1, has_prev)):
            @pl.when(has[side])
            def _():
                x_copy(e, side, way).start()
        for n in range(10):
            W[e][side][member[side], n] = Q[e, side, 8 * member[side] + n]

    def spread_wait_send(e, side):
        for s in range(4):
            @pl.when(member[side] != s)
            def _():
                b_copy(e, side, s, member[side]).wait_send()
        for way, has in ((0, has_next), (1, has_prev)):
            @pl.when(has[side])
            def _():
                x_copy(e, side, way).wait_send()

    def collect(e, side, o_near):
        for s in range(4):
            @pl.when(member[side] != s)
            def _():
                b_copy(e, side, 0, s).wait_recv()
        for way, has, edge in ((0, has_prev, 0), (1, has_next, 3)):
            @pl.when(jnp.logical_and(has[side], member[side] == edge))
            def _():
                x_wait_recv(e, side, way)

        def place(cell):
            for rho in range(4):
                who = (rho - o_near + LOOP) & 3
                for n in range(10):
                    value = W[e][side][who, n]
                    if n in (0, 9):
                        way, has, edge = (0, has_prev, 0) if n == 0 else (1, has_next, 3)
                        far_value = jnp.where(has[side], X[e][side][way, who], 0.0)
                        value = jnp.where(member[side] == edge, far_value, value)
                    r, q = cell(2 * n + rho // 2, rho % 2)
                    Y[e][r, q] = value

        cells = (
            ((on_top, lambda h, o: (o, h)), (on_bottom, lambda h, o: (18 + o, 19 - h))),
            ((on_right, lambda h, o: (h, 18 + o)), (on_left, lambda h, o: (19 - h, o))),
        )[side]
        for on, cell in cells:
            @pl.when(on)
            def _():
                place(cell)

    def curl(A, ap, am, bb, br, rh):
        a1, a2 = A(1, 0, 0), A(2, 0, 0)
        return (
            ri * ((A(2, 1, 0) * ap - A(2, -1, 0) * am) - (A(1, 0, 1) - A(1, 0, -1)) * bb),
            (A(0, 0, 1) - A(0, 0, -1)) * br - (above(a2) * cp - below(a2) * cm),
            (above(a1) * cp - below(a1) * cm) - (A(0, 1, 0) - A(0, -1, 0)) * rh,
        )

    rh = ri * H_THETA

    def mid(q, r, k):
        return pl.ds((q * 18 + r) * 24 + k, 8)

    def first_pass(e, i, starts):
        y = flat(e)
        gi = a * CB + i + 3
        ap, am, bb = rows[0, gi], rows[1, gi], rows[2, gi]
        br = ri * bb
        for ic in starts:
            def ld(f, dg, dj):
                return y[pl.ds(((i + 1 + dg) * 20 + ic + 1 + dj) * NF + f, 8, stride=NF), :]

            def U(k, dg, dj):
                return ld(k, dg, dj)

            def B(k, dg, dj):
                return ld(3 + k, dg, dj)

            u = [U(k, 0, 0) for k in range(3)]
            mag = [B(k, 0, 0) for k in range(3)]
            w = curl(U, ap, am, bb, br, rh)
            cur = curl(B, ap, am, bb, br, rh)
            ind = cross(u, mag)
            el = [ind[k] - ETA * cur[k] for k in range(3)]
            t = ld(6, 0, 0)
            grad = [
                above(t) * dp - below(t) * dm,
                (ld(6, 1, 0) - ld(6, -1, 0)) * rh,
                (ld(6, 0, 1) - ld(6, 0, -1)) * br,
            ]
            head = ld(7, 0, 0) + np.float32(0.5) * (u[0] * u[0] + u[1] * u[1] + u[2] * u[2])
            for q, v in enumerate([*w, *cur, *el, *grad, head]):
                L1[mid(q, i, ic), :] = v

    def second_pass(e, i, starts, sink):
        y = flat(e)
        gi = a * CB + i + 4
        ap, am, bb = rows[0, gi], rows[1, gi], rows[2, gi]
        br = ri * bb
        for j in starts:
            def ld(f, dg, dj):
                return y[pl.ds(((i + 2 + dg) * 20 + j + 2 + dj) * NF + f, 8, stride=NF), :]

            def l1(q):
                return lambda k, dg, dj: L1[mid(q + k, i + 1 + dg, j + 1 + dj), :]

            Wv, J, E, T, H = l1(0), l1(3), l1(6), l1(9), l1(12)
            cw = curl(Wv, ap, am, bb, br, rh)
            ce = curl(E, ap, am, bb, br, rh)
            u = [ld(k, 0, 0) for k in range(3)]
            mag = [ld(3 + k, 0, 0) for k in range(3)]
            w = [Wv(k, 0, 0) for k in range(3)]
            cur = [J(k, 0, 0) for k in range(3)]
            adv, lor = cross(u, w), cross(cur, mag)
            h = H(0, 0, 0)
            slope = (
                above(h) * dp - below(h) * dm,
                (H(0, 1, 0) - H(0, -1, 0)) * rh,
                (H(0, 0, 1) - H(0, 0, -1)) * br,
            )
            t0 = T(0, 0, 0)
            lap = (above(t0) * ep - below(t0) * em) + ri * (
                (T(1, 1, 0) * ap - T(1, -1, 0) * am) + (T(2, 0, 1) - T(2, 0, -1)) * bb
            )
            div = (above(u[0]) * ep - below(u[0]) * em) + ri * (
                (ld(1, 1, 0) * ap - ld(1, -1, 0) * am) + (ld(2, 0, 1) - ld(2, 0, -1)) * bb
            )
            ru = [adv[k] + lor[k] - slope[k] - NU * cw[k] for k in range(3)]
            ru[0] = ru[0] + LIFT * ld(6, 0, 0)
            rt = KAPPA * lap - (u[0] * t0 + u[1] * T(1, 0, 0) + u[2] * T(2, 0, 0))
            for f, v in enumerate([*ru, *ce, rt, -div]):
                sink(i, j, f, v)

    y_second = flat(1)
    y_first = flat(0)
    out_flat = out.reshape(CB * CB * NF, NR)

    def keep(i, j, f, v):
        K1[pl.ds((f * CB + i) * CB + j, 8), :] = v
        at = pl.ds(((i + 2) * 20 + j + 2) * NF + f, 8, stride=NF)
        y_second[at, :] = y_first[at, :] + DT * v

    def finish(i, j, f, v):
        k1 = K1[pl.ds((f * CB + i) * CB + j, 8), :]
        out_flat[pl.ds((i * CB + j) * NF + f, 8, stride=NF), :] = np.float32(0.1) * (k1 + v)

    halo_start(0)
    local = pltpu.make_async_copy(state, Y[0].at[pl.ds(2, CB), pl.ds(2, CB)], misc.at[0])
    local.start()
    tell = pltpu.make_async_remote_copy(
        src_ref=mine, dst_ref=far, send_sem=misc.at[1], recv_sem=misc.at[2],
        device_id=(1 - p, a, c), device_id_type=MESH,
    )
    tell.start()
    own_off = pltpu.make_async_copy(mine, off.at[0], misc.at[3])
    own_off.start()

    trig[0] = jnp.zeros((16, NR), jnp.float32)
    for i in range(ENTRIES):
        trig[0, i : i + 1, :] = jnp.full((1, NR), angle[i], jnp.float32)
    turned = trig[0]
    trig[0] = jnp.cos(turned)
    trig[1] = jnp.sin(turned)

    tell.wait_recv()
    far_off = pltpu.make_async_copy(far, off.at[1], misc.at[4])
    far_off.start()
    own_off.wait()
    far_off.wait()
    local.wait()
    o_near = off[0, 0, 0]
    o_far = off[1, 0, 0]

    for e in range(2):
        if e == 1:
            halo_start(1)
        halo_wait_recv(e)
        interpolate(e, o_far)
        for g in range(ENTRIES):
            a_copy(e, g).start()

        def middle(side):
            a_wait_recv(e, side)
            spread(e, side, o_near)

        side_loop(middle)
        side_loop(lambda side: collect(e, side, o_near))

        @pl.loop(0, 18)
        def _(i):
            first_pass(e, i, (0, 8, 10))

        @pl.loop(0, 16)
        def _(i):
            second_pass(e, i, (0, 8), keep if e == 0 else finish)

    tell.wait_send()
    for e in range(2):
        halo_wait_send(e)
        a_wait_send(e)
        side_loop(lambda side: spread_wait_send(e, side))


def loop_place(target):
    row, col = target[0], target[1]
    return jnp.where(
        row < 0,
        2 * col + row + 2,
        jnp.where(
            col >= NPH,
            2 * NPH + 2 * row + col - NPH,
            jnp.where(
                row >= NTH,
                2 * NPH + 2 * NTH + 2 * (NPH - 1 - col) + row - NTH,
                4 * NPH + 2 * NTH + 2 * (NTH - 1 - row) + col + 2,
            ),
        ),
    )


def per_device(state, rim_base, rim_weight, rim_angle, rim_target):
    place = loop_place(rim_target[0, 0])
    mine = jnp.full((8, 128), place, jnp.int32)
    smem = pl.BlockSpec(memory_space=pltpu.SMEM)
    vmem = pl.BlockSpec(memory_space=pltpu.VMEM)
    anywhere = pl.BlockSpec(memory_space=pl.ANY)
    f32 = jnp.float32
    result = pl.pallas_call(
        kernel,
        out_shape=jax.ShapeDtypeStruct((CB, CB, NF, NR), f32),
        in_specs=[smem, vmem, anywhere, smem, smem, smem, anywhere],
        out_specs=vmem,
        scratch_shapes=[
            pltpu.VMEM((20, 20, NF, NR), f32),
            pltpu.VMEM((20, 20, NF, NR), f32),
            pltpu.VMEM((NF * CB * CB, NR), f32),
            pltpu.VMEM((13 * 18 * 24, NR), f32),
            pltpu.VMEM((2, ENTRIES, NF, NR), f32),
            *[pltpu.VMEM((32, NF, NR), f32)] * 4,
            pltpu.VMEM((2, 2, 34, NF, NR), f32),
            *[pltpu.VMEM((4, 10, NF, NR), f32)] * 4,
            *[pltpu.VMEM((2, 4, NF, NR), f32)] * 4,
            pltpu.VMEM((2, 16, NR), f32),
            pltpu.VMEM((8, 128), jnp.int32),
            pltpu.SMEM((2, 8, 128), jnp.int32),
            pltpu.SemaphoreType.DMA((2, 8)),
            pltpu.SemaphoreType.DMA((2, 8)),
            pltpu.SemaphoreType.DMA((2,)),
            pltpu.SemaphoreType.DMA((2, 2)),
            pltpu.SemaphoreType.DMA((2, 2, 4)),
            pltpu.SemaphoreType.DMA((2, 2, 4)),
            pltpu.SemaphoreType.DMA((2, 2, 2)),
            pltpu.SemaphoreType.DMA((2, 2, 2)),
            pltpu.SemaphoreType.DMA((5,)),
        ],
        compiler_params=pltpu.CompilerParams(
            has_side_effects=True, vmem_limit_bytes=40 << 20
        ),
    )(
        jnp.asarray(row_table()),
        jnp.asarray(level_table()),
        state[0],
        rim_base[0],
        rim_weight[0],
        rim_angle[0],
        mine,
    )
    return result[None]


def solution(mesh):
    return jax.shard_map(
        per_device,
        mesh=mesh,
        in_specs=(
            P("panel", "lat", "lon", None, None),
            P("panel", ("lat", "lon"), None),
            P("panel", ("lat", "lon"), None),
            P("panel", ("lat", "lon")),
            P("panel", None, None),
        ),
        out_specs=P("panel", "lat", "lon", None, None),
        check_vma=False,
    )
```

```python
import math

import jax
import jax.numpy as jnp
import numpy as np
from jax import lax
from jax.experimental import pallas as pl
from jax.experimental.pallas import tpu as pltpu
from jax.sharding import PartitionSpec as P

NTH, NPH, NR, NF, CB = 128, 256, 128, 8, 16
LAT, LON = NTH // CB, NPH // CB
LOOP = 1536
ENTRIES = 12
ETA = np.float32(0.2)
NU = np.float32(0.2)
KAPPA = np.float32(0.3)
LIFT = np.float32(0.5)
DT = np.float32(0.2)
MESH = pl.DeviceIdType.MESH

DTHETA = math.pi / (2 * NTH)
DPHI = 1.5 * math.pi / NPH
H_THETA = np.float32(0.5 / DTHETA)


def row_table():
    g = np.arange(-4, NTH + 4)
    sine = lambda k: np.sin(math.pi / 4 + (k + 0.5) * DTHETA)
    s = sine(g)
    half = 0.5 / DTHETA
    return np.stack([sine(g + 1) * half / s, sine(g - 1) * half / s, 0.5 / DPHI / s]).astype(
        np.float32
    )


def level_table():
    scale = 2.0 * NTH / math.pi
    dr = 0.65 * scale / NR
    r = 0.35 * scale + (np.arange(NR) + 0.5) * dr
    half = 0.5 / dr
    up = np.where(np.arange(NR) < NR - 1, half, 0.0)
    down = np.where(np.arange(NR) > 0, half, 0.0)
    r_up, r_down = np.roll(r, -1), np.roll(r, 1)
    rows = [
        1 / r,
        up * r_up / r,
        down * r_down / r,
        up,
        down,
        up * r_up**2 / r**2,
        down * r_down**2 / r**2,
        0 * r,
    ]
    return np.stack(rows).astype(np.float32)


def above(x):
    return pltpu.roll(x, NR - 1, 1)


def below(x):
    return pltpu.roll(x, 1, 1)


def cross(a, b):
    return (
        a[1] * b[2] - a[2] * b[1],
        a[2] * b[0] - a[0] * b[2],
        a[0] * b[1] - a[1] * b[0],
    )


def kernel(
    rows, levels, state, base_hbm, weight_hbm, angle_hbm, target_hbm,
    out,
    Y0, Y1, K1, L1, V,
    R00, R01, R10, R11, Q, W00, W01, W10, W11, X00, X01, X10, X11,
    trig, far, base, weight, angle, near_at, far_at, rows_s,
    halo_send, halo_recv, a_send, a_recv, b_send, b_recv, x_send, x_recv, misc,
):
    p, a, c = lax.axis_index("panel"), lax.axis_index("lat"), lax.axis_index("lon")
    b = a * LON + c
    Y = (Y0, Y1)
    R = ((R00, R01), (R10, R11))
    W = ((W00, W01), (W10, W11))
    X = ((X00, X01), (X10, X11))

    ri = levels[0:1, :]
    cp, cm = levels[1:2, :], levels[2:3, :]
    dp, dm = levels[3:4, :], levels[4:5, :]
    ep, em = levels[5:6, :], levels[6:7, :]

    steps = [(1, 1), (1, -1), (-1, 1), (-1, -1), (1, 0), (-1, 0), (0, 1), (0, -1)]

    def span(step, extent_src):
        if step == 0:
            return 0, 2, CB
        return (CB - 2, 0, 2) if step > 0 else (0, CB + 2, 2)

    def halo_copy(e, k):
        dr, dc = steps[k]
        r0, rd, rn = span(dr, CB)
        c0, cd, cn = span(dc, CB)
        if e == 0:
            src = state.at[pl.ds(r0, rn), pl.ds(c0, cn)]
        else:
            src = Y[1].at[pl.ds(r0 + 2, rn), pl.ds(c0 + 2, cn)]
        return pltpu.make_async_remote_copy(
            src_ref=src,
            dst_ref=Y[e].at[pl.ds(rd, rn), pl.ds(cd, cn)],
            send_sem=halo_send.at[e, k],
            recv_sem=halo_recv.at[e, k],
            device_id=(p, a + dr, c + dc),
            device_id_type=MESH,
        )

    def exists(dr, dc):
        ok = None
        for pos, d, n in ((a, dr, LAT), (c, dc, LON)):
            if d:
                t = (pos < n - 1) if d > 0 else (pos > 0)
                ok = t if ok is None else jnp.logical_and(ok, t)
        return ok

    def halo_start(e):
        for k, (dr, dc) in enumerate(steps):
            @pl.when(exists(dr, dc))
            def _():
                halo_copy(e, k).start()

    def halo_wait_recv(e):
        for k, (dr, dc) in enumerate(steps):
            @pl.when(exists(-dr, -dc))
            def _():
                halo_copy(e, k).wait_recv()

    def halo_wait_send(e):
        for k, (dr, dc) in enumerate(steps):
            @pl.when(exists(dr, dc))
            def _():
                halo_copy(e, k).wait_send()

    on_top, on_bottom = a == 0, a == LAT - 1
    on_right, on_left = c == LON - 1, c == 0
    active = (jnp.logical_or(on_top, on_bottom), jnp.logical_or(on_right, on_left))
    sign = (jnp.where(on_top, 1, -1), jnp.where(on_right, 1, -1))
    rank = (jnp.where(on_top, c, LON - 1 - c), jnp.where(on_right, a, LAT - 1 - a))
    groups = (LON // 4, LAT // 4)
    member = tuple(lax.rem(u, 4) for u in rank)
    has_next = tuple(u // 4 < n - 1 for u, n in zip(rank, groups))
    has_prev = tuple(u // 4 > 0 for u in rank)

    def along(side, step):
        if side == 0:
            return (p, a, c + sign[0] * step)
        return (p, a + sign[1] * step, c)

    m_src = lax.rem(c, 4)

    def a_copy(e, g):
        if g < 4:
            side, dev = 0, (1 - p, 0, 4 * g + m_src)
        elif g < 6:
            side, dev = 1, (1 - p, 4 * (g - 4) + m_src, LON - 1)
        elif g < 10:
            side, dev = 0, (1 - p, LAT - 1, 39 - 4 * g - m_src)
        else:
            side, dev = 1, (1 - p, 47 - 4 * g - m_src, 0)
        return pltpu.make_async_remote_copy(
            src_ref=V.at[e, g],
            dst_ref=R[e][side].at[4 * a + c // 4],
            send_sem=a_send.at[e],
            recv_sem=a_recv.at[e, side],
            device_id=dev,
            device_id_type=MESH,
        )

    def a_wait_send(e):
        pltpu.make_async_remote_copy(
            src_ref=V.at[e],
            dst_ref=R[e][0].at[pl.ds(0, ENTRIES)],
            send_sem=a_send.at[e],
            recv_sem=a_recv.at[e, 0],
            device_id=(1 - p, a, c),
            device_id_type=MESH,
        ).wait_send()

    def a_wait_recv(e, side):
        pltpu.make_async_remote_copy(
            src_ref=R[e][side],
            dst_ref=R[e][side],
            send_sem=a_send.at[e],
            recv_sem=a_recv.at[e, side],
            device_id=(1 - p, a, c),
            device_id_type=MESH,
        ).wait_recv()

    def b_copy(e, side, s, slot):
        return pltpu.make_async_remote_copy(
            src_ref=Q.at[e, side, pl.ds(8 * s, 10)],
            dst_ref=W[e][side].at[slot],
            send_sem=b_send.at[e, side, s],
            recv_sem=b_recv.at[e, side, slot],
            device_id=along(side, s - member[side]),
            device_id_type=MESH,
        )

    def x_copy(e, side, way):
        return pltpu.make_async_remote_copy(
            src_ref=Q.at[e, side, 32 if way == 0 else 1],
            dst_ref=X[e][side].at[way, member[side]],
            send_sem=x_send.at[e, side, way],
            recv_sem=x_recv.at[e, side, way],
            device_id=along(side, (4 if way == 0 else -1) - member[side]),
            device_id_type=MESH,
        )

    def x_wait_recv(e, side, way):
        pltpu.make_async_remote_copy(
            src_ref=X[e][side].at[way],
            dst_ref=X[e][side].at[way],
            send_sem=x_send.at[e, side, way],
            recv_sem=x_recv.at[e, side, way],
            device_id=along(side, 1),
            device_id_type=MESH,
        ).wait_recv()

    def greet():
        barrier = pltpu.get_barrier_semaphore()

        def hello(dev):
            pl.semaphore_signal(barrier, inc=1, device_id=dev, device_id_type=MESH)

        for side in range(2):
            @pl.when(active[side])
            def _():
                @pl.loop(0, 32)
                def _(k):
                    hello((1 - p, k // 4, 4 * lax.rem(k, 4) + member[side]))

        hello((1 - p, a, c))
        awaited = jnp.int32(1 + ENTRIES)
        for dr, dc in steps:
            there = exists(dr, dc)
            awaited += there.astype(jnp.int32)

            @pl.when(there)
            def _():
                hello((p, a + dr, c + dc))

        for side in range(2):
            for s in range(4):
                other = jnp.logical_and(active[side], member[side] != s)
                awaited += other.astype(jnp.int32)

                @pl.when(other)
                def _():
                    hello(along(side, s - member[side]))

            for has, edge, way in ((has_prev, 0, -1), (has_next, 3, 1)):
                spoken = jnp.logical_and(active[side], has[side])
                awaited += spoken.astype(jnp.int32)

                @pl.when(jnp.logical_and(spoken, member[side] == edge))
                def _():
                    for k in range(1, 5):
                        hello(along(side, way * k))

        pl.semaphore_wait(barrier, awaited)

    def flat(e):
        return Y[e].reshape(20 * 20 * NF, NR)

    def interpolate(e, o_far):
        turn = (b + o_far) >> 7
        sub = lax.broadcasted_iota(jnp.int32, (NF, NR), 0)
        first = jnp.logical_or(sub == 1, sub == 4)
        second = jnp.logical_or(sub == 2, sub == 5)
        turned = jnp.logical_or(first, second)

        @pl.loop(0, ENTRIES)
        def _(g):
            i = lax.rem(g - turn + 2 * ENTRIES, ENTRIES)
            r0 = jnp.clip(base[0, i] - a * CB + 1, 1, CB)
            c0 = jnp.clip(base[1, i] - c * CB + 1, 1, CB)
            parts = []
            for x in range(4):
                acc = None
                for y in range(4):
                    term = weight[i, 0, 4 * x + y] * Y[e][r0 + x, c0 + y]
                    acc = term if acc is None else acc + term
                parts.append(acc)
            m = (parts[0] + parts[1]) + (parts[2] + parts[3])
            cosine = trig[0, pl.ds(i, 1), :]
            sine = trig[1, pl.ds(i, 1), :]
            partner = jnp.where(first, -pltpu.roll(m, NF - 1, 0), pltpu.roll(m, 1, 0))
            V[e, g] = jnp.where(turned, cosine * m + sine * partner, m)

    def side_loop(fn):
        for side in range(2):
            @pl.when(active[side])
            def _():
                fn(side)

    def spread(e, side, o_near):
        shift = (member[side] + o_near) >> 2
        for n in range(34):
            Q[e, side, n] = R[e][side][(n - 1 - shift + LOOP) & 31]
        for s in range(4):
            @pl.when(member[side] != s)
            def _():
                b_copy(e, side, s, member[side]).start()
        for way, has in ((0, has_next), (1, has_prev)):
            @pl.when(has[side])
            def _():
                x_copy(e, side, way).start()
        for n in range(10):
            W[e][side][member[side], n] = Q[e, side, 8 * member[side] + n]

    def spread_wait_send(e, side):
        for s in range(4):
            @pl.when(member[side] != s)
            def _():
                b_copy(e, side, s, member[side]).wait_send()
        for way, has in ((0, has_next), (1, has_prev)):
            @pl.when(has[side])
            def _():
                x_copy(e, side, way).wait_send()

    def collect(e, side, o_near):
        for s in range(4):
            @pl.when(member[side] != s)
            def _():
                b_copy(e, side, 0, s).wait_recv()
        for way, has, edge in ((0, has_prev, 0), (1, has_next, 3)):
            @pl.when(jnp.logical_and(has[side], member[side] == edge))
            def _():
                x_wait_recv(e, side, way)

        def place(cell):
            for rho in range(4):
                who = (rho - o_near + LOOP) & 3
                for n in range(10):
                    value = W[e][side][who, n]
                    if n in (0, 9):
                        way, has, edge = (0, has_prev, 0) if n == 0 else (1, has_next, 3)
                        far_value = jnp.where(has[side], X[e][side][way, who], 0.0)
                        value = jnp.where(member[side] == edge, far_value, value)
                    r, q = cell(2 * n + rho // 2, rho % 2)
                    Y[e][r, q] = value

        cells = (
            ((on_top, lambda h, o: (o, h)), (on_bottom, lambda h, o: (18 + o, 19 - h))),
            ((on_right, lambda h, o: (h, 18 + o)), (on_left, lambda h, o: (19 - h, o))),
        )[side]
        for on, cell in cells:
            @pl.when(on)
            def _():
                place(cell)

    def curl(A, ap, am, bb, br, rh):
        a1, a2 = A(1, 0, 0), A(2, 0, 0)
        return (
            ri * ((A(2, 1, 0) * ap - A(2, -1, 0) * am) - (A(1, 0, 1) - A(1, 0, -1)) * bb),
            (A(0, 0, 1) - A(0, 0, -1)) * br - (above(a2) * cp - below(a2) * cm),
            (above(a1) * cp - below(a1) * cm) - (A(0, 1, 0) - A(0, -1, 0)) * rh,
        )

    rh = ri * H_THETA

    def mid(q, r, k):
        return pl.ds((q * 18 + r) * 24 + k, 8)

    def first_pass(e, i, starts):
        y = flat(e)
        gi = a * CB + i + 3
        ap, am, bb = rows_s[0, gi], rows_s[1, gi], rows_s[2, gi]
        br = ri * bb
        for ic in starts:
            def ld(f, dg, dj):
                return y[pl.ds(((i + 1 + dg) * 20 + ic + 1 + dj) * NF + f, 8, stride=NF), :]

            def U(k, dg, dj):
                return ld(k, dg, dj)

            def B(k, dg, dj):
                return ld(3 + k, dg, dj)

            u = [U(k, 0, 0) for k in range(3)]
            mag = [B(k, 0, 0) for k in range(3)]
            w = curl(U, ap, am, bb, br, rh)
            cur = curl(B, ap, am, bb, br, rh)
            ind = cross(u, mag)
            el = [ind[k] - ETA * cur[k] for k in range(3)]
            t = ld(6, 0, 0)
            grad = [
                above(t) * dp - below(t) * dm,
                (ld(6, 1, 0) - ld(6, -1, 0)) * rh,
                (ld(6, 0, 1) - ld(6, 0, -1)) * br,
            ]
            head = ld(7, 0, 0) + np.float32(0.5) * (u[0] * u[0] + u[1] * u[1] + u[2] * u[2])
            for q, v in enumerate([*w, *cur, *el, *grad, head]):
                L1[mid(q, i, ic), :] = v

    def second_pass(e, i, starts, sink):
        y = flat(e)
        gi = a * CB + i + 4
        ap, am, bb = rows_s[0, gi], rows_s[1, gi], rows_s[2, gi]
        br = ri * bb
        for j in starts:
            def ld(f, dg, dj):
                return y[pl.ds(((i + 2 + dg) * 20 + j + 2 + dj) * NF + f, 8, stride=NF), :]

            def l1(q):
                return lambda k, dg, dj: L1[mid(q + k, i + 1 + dg, j + 1 + dj), :]

            Wv, J, E, T, H = l1(0), l1(3), l1(6), l1(9), l1(12)
            cw = curl(Wv, ap, am, bb, br, rh)
            ce = curl(E, ap, am, bb, br, rh)
            u = [ld(k, 0, 0) for k in range(3)]
            mag = [ld(3 + k, 0, 0) for k in range(3)]
            w = [Wv(k, 0, 0) for k in range(3)]
            cur = [J(k, 0, 0) for k in range(3)]
            adv, lor = cross(u, w), cross(cur, mag)
            h = H(0, 0, 0)
            slope = (
                above(h) * dp - below(h) * dm,
                (H(0, 1, 0) - H(0, -1, 0)) * rh,
                (H(0, 0, 1) - H(0, 0, -1)) * br,
            )
            t0 = T(0, 0, 0)
            lap = (above(t0) * ep - below(t0) * em) + ri * (
                (T(1, 1, 0) * ap - T(1, -1, 0) * am) + (T(2, 0, 1) - T(2, 0, -1)) * bb
            )
            div = (above(u[0]) * ep - below(u[0]) * em) + ri * (
                (ld(1, 1, 0) * ap - ld(1, -1, 0) * am) + (ld(2, 0, 1) - ld(2, 0, -1)) * bb
            )
            ru = [adv[k] + lor[k] - slope[k] - NU * cw[k] for k in range(3)]
            ru[0] = ru[0] + LIFT * ld(6, 0, 0)
            rt = KAPPA * lap - (u[0] * t0 + u[1] * T(1, 0, 0) + u[2] * T(2, 0, 0))
            for f, v in enumerate([*ru, *ce, rt, -div]):
                sink(i, j, f, v)

    y_second = flat(1)
    y_first = flat(0)
    out_flat = out.reshape(CB * CB * NF, NR)

    def keep(i, j, f, v):
        K1[pl.ds((f * CB + i) * CB + j, 8), :] = v
        at = pl.ds(((i + 2) * 20 + j + 2) * NF + f, 8, stride=NF)
        y_second[at, :] = y_first[at, :] + DT * v

    def finish(i, j, f, v):
        k1 = K1[pl.ds((f * CB + i) * CB + j, 8), :]
        out_flat[pl.ds((i * CB + j) * NF + f, 8, stride=NF), :] = np.float32(0.1) * (k1 + v)

    def fetch(k, src, dst):
        copy = pltpu.make_async_copy(src, dst, misc.at[k])
        copy.start()
        return copy

    corner = target_hbm.at[:, pl.ds(0, 128)]
    local = fetch(0, state, Y0.at[pl.ds(2, CB), pl.ds(2, CB)])
    small = [
        fetch(3, angle_hbm, angle),
        fetch(4, corner, near_at),
        fetch(5, base_hbm, base),
        fetch(6, weight_hbm, weight),
        fetch(7, rows, rows_s),
    ]
    greet()
    halo_start(0)
    tell = pltpu.make_async_remote_copy(
        src_ref=corner, dst_ref=far, send_sem=misc.at[1], recv_sem=misc.at[2],
        device_id=(1 - p, a, c), device_id_type=MESH,
    )
    tell.start()

    for copy in small:
        copy.wait()
    trig[0] = jnp.zeros((16, NR), jnp.float32)
    for i in range(ENTRIES):
        trig[0, i : i + 1, :] = jnp.full((1, NR), angle[0, i], jnp.float32)
    turned = trig[0]
    trig[0] = jnp.cos(turned)
    trig[1] = jnp.sin(turned)

    tell.wait_recv()
    fetch(8, far, far_at).wait()
    local.wait()
    o_near = loop_place(near_at[0, 0], near_at[1, 0])
    o_far = loop_place(far_at[0, 0], far_at[1, 0])

    for e in range(2):
        if e == 1:
            halo_start(1)
        halo_wait_recv(e)
        interpolate(e, o_far)
        for g in range(ENTRIES):
            a_copy(e, g).start()

        def middle(side):
            a_wait_recv(e, side)
            spread(e, side, o_near)

        side_loop(middle)
        side_loop(lambda side: collect(e, side, o_near))

        @pl.loop(0, 18)
        def _(i):
            first_pass(e, i, (0, 8, 10))

        @pl.loop(0, 16)
        def _(i):
            second_pass(e, i, (0, 8), keep if e == 0 else finish)

    tell.wait_send()
    for e in range(2):
        halo_wait_send(e)
        a_wait_send(e)
        side_loop(lambda side: spread_wait_send(e, side))


def loop_place(row, col):
    return jnp.where(
        row < 0,
        2 * col + row + 2,
        jnp.where(
            col >= NPH,
            2 * NPH + 2 * row + col - NPH,
            jnp.where(
                row >= NTH,
                2 * NPH + 2 * NTH + 2 * (NPH - 1 - col) + row - NTH,
                4 * NPH + 2 * NTH + 2 * (NTH - 1 - row) + col + 2,
            ),
        ),
    )


def per_device(state, rim_base, rim_weight, rim_angle, rim_target):
    vmem = pl.BlockSpec(memory_space=pltpu.VMEM)
    anywhere = pl.BlockSpec(memory_space=pl.ANY)
    f32 = jnp.float32
    result = pl.pallas_call(
        kernel,
        out_shape=jax.ShapeDtypeStruct((CB, CB, NF, NR), f32),
        in_specs=[anywhere, vmem] + [anywhere] * 5,
        out_specs=vmem,
        scratch_shapes=[
            pltpu.VMEM((20, 20, NF, NR), f32),
            pltpu.VMEM((20, 20, NF, NR), f32),
            pltpu.VMEM((NF * CB * CB, NR), f32),
            pltpu.VMEM((13 * 18 * 24, NR), f32),
            pltpu.VMEM((2, ENTRIES, NF, NR), f32),
            *[pltpu.VMEM((32, NF, NR), f32)] * 4,
            pltpu.VMEM((2, 2, 34, NF, NR), f32),
            *[pltpu.VMEM((4, 10, NF, NR), f32)] * 4,
            *[pltpu.VMEM((2, 4, NF, NR), f32)] * 4,
            pltpu.VMEM((2, 16, NR), f32),
            pltpu.VMEM((2, 128), jnp.int32),
            pltpu.SMEM((2, ENTRIES), jnp.int32),
            pltpu.SMEM((ENTRIES, 1, 16), f32),
            pltpu.SMEM((1, ENTRIES), f32),
            pltpu.SMEM((2, 128), jnp.int32),
            pltpu.SMEM((2, 128), jnp.int32),
            pltpu.SMEM((3, NTH + 8), f32),
            pltpu.SemaphoreType.DMA((2, 8)),
            pltpu.SemaphoreType.DMA((2, 8)),
            pltpu.SemaphoreType.DMA((2,)),
            pltpu.SemaphoreType.DMA((2, 2)),
            pltpu.SemaphoreType.DMA((2, 2, 4)),
            pltpu.SemaphoreType.DMA((2, 2, 4)),
            pltpu.SemaphoreType.DMA((2, 2, 2)),
            pltpu.SemaphoreType.DMA((2, 2, 2)),
            pltpu.SemaphoreType.DMA((9,)),
        ],
        compiler_params=pltpu.CompilerParams(
            collective_id=0, has_side_effects=True, vmem_limit_bytes=56 << 20
        ),
    )(
        jnp.asarray(row_table()),
        jnp.asarray(level_table()),
        state[0],
        rim_base[0].T,
        jnp.transpose(rim_weight, (1, 0, 2)),
        rim_angle,
        rim_target[0].T,
    )
    return result[None]


def solution(mesh):
    return jax.shard_map(
        per_device,
        mesh=mesh,
        in_specs=(
            P("panel", "lat", "lon", None, None),
            P("panel", ("lat", "lon"), None),
            P("panel", ("lat", "lon"), None),
            P("panel", ("lat", "lon")),
            P("panel", None, None),
        ),
        out_specs=P("panel", "lat", "lon", None, None),
        check_vma=False,
    )
```

```python
import math

import jax
import jax.numpy as jnp
import numpy as np
from jax import lax
from jax.experimental import pallas as pl
from jax.experimental.pallas import tpu as pltpu
from jax.sharding import PartitionSpec as P

NTH, NPH, NR, NF, CB = 128, 256, 128, 8, 16
LAT, LON = NTH // CB, NPH // CB
LOOP = 1536
ENTRIES = 12
ETA = np.float32(0.2)
NU = np.float32(0.2)
KAPPA = np.float32(0.3)
LIFT = np.float32(0.5)
DT = np.float32(0.2)
MESH = pl.DeviceIdType.MESH

DTHETA = math.pi / (2 * NTH)
DPHI = 1.5 * math.pi / NPH
H_THETA = np.float32(0.5 / DTHETA)


def row_table():
    g = np.arange(-4, NTH + 4)
    sine = lambda k: np.sin(math.pi / 4 + (k + 0.5) * DTHETA)
    s = sine(g)
    half = 0.5 / DTHETA
    return np.stack([sine(g + 1) * half / s, sine(g - 1) * half / s, 0.5 / DPHI / s]).astype(
        np.float32
    )


def level_table():
    scale = 2.0 * NTH / math.pi
    dr = 0.65 * scale / NR
    r = 0.35 * scale + (np.arange(NR) + 0.5) * dr
    half = 0.5 / dr
    up = np.where(np.arange(NR) < NR - 1, half, 0.0)
    down = np.where(np.arange(NR) > 0, half, 0.0)
    r_up, r_down = np.roll(r, -1), np.roll(r, 1)
    rows = [
        1 / r,
        up * r_up / r,
        down * r_down / r,
        up,
        down,
        up * r_up**2 / r**2,
        down * r_down**2 / r**2,
        0 * r,
    ]
    return np.stack(rows).astype(np.float32)


def above(x):
    return pltpu.roll(x, NR - 1, 1)


def below(x):
    return pltpu.roll(x, 1, 1)


def cross(a, b):
    return (
        a[1] * b[2] - a[2] * b[1],
        a[2] * b[0] - a[0] * b[2],
        a[0] * b[1] - a[1] * b[0],
    )


def kernel(
    rows, levels, state, base_hbm, weight_hbm, angle_hbm, target_hbm,
    out,
    Y0, Y1, K1, L1, V,
    R00, R01, R10, R11, Q, W00, W01, W10, W11, X00, X01, X10, X11,
    trig, far, base, weight, angle, near_at, far_at, rows_s, slopes,
    halo_send, halo_recv, a_send, a_recv, b_send, b_recv, x_send, x_recv, misc,
):
    p, a, c = lax.axis_index("panel"), lax.axis_index("lat"), lax.axis_index("lon")
    b = a * LON + c
    Y = (Y0, Y1)
    R = ((R00, R01), (R10, R11))
    W = ((W00, W01), (W10, W11))
    X = ((X00, X01), (X10, X11))

    ri = levels[0:1, :]
    cp, cm = levels[1:2, :], levels[2:3, :]
    dp, dm = levels[3:4, :], levels[4:5, :]
    ep, em = levels[5:6, :], levels[6:7, :]

    steps = [(1, 1), (1, -1), (-1, 1), (-1, -1), (1, 0), (-1, 0), (0, 1), (0, -1)]

    def span(step):
        if step == 0:
            return 0, 2, CB
        return (CB - 2, 0, 2) if step > 0 else (0, CB + 2, 2)

    def halo_copy(e, k, part=None):
        dr, dc = steps[k]
        r0, rd, rn = span(dr)
        c0, cd, cn = span(dc)
        if part is not None:
            first, count = ((0, 2), (2, CB - 4), (CB - 2, 2))[part]
            if dr:
                c0, cd, cn = c0 + first, cd + first, count
            else:
                r0, rd, rn = r0 + first, rd + first, count
        if e == 0:
            src = state.at[pl.ds(r0, rn), pl.ds(c0, cn)]
        else:
            src = Y[1].at[pl.ds(r0 + 2, rn), pl.ds(c0 + 2, cn)]
        return pltpu.make_async_remote_copy(
            src_ref=src,
            dst_ref=Y[e].at[pl.ds(rd, rn), pl.ds(cd, cn)],
            send_sem=halo_send.at[e, k],
            recv_sem=halo_recv.at[e, k],
            device_id=(p, a + dr, c + dc),
            device_id_type=MESH,
        )

    def exists(dr, dc):
        ok = None
        for pos, d, n in ((a, dr, LAT), (c, dc, LON)):
            if d:
                t = (pos < n - 1) if d > 0 else (pos > 0)
                ok = t if ok is None else jnp.logical_and(ok, t)
        return ok

    def halo_start(e):
        for k, (dr, dc) in enumerate(steps):
            @pl.when(exists(dr, dc))
            def _():
                halo_copy(e, k).start()

    def late_part(dr, dc, part):
        if part == 1 or (dr and dc):
            return None
        if dc:
            return on_top if part == 0 else on_bottom
        return on_left if part == 0 else on_right

    def second_halo_start(late):
        for k, (dr, dc) in enumerate(steps):
            if dr and dc:
                if not late:
                    @pl.when(exists(dr, dc))
                    def _():
                        halo_copy(1, k).start()
                continue
            for part in range(3):
                is_late = late_part(dr, dc, part)
                if is_late is None:
                    if late:
                        continue
                    now = exists(dr, dc)
                else:
                    now = jnp.logical_and(
                        exists(dr, dc), is_late if late else jnp.logical_not(is_late)
                    )

                @pl.when(now)
                def _():
                    halo_copy(1, k, part).start()

    def halo_wait_recv(e):
        for k, (dr, dc) in enumerate(steps):
            @pl.when(exists(-dr, -dc))
            def _():
                halo_copy(e, k).wait_recv()

    def halo_wait_send(e):
        for k, (dr, dc) in enumerate(steps):
            @pl.when(exists(dr, dc))
            def _():
                halo_copy(e, k).wait_send()

    on_top, on_bottom = a == 0, a == LAT - 1
    on_right, on_left = c == LON - 1, c == 0
    active = (jnp.logical_or(on_top, on_bottom), jnp.logical_or(on_right, on_left))
    sign = (jnp.where(on_top, 1, -1), jnp.where(on_right, 1, -1))
    rank = (jnp.where(on_top, c, LON - 1 - c), jnp.where(on_right, a, LAT - 1 - a))
    groups = (LON // 4, LAT // 4)
    member = tuple(lax.rem(u, 4) for u in rank)
    has_next = tuple(u // 4 < n - 1 for u, n in zip(rank, groups))
    has_prev = tuple(u // 4 > 0 for u in rank)

    def along(side, step):
        if side == 0:
            return (p, a, c + sign[0] * step)
        return (p, a + sign[1] * step, c)

    m_src = lax.rem(c, 4)

    def a_copy(e, g):
        if g < 4:
            side, dev = 0, (1 - p, 0, 4 * g + m_src)
        elif g < 6:
            side, dev = 1, (1 - p, 4 * (g - 4) + m_src, LON - 1)
        elif g < 10:
            side, dev = 0, (1 - p, LAT - 1, 39 - 4 * g - m_src)
        else:
            side, dev = 1, (1 - p, 47 - 4 * g - m_src, 0)
        return pltpu.make_async_remote_copy(
            src_ref=V.at[e, g],
            dst_ref=R[e][side].at[4 * a + c // 4],
            send_sem=a_send.at[e],
            recv_sem=a_recv.at[e, side],
            device_id=dev,
            device_id_type=MESH,
        )

    def a_wait_send(e):
        pltpu.make_async_remote_copy(
            src_ref=V.at[e],
            dst_ref=R[e][0].at[pl.ds(0, ENTRIES)],
            send_sem=a_send.at[e],
            recv_sem=a_recv.at[e, 0],
            device_id=(1 - p, a, c),
            device_id_type=MESH,
        ).wait_send()

    def a_wait_recv(e, side):
        pltpu.make_async_remote_copy(
            src_ref=R[e][side],
            dst_ref=R[e][side],
            send_sem=a_send.at[e],
            recv_sem=a_recv.at[e, side],
            device_id=(1 - p, a, c),
            device_id_type=MESH,
        ).wait_recv()

    def b_copy(e, side, s, slot):
        return pltpu.make_async_remote_copy(
            src_ref=Q.at[e, side, pl.ds(8 * s, 10)],
            dst_ref=W[e][side].at[slot],
            send_sem=b_send.at[e, side, s],
            recv_sem=b_recv.at[e, side, slot],
            device_id=along(side, s - member[side]),
            device_id_type=MESH,
        )

    def x_copy(e, side, way):
        return pltpu.make_async_remote_copy(
            src_ref=Q.at[e, side, 32 if way == 0 else 1],
            dst_ref=X[e][side].at[way, member[side]],
            send_sem=x_send.at[e, side, way],
            recv_sem=x_recv.at[e, side, way],
            device_id=along(side, (4 if way == 0 else -1) - member[side]),
            device_id_type=MESH,
        )

    def x_wait_recv(e, side, way):
        pltpu.make_async_remote_copy(
            src_ref=X[e][side].at[way],
            dst_ref=X[e][side].at[way],
            send_sem=x_send.at[e, side, way],
            recv_sem=x_recv.at[e, side, way],
            device_id=along(side, 1),
            device_id_type=MESH,
        ).wait_recv()

    def greet():
        barrier = pltpu.get_barrier_semaphore()

        def hello(dev):
            pl.semaphore_signal(barrier, inc=1, device_id=dev, device_id_type=MESH)

        for side in range(2):
            @pl.when(active[side])
            def _():
                @pl.loop(0, 32)
                def _(k):
                    hello((1 - p, k // 4, 4 * lax.rem(k, 4) + member[side]))

        hello((1 - p, a, c))
        awaited = jnp.int32(1 + ENTRIES)
        for dr, dc in steps:
            there = exists(dr, dc)
            awaited += there.astype(jnp.int32)

            @pl.when(there)
            def _():
                hello((p, a + dr, c + dc))

        for side in range(2):
            for s in range(4):
                other = jnp.logical_and(active[side], member[side] != s)
                awaited += other.astype(jnp.int32)

                @pl.when(other)
                def _():
                    hello(along(side, s - member[side]))

            for has, edge, way in ((has_prev, 0, -1), (has_next, 3, 1)):
                spoken = jnp.logical_and(active[side], has[side])
                awaited += spoken.astype(jnp.int32)

                @pl.when(jnp.logical_and(spoken, member[side] == edge))
                def _():
                    for k in range(1, 5):
                        hello(along(side, way * k))

        pl.semaphore_wait(barrier, awaited)

    def flat(e):
        return Y[e].reshape(20 * 20 * NF, NR)

    def interpolate(e, o_far):
        turn = (b + o_far) >> 7
        sub = lax.broadcasted_iota(jnp.int32, (NF, NR), 0)
        first = jnp.logical_or(sub == 1, sub == 4)
        second = jnp.logical_or(sub == 2, sub == 5)
        turned = jnp.logical_or(first, second)

        @pl.loop(0, ENTRIES)
        def _(g):
            i = lax.rem(g - turn + 2 * ENTRIES, ENTRIES)
            r0 = jnp.clip(base[0, i] - a * CB + 1, 1, CB)
            c0 = jnp.clip(base[1, i] - c * CB + 1, 1, CB)
            parts = []
            for x in range(4):
                acc = None
                for y in range(4):
                    term = weight[i, 0, 4 * x + y] * Y[e][r0 + x, c0 + y]
                    acc = term if acc is None else acc + term
                parts.append(acc)
            m = (parts[0] + parts[1]) + (parts[2] + parts[3])
            cosine = trig[0, pl.ds(i, 1), :]
            sine = trig[1, pl.ds(i, 1), :]
            partner = jnp.where(first, -pltpu.roll(m, NF - 1, 0), pltpu.roll(m, 1, 0))
            V[e, g] = jnp.where(turned, cosine * m + sine * partner, m)

    def side_loop(fn):
        for side in range(2):
            @pl.when(active[side])
            def _():
                fn(side)

    def spread(e, side, o_near):
        shift = (member[side] + o_near) >> 2
        for n in range(34):
            Q[e, side, n] = R[e][side][(n - 1 - shift + LOOP) & 31]
        for s in range(4):
            @pl.when(member[side] != s)
            def _():
                b_copy(e, side, s, member[side]).start()
        for way, has in ((0, has_next), (1, has_prev)):
            @pl.when(has[side])
            def _():
                x_copy(e, side, way).start()
        for n in range(10):
            W[e][side][member[side], n] = Q[e, side, 8 * member[side] + n]

    def spread_wait_send(e, side):
        for s in range(4):
            @pl.when(member[side] != s)
            def _():
                b_copy(e, side, s, member[side]).wait_send()
        for way, has in ((0, has_next), (1, has_prev)):
            @pl.when(has[side])
            def _():
                x_copy(e, side, way).wait_send()

    def collect(e, side, o_near):
        for s in range(4):
            @pl.when(member[side] != s)
            def _():
                b_copy(e, side, 0, s).wait_recv()
        for way, has, edge in ((0, has_prev, 0), (1, has_next, 3)):
            @pl.when(jnp.logical_and(has[side], member[side] == edge))
            def _():
                x_wait_recv(e, side, way)

        def place(cell):
            for rho in range(4):
                who = (rho - o_near + LOOP) & 3
                for n in range(10):
                    value = W[e][side][who, n]
                    if n in (0, 9):
                        way, has, edge = (0, has_prev, 0) if n == 0 else (1, has_next, 3)
                        far_value = jnp.where(has[side], X[e][side][way, who], 0.0)
                        value = jnp.where(member[side] == edge, far_value, value)
                    r, q = cell(2 * n + rho // 2, rho % 2)
                    Y[e][r, q] = value

        cells = (
            ((on_top, lambda h, o: (o, h)), (on_bottom, lambda h, o: (18 + o, 19 - h))),
            ((on_right, lambda h, o: (h, 18 + o)), (on_left, lambda h, o: (19 - h, o))),
        )[side]
        for on, cell in cells:
            @pl.when(on)
            def _():
                place(cell)

    def curl(A, ap, am, bb, br, rh):
        a1, a2 = A(1, 0, 0), A(2, 0, 0)
        return (
            ri * ((A(2, 1, 0) * ap - A(2, -1, 0) * am) - (A(1, 0, 1) - A(1, 0, -1)) * bb),
            (A(0, 0, 1) - A(0, 0, -1)) * br - (above(a2) * cp - below(a2) * cm),
            (above(a1) * cp - below(a1) * cm) - (A(0, 1, 0) - A(0, -1, 0)) * rh,
        )

    rh = ri * H_THETA

    def first_values(ld, ap, am, bb, br):
        u = [ld(k, 0, 0) for k in range(3)]
        mag = [ld(3 + k, 0, 0) for k in range(3)]
        w = curl(lambda k, dg, dj: ld(k, dg, dj), ap, am, bb, br, rh)
        cur = curl(lambda k, dg, dj: ld(3 + k, dg, dj), ap, am, bb, br, rh)
        ind = cross(u, mag)
        el = [ind[k] - ETA * cur[k] for k in range(3)]
        t = ld(6, 0, 0)
        grad = [
            above(t) * dp - below(t) * dm,
            (ld(6, 1, 0) - ld(6, -1, 0)) * rh,
            (ld(6, 0, 1) - ld(6, 0, -1)) * br,
        ]
        head = ld(7, 0, 0) + np.float32(0.5) * (u[0] * u[0] + u[1] * u[1] + u[2] * u[2])
        return [*w, *cur, *el, *grad, head]

    def second_values(ld, mid, ap, am, bb, br):
        Wv, J, E, T, H = (lambda k, dg, dj, q=q: mid(q + k, dg, dj) for q in (0, 3, 6, 9, 12))
        cw = curl(Wv, ap, am, bb, br, rh)
        ce = curl(E, ap, am, bb, br, rh)
        u = [ld(k, 0, 0) for k in range(3)]
        mag = [ld(3 + k, 0, 0) for k in range(3)]
        w = [Wv(k, 0, 0) for k in range(3)]
        cur = [J(k, 0, 0) for k in range(3)]
        adv, lor = cross(u, w), cross(cur, mag)
        h = H(0, 0, 0)
        slope = (
            above(h) * dp - below(h) * dm,
            (H(0, 1, 0) - H(0, -1, 0)) * rh,
            (H(0, 0, 1) - H(0, 0, -1)) * br,
        )
        t0 = T(0, 0, 0)
        lap = (above(t0) * ep - below(t0) * em) + ri * (
            (T(1, 1, 0) * ap - T(1, -1, 0) * am) + (T(2, 0, 1) - T(2, 0, -1)) * bb
        )
        div = (above(u[0]) * ep - below(u[0]) * em) + ri * (
            (ld(1, 1, 0) * ap - ld(1, -1, 0) * am) + (ld(2, 0, 1) - ld(2, 0, -1)) * bb
        )
        ru = [adv[k] + lor[k] - slope[k] - NU * cw[k] for k in range(3)]
        ru[0] = ru[0] + LIFT * ld(6, 0, 0)
        rt = KAPPA * lap - (u[0] * t0 + u[1] * T(1, 0, 0) + u[2] * T(2, 0, 0))
        return [*ru, *ce, rt, -div]

    def eight(first, step):
        return pl.ds(first, 8) if step == 1 else pl.ds(first, 8, stride=step)

    def factors(i, column):
        if column:
            ap, am, bb = (slopes[k, pl.ds(i, 8), :] for k in range(3))
        else:
            ap, am, bb = (rows_s[k, a * CB + i + 3] for k in range(3))
        return ap, am, bb, ri * bb

    def first_pass(e, i, k, column=False):
        y = flat(e)
        step = 20 * NF if column else NF

        def ld(f, dg, dj):
            return y[eight(((i + 1 + dg) * 20 + k + 1 + dj) * NF + f, step), :]

        for q, v in enumerate(first_values(ld, *factors(i, column))):
            L1[eight((q * 18 + i) * 24 + k, 24 if column else 1), :] = v

    def second_pass(e, i, j, column=False):
        y = flat(e)
        step = 20 * NF if column else NF

        def ld(f, dg, dj):
            return y[eight(((i + 2 + dg) * 20 + j + 2 + dj) * NF + f, step), :]

        def mid(q, dg, dj):
            return L1[eight((q * 18 + i + 1 + dg) * 24 + j + 1 + dj, 24 if column else 1), :]

        sink = keep if e == 0 else finish
        for f, v in enumerate(second_values(ld, mid, *factors(i + 1, column))):
            sink(i, j, f, v, column)

    def whole(e):
        @pl.loop(0, 18)
        def _(i):
            for k in (0, 8, 10):
                first_pass(e, i, k)

        @pl.loop(0, 16)
        def _(i):
            for j in (0, 8):
                second_pass(e, i, j)

    def strips(e):
        @pl.when(active[0])
        def _():
            base_row = jnp.where(on_top, 0, CB)

            @pl.loop(0, 2)
            def _(n):
                for k in (0, 8, 10):
                    first_pass(e, base_row + n, k)

        @pl.when(active[1])
        def _():
            base_col = jnp.where(on_left, 0, CB)

            @pl.loop(0, 6)
            def _(n):
                first_pass(e, jnp.minimum(8 * (n // 2), 10), base_col + lax.rem(n, 2), True)

        @pl.when(active[0])
        def _():
            base_row = jnp.where(on_top, 0, CB - 2)

            @pl.loop(0, 2)
            def _(n):
                for j in (0, 8):
                    second_pass(e, base_row + n, j)

        @pl.when(active[1])
        def _():
            base_col = jnp.where(on_left, 0, CB - 2)

            @pl.loop(0, 4)
            def _(n):
                second_pass(e, 8 * (n // 2), base_col + lax.rem(n, 2), True)

    y_second = flat(1)
    y_first = flat(0)
    out_flat = out.reshape(CB * CB * NF, NR)

    def keep(i, j, f, v, column):
        K1[eight((f * CB + i) * CB + j, CB if column else 1), :] = v
        at = eight(((i + 2) * 20 + j + 2) * NF + f, 20 * NF if column else NF)
        y_second[at, :] = y_first[at, :] + DT * v

    def finish(i, j, f, v, column):
        k1 = K1[eight((f * CB + i) * CB + j, CB if column else 1), :]
        at = eight((i * CB + j) * NF + f, CB * NF if column else NF)
        out_flat[at, :] = np.float32(0.1) * (k1 + v)

    def fetch(k, src, dst):
        copy = pltpu.make_async_copy(src, dst, misc.at[k])
        copy.start()
        return copy

    corner = target_hbm.at[:, pl.ds(0, 128)]
    local = fetch(0, state, Y0.at[pl.ds(2, CB), pl.ds(2, CB)])
    small = [
        fetch(3, angle_hbm, angle),
        fetch(4, corner, near_at),
        fetch(5, base_hbm, base),
        fetch(6, weight_hbm, weight),
        fetch(7, rows, rows_s),
    ]
    greet()
    halo_start(0)
    tell = pltpu.make_async_remote_copy(
        src_ref=corner, dst_ref=far, send_sem=misc.at[1], recv_sem=misc.at[2],
        device_id=(1 - p, a, c), device_id_type=MESH,
    )
    tell.start()

    for copy in small:
        copy.wait()
    trig[0] = jnp.zeros((16, NR), jnp.float32)
    for i in range(ENTRIES):
        trig[0, i : i + 1, :] = jnp.full((1, NR), angle[0, i], jnp.float32)
    turned = trig[0]
    trig[0] = jnp.cos(turned)
    trig[1] = jnp.sin(turned)

    for i in range(24):
        gi = jnp.minimum(a * CB + i + 3, NTH + 7)
        for k in range(3):
            slopes[k, i : i + 1, :] = jnp.full((1, NR), rows_s[k, gi], jnp.float32)

    tell.wait_recv()
    fetch(8, far, far_at).wait()
    local.wait()
    o_near = loop_place(near_at[0, 0], near_at[1, 0])
    o_far = loop_place(far_at[0, 0], far_at[1, 0])

    for e in range(2):
        halo_wait_recv(e)
        interpolate(e, o_far)
        for g in range(ENTRIES):
            a_copy(e, g).start()
        whole(e)
        if e == 0:
            second_halo_start(late=False)

        def middle(side):
            a_wait_recv(e, side)
            spread(e, side, o_near)

        side_loop(middle)
        side_loop(lambda side: collect(e, side, o_near))
        strips(e)
        if e == 0:
            second_halo_start(late=True)

    tell.wait_send()
    for e in range(2):
        halo_wait_send(e)
        a_wait_send(e)
        side_loop(lambda side: spread_wait_send(e, side))


def loop_place(row, col):
    return jnp.where(
        row < 0,
        2 * col + row + 2,
        jnp.where(
            col >= NPH,
            2 * NPH + 2 * row + col - NPH,
            jnp.where(
                row >= NTH,
                2 * NPH + 2 * NTH + 2 * (NPH - 1 - col) + row - NTH,
                4 * NPH + 2 * NTH + 2 * (NTH - 1 - row) + col + 2,
            ),
        ),
    )


def per_device(state, rim_base, rim_weight, rim_angle, rim_target):
    vmem = pl.BlockSpec(memory_space=pltpu.VMEM)
    anywhere = pl.BlockSpec(memory_space=pl.ANY)
    f32 = jnp.float32
    result = pl.pallas_call(
        kernel,
        out_shape=jax.ShapeDtypeStruct((CB, CB, NF, NR), f32),
        in_specs=[anywhere, vmem] + [anywhere] * 5,
        out_specs=vmem,
        scratch_shapes=[
            pltpu.VMEM((20, 20, NF, NR), f32),
            pltpu.VMEM((20, 20, NF, NR), f32),
            pltpu.VMEM((NF * CB * CB, NR), f32),
            pltpu.VMEM((13 * 18 * 24, NR), f32),
            pltpu.VMEM((2, ENTRIES, NF, NR), f32),
            *[pltpu.VMEM((32, NF, NR), f32)] * 4,
            pltpu.VMEM((2, 2, 34, NF, NR), f32),
            *[pltpu.VMEM((4, 10, NF, NR), f32)] * 4,
            *[pltpu.VMEM((2, 4, NF, NR), f32)] * 4,
            pltpu.VMEM((2, 16, NR), f32),
            pltpu.VMEM((2, 128), jnp.int32),
            pltpu.SMEM((2, ENTRIES), jnp.int32),
            pltpu.SMEM((ENTRIES, 1, 16), f32),
            pltpu.SMEM((1, ENTRIES), f32),
            pltpu.SMEM((2, 128), jnp.int32),
            pltpu.SMEM((2, 128), jnp.int32),
            pltpu.SMEM((3, NTH + 8), f32),
            pltpu.VMEM((3, 24, NR), f32),
            pltpu.SemaphoreType.DMA((2, 8)),
            pltpu.SemaphoreType.DMA((2, 8)),
            pltpu.SemaphoreType.DMA((2,)),
            pltpu.SemaphoreType.DMA((2, 2)),
            pltpu.SemaphoreType.DMA((2, 2, 4)),
            pltpu.SemaphoreType.DMA((2, 2, 4)),
            pltpu.SemaphoreType.DMA((2, 2, 2)),
            pltpu.SemaphoreType.DMA((2, 2, 2)),
            pltpu.SemaphoreType.DMA((9,)),
        ],
        compiler_params=pltpu.CompilerParams(
            collective_id=0, has_side_effects=True, vmem_limit_bytes=56 << 20
        ),
    )(
        jnp.asarray(row_table()),
        jnp.asarray(level_table()),
        state[0],
        rim_base[0].T,
        jnp.transpose(rim_weight, (1, 0, 2)),
        rim_angle,
        rim_target[0].T,
    )
    return result[None]


def solution(mesh):
    return jax.shard_map(
        per_device,
        mesh=mesh,
        in_specs=(
            P("panel", "lat", "lon", None, None),
            P("panel", ("lat", "lon"), None),
            P("panel", ("lat", "lon"), None),
            P("panel", ("lat", "lon")),
            P("panel", None, None),
        ),
        out_specs=P("panel", "lat", "lon", None, None),
        check_vma=False,
    )
```

```python
import math

import jax
import jax.numpy as jnp
import numpy as np
from jax import lax
from jax.experimental import pallas as pl
from jax.experimental.pallas import tpu as pltpu
from jax.sharding import PartitionSpec as P

NTH, NPH, NR, NF, CB = 128, 256, 128, 8, 16
LAT, LON = NTH // CB, NPH // CB
LOOP = 1536
ENTRIES = 12
ETA = np.float32(0.2)
NU = np.float32(0.2)
KAPPA = np.float32(0.3)
LIFT = np.float32(0.5)
DT = np.float32(0.2)
MESH = pl.DeviceIdType.MESH

DTHETA = math.pi / (2 * NTH)
DPHI = 1.5 * math.pi / NPH
H_THETA = np.float32(0.5 / DTHETA)


def row_table():
    g = np.arange(-4, NTH + 4)
    sine = lambda k: np.sin(math.pi / 4 + (k + 0.5) * DTHETA)
    s = sine(g)
    half = 0.5 / DTHETA
    return np.stack([sine(g + 1) * half / s, sine(g - 1) * half / s, 0.5 / DPHI / s]).astype(
        np.float32
    )


def level_table():
    scale = 2.0 * NTH / math.pi
    dr = 0.65 * scale / NR
    r = 0.35 * scale + (np.arange(NR) + 0.5) * dr
    half = 0.5 / dr
    up = np.where(np.arange(NR) < NR - 1, half, 0.0)
    down = np.where(np.arange(NR) > 0, half, 0.0)
    r_up, r_down = np.roll(r, -1), np.roll(r, 1)
    rows = [
        1 / r,
        up * r_up / r,
        down * r_down / r,
        up,
        down,
        up * r_up**2 / r**2,
        down * r_down**2 / r**2,
        0 * r,
    ]
    return np.stack(rows).astype(np.float32)


def above(x):
    return pltpu.roll(x, NR - 1, 1)


def below(x):
    return pltpu.roll(x, 1, 1)


def cross(a, b):
    return (
        a[1] * b[2] - a[2] * b[1],
        a[2] * b[0] - a[0] * b[2],
        a[0] * b[1] - a[1] * b[0],
    )


def kernel(
    rows, levels, state, base_hbm, weight_hbm, angle_hbm, target_hbm,
    out,
    Y0, Y1, K1, L1, V,
    R00, R01, R10, R11, Q, W00, W01, W10, W11, X00, X01, X10, X11,
    trig, far, base, weight, angle, near_at, far_at, rows_s, slopes,
    halo_send, halo_recv, a_send, a_recv, b_send, b_recv, x_send, x_recv, misc, heard,
):
    p, a, c = lax.axis_index("panel"), lax.axis_index("lat"), lax.axis_index("lon")
    b = a * LON + c
    Y = (Y0, Y1)
    R = ((R00, R01), (R10, R11))
    W = ((W00, W01), (W10, W11))
    X = ((X00, X01), (X10, X11))

    ri = levels[0:1, :]
    cp, cm = levels[1:2, :], levels[2:3, :]
    dp, dm = levels[3:4, :], levels[4:5, :]
    ep, em = levels[5:6, :], levels[6:7, :]

    steps = [(1, 1), (1, -1), (-1, 1), (-1, -1), (1, 0), (-1, 0), (0, 1), (0, -1)]

    def span(step):
        if step == 0:
            return 0, 2, CB
        return (CB - 2, 0, 2) if step > 0 else (0, CB + 2, 2)

    def halo_copy(e, k, part=None):
        dr, dc = steps[k]
        r0, rd, rn = span(dr)
        c0, cd, cn = span(dc)
        if part is not None:
            first, count = ((0, 2), (2, CB - 4), (CB - 2, 2))[part]
            if dr:
                c0, cd, cn = c0 + first, cd + first, count
            else:
                r0, rd, rn = r0 + first, rd + first, count
        if e == 0:
            src = state.at[pl.ds(r0, rn), pl.ds(c0, cn)]
        else:
            src = Y[1].at[pl.ds(r0 + 2, rn), pl.ds(c0 + 2, cn)]
        return pltpu.make_async_remote_copy(
            src_ref=src,
            dst_ref=Y[e].at[pl.ds(rd, rn), pl.ds(cd, cn)],
            send_sem=halo_send.at[e, k],
            recv_sem=halo_recv.at[e, k],
            device_id=(p, a + dr, c + dc),
            device_id_type=MESH,
        )

    def exists(dr, dc):
        ok = None
        for pos, d, n in ((a, dr, LAT), (c, dc, LON)):
            if d:
                t = (pos < n - 1) if d > 0 else (pos > 0)
                ok = t if ok is None else jnp.logical_and(ok, t)
        return ok

    def halo_start(e):
        for k, (dr, dc) in enumerate(steps):
            @pl.when(exists(dr, dc))
            def _():
                halo_copy(e, k).start()

    def late_part(dr, dc, part):
        if part == 1 or (dr and dc):
            return None
        if dc:
            return on_top if part == 0 else on_bottom
        return on_left if part == 0 else on_right

    def second_halo_start(late):
        for k, (dr, dc) in enumerate(steps):
            if dr and dc:
                if not late:
                    @pl.when(exists(dr, dc))
                    def _():
                        halo_copy(1, k).start()
                continue
            for part in range(3):
                is_late = late_part(dr, dc, part)
                if is_late is None:
                    if late:
                        continue
                    now = exists(dr, dc)
                else:
                    now = jnp.logical_and(
                        exists(dr, dc), is_late if late else jnp.logical_not(is_late)
                    )

                @pl.when(now)
                def _():
                    halo_copy(1, k, part).start()

    def halo_wait_recv(e):
        for k, (dr, dc) in enumerate(steps):
            @pl.when(exists(-dr, -dc))
            def _():
                halo_copy(e, k).wait_recv()

    def halo_wait_send(e):
        for k, (dr, dc) in enumerate(steps):
            @pl.when(exists(dr, dc))
            def _():
                halo_copy(e, k).wait_send()

    on_top, on_bottom = a == 0, a == LAT - 1
    on_right, on_left = c == LON - 1, c == 0
    active = (jnp.logical_or(on_top, on_bottom), jnp.logical_or(on_right, on_left))
    at_right = c >= LON // 2
    sign = (jnp.where(on_top, 1, -1), jnp.where(at_right, 1, -1))
    rank = (jnp.where(on_top, c, LON - 1 - c), jnp.where(at_right, a, LAT - 1 - a))
    groups = (LON // 4, LAT // 4)
    segment = tuple(lax.rem(u, 4) for u in rank)
    has_next = tuple(u // 4 < n - 1 for u, n in zip(rank, groups))
    has_prev = tuple(u // 4 > 0 for u in rank)
    in_middle = jnp.logical_or(segment[1] == 1, segment[1] == 2)
    relays = (
        active[0],
        jnp.logical_and(in_middle, jnp.logical_or(c < 2, c >= LON - 2)),
    )
    member = (segment[0], jnp.where(in_middle, 2 * (segment[1] - 1) + lax.rem(c, 2), 0))
    own_slot = (segment[0], jnp.where(in_middle, member[1], -1))

    def along(side, step):
        if side == 0:
            return (p, a, c + sign[0] * step)
        return (p, a + sign[1] * step, jnp.where(at_right, LON - 1, 0))

    m_src = lax.rem(c, 4)

    def a_copy(e, g):
        if g < 4:
            side, dev = 0, (1 - p, 0, 4 * g + m_src)
        elif g < 6:
            side, dev = 1, (1 - p, 4 * (g - 4) + 1 + m_src // 2, LON - 2 + lax.rem(m_src, 2))
        elif g < 10:
            side, dev = 0, (1 - p, LAT - 1, 39 - 4 * g - m_src)
        else:
            side, dev = 1, (1 - p, 46 - 4 * g - m_src // 2, lax.rem(m_src, 2))
        return pltpu.make_async_remote_copy(
            src_ref=V.at[e, g],
            dst_ref=R[e][side].at[4 * a + c // 4],
            send_sem=a_send.at[e],
            recv_sem=a_recv.at[e, side],
            device_id=dev,
            device_id_type=MESH,
        )

    def a_wait_send(e):
        pltpu.make_async_remote_copy(
            src_ref=V.at[e],
            dst_ref=R[e][0].at[pl.ds(0, ENTRIES)],
            send_sem=a_send.at[e],
            recv_sem=a_recv.at[e, 0],
            device_id=(1 - p, a, c),
            device_id_type=MESH,
        ).wait_send()

    def a_wait_recv(e, side):
        pltpu.make_async_remote_copy(
            src_ref=R[e][side],
            dst_ref=R[e][side],
            send_sem=a_send.at[e],
            recv_sem=a_recv.at[e, side],
            device_id=(1 - p, a, c),
            device_id_type=MESH,
        ).wait_recv()

    def b_copy(e, side, s, slot):
        return pltpu.make_async_remote_copy(
            src_ref=Q.at[e, side, pl.ds(8 * s, 10)],
            dst_ref=W[e][side].at[slot],
            send_sem=b_send.at[e, side, s],
            recv_sem=b_recv.at[e, side, slot],
            device_id=along(side, s - segment[side]),
            device_id_type=MESH,
        )

    def x_copy(e, side, way):
        return pltpu.make_async_remote_copy(
            src_ref=Q.at[e, side, 32 if way == 0 else 1],
            dst_ref=X[e][side].at[way, member[side]],
            send_sem=x_send.at[e, side, way],
            recv_sem=x_recv.at[e, side, way],
            device_id=along(side, (4 if way == 0 else -1) - segment[side]),
            device_id_type=MESH,
        )

    def x_wait_recv(e, side, way):
        pltpu.make_async_remote_copy(
            src_ref=X[e][side].at[way],
            dst_ref=X[e][side].at[way],
            send_sem=x_send.at[e, side, way],
            recv_sem=x_recv.at[e, side, way],
            device_id=along(side, 1),
            device_id_type=MESH,
        ).wait_recv()

    def greet():
        barrier = pltpu.get_barrier_semaphore()

        def hello(dev):
            pl.semaphore_signal(barrier, inc=1, device_id=dev, device_id_type=MESH)

        @pl.loop(0, LON)
        def _(k):
            hello((1 - p, a, k))

        @pl.loop(1, LAT)
        def _(k):
            hello((p, lax.rem(a + k, LAT), c))

        @pl.when(active[0])
        def _():
            @pl.loop(1, LON)
            def _(k):
                hello((p, a, lax.rem(c + k, LON)))

        awaited = jnp.where(active[0], LON + LAT - 1 + LON - 1, LON + LAT - 1)
        for dr, dc in steps:
            if not dc:
                continue
            there = exists(dr, dc)
            awaited += there.astype(jnp.int32)

            @pl.when(there)
            def _():
                hello((p, a + dr, c + dc))

        pl.semaphore_wait(barrier, awaited)

    def pass_on():
        @pl.loop(1, LAT)
        def _(k):
            pl.semaphore_signal(
                heard, inc=1, device_id=(p, lax.rem(a + k, LAT), c), device_id_type=MESH
            )

    def flat(e):
        return Y[e].reshape(20 * 20 * NF, NR)

    def interpolate(e, o_far):
        turn = (b + o_far) >> 7
        sub = lax.broadcasted_iota(jnp.int32, (NF, NR), 0)
        first = jnp.logical_or(sub == 1, sub == 4)
        second = jnp.logical_or(sub == 2, sub == 5)
        turned = jnp.logical_or(first, second)

        @pl.loop(0, ENTRIES)
        def _(g):
            i = lax.rem(g - turn + 2 * ENTRIES, ENTRIES)
            r0 = jnp.clip(base[0, i] - a * CB + 1, 1, CB)
            c0 = jnp.clip(base[1, i] - c * CB + 1, 1, CB)
            parts = []
            for x in range(4):
                acc = None
                for y in range(4):
                    term = weight[i, 0, 4 * x + y] * Y[e][r0 + x, c0 + y]
                    acc = term if acc is None else acc + term
                parts.append(acc)
            m = (parts[0] + parts[1]) + (parts[2] + parts[3])
            cosine = trig[0, pl.ds(i, 1), :]
            sine = trig[1, pl.ds(i, 1), :]
            partner = jnp.where(first, -pltpu.roll(m, NF - 1, 0), pltpu.roll(m, 1, 0))
            V[e, g] = jnp.where(turned, cosine * m + sine * partner, m)

    def is_self(side, s):
        here = segment[side] == s
        return here if side == 0 else jnp.logical_and(here, active[1])

    def side_loop(fn, roles):
        for side in range(2):
            @pl.when(roles[side])
            def _():
                fn(side)

    def spread(e, side, o_near):
        shift = (member[side] + o_near) >> 2
        for n in range(34):
            Q[e, side, n] = R[e][side][(n - 1 - shift + LOOP) & 31]
        for s in range(4):
            @pl.when(jnp.logical_not(is_self(side, s)))
            def _():
                b_copy(e, side, s, member[side]).start()
        for way, has in ((0, has_next), (1, has_prev)):
            @pl.when(has[side])
            def _():
                x_copy(e, side, way).start()

        @pl.when(active[side])
        def _():
            for n in range(10):
                W[e][side][member[side], n] = Q[e, side, 8 * segment[side] + n]

    def spread_wait_send(e, side):
        for s in range(4):
            @pl.when(jnp.logical_not(is_self(side, s)))
            def _():
                b_copy(e, side, s, member[side]).wait_send()
        for way, has in ((0, has_next), (1, has_prev)):
            @pl.when(has[side])
            def _():
                x_copy(e, side, way).wait_send()

    def collect(e, side, o_near):
        for s in range(4):
            @pl.when(own_slot[side] != s)
            def _():
                b_copy(e, side, 0, s).wait_recv()
        for way, has, edge in ((0, has_prev, 0), (1, has_next, 3)):
            @pl.when(jnp.logical_and(has[side], segment[side] == edge))
            def _():
                x_wait_recv(e, side, way)

        def place(cell):
            for rho in range(4):
                who = (rho - o_near + LOOP) & 3
                for n in range(10):
                    value = W[e][side][who, n]
                    if n in (0, 9):
                        way, has, edge = (0, has_prev, 0) if n == 0 else (1, has_next, 3)
                        far_value = jnp.where(has[side], X[e][side][way, who], 0.0)
                        value = jnp.where(segment[side] == edge, far_value, value)
                    r, q = cell(2 * n + rho // 2, rho % 2)
                    Y[e][r, q] = value

        cells = (
            ((on_top, lambda h, o: (o, h)), (on_bottom, lambda h, o: (18 + o, 19 - h))),
            ((on_right, lambda h, o: (h, 18 + o)), (on_left, lambda h, o: (19 - h, o))),
        )[side]
        for on, cell in cells:
            @pl.when(on)
            def _():
                place(cell)

    def curl(A, ap, am, bb, br, rh):
        a1, a2 = A(1, 0, 0), A(2, 0, 0)
        return (
            ri * ((A(2, 1, 0) * ap - A(2, -1, 0) * am) - (A(1, 0, 1) - A(1, 0, -1)) * bb),
            (A(0, 0, 1) - A(0, 0, -1)) * br - (above(a2) * cp - below(a2) * cm),
            (above(a1) * cp - below(a1) * cm) - (A(0, 1, 0) - A(0, -1, 0)) * rh,
        )

    rh = ri * H_THETA

    def first_values(ld, ap, am, bb, br):
        u = [ld(k, 0, 0) for k in range(3)]
        mag = [ld(3 + k, 0, 0) for k in range(3)]
        w = curl(lambda k, dg, dj: ld(k, dg, dj), ap, am, bb, br, rh)
        cur = curl(lambda k, dg, dj: ld(3 + k, dg, dj), ap, am, bb, br, rh)
        ind = cross(u, mag)
        el = [ind[k] - ETA * cur[k] for k in range(3)]
        t = ld(6, 0, 0)
        grad = [
            above(t) * dp - below(t) * dm,
            (ld(6, 1, 0) - ld(6, -1, 0)) * rh,
            (ld(6, 0, 1) - ld(6, 0, -1)) * br,
        ]
        head = ld(7, 0, 0) + np.float32(0.5) * (u[0] * u[0] + u[1] * u[1] + u[2] * u[2])
        return [*w, *cur, *el, *grad, head]

    def second_values(ld, mid, ap, am, bb, br):
        Wv, J, E, T, H = (lambda k, dg, dj, q=q: mid(q + k, dg, dj) for q in (0, 3, 6, 9, 12))
        cw = curl(Wv, ap, am, bb, br, rh)
        ce = curl(E, ap, am, bb, br, rh)
        u = [ld(k, 0, 0) for k in range(3)]
        mag = [ld(3 + k, 0, 0) for k in range(3)]
        w = [Wv(k, 0, 0) for k in range(3)]
        cur = [J(k, 0, 0) for k in range(3)]
        adv, lor = cross(u, w), cross(cur, mag)
        h = H(0, 0, 0)
        slope = (
            above(h) * dp - below(h) * dm,
            (H(0, 1, 0) - H(0, -1, 0)) * rh,
            (H(0, 0, 1) - H(0, 0, -1)) * br,
        )
        t0 = T(0, 0, 0)
        lap = (above(t0) * ep - below(t0) * em) + ri * (
            (T(1, 1, 0) * ap - T(1, -1, 0) * am) + (T(2, 0, 1) - T(2, 0, -1)) * bb
        )
        div = (above(u[0]) * ep - below(u[0]) * em) + ri * (
            (ld(1, 1, 0) * ap - ld(1, -1, 0) * am) + (ld(2, 0, 1) - ld(2, 0, -1)) * bb
        )
        ru = [adv[k] + lor[k] - slope[k] - NU * cw[k] for k in range(3)]
        ru[0] = ru[0] + LIFT * ld(6, 0, 0)
        rt = KAPPA * lap - (u[0] * t0 + u[1] * T(1, 0, 0) + u[2] * T(2, 0, 0))
        return [*ru, *ce, rt, -div]

    def eight(first, step):
        return pl.ds(first, 8) if step == 1 else pl.ds(first, 8, stride=step)

    def factors(i, column):
        if column:
            ap, am, bb = (slopes[k, pl.ds(i, 8), :] for k in range(3))
        else:
            ap, am, bb = (rows_s[k, a * CB + i + 3] for k in range(3))
        return ap, am, bb, ri * bb

    def first_pass(e, i, k, column=False):
        y = flat(e)
        step = 20 * NF if column else NF

        def ld(f, dg, dj):
            return y[eight(((i + 1 + dg) * 20 + k + 1 + dj) * NF + f, step), :]

        for q, v in enumerate(first_values(ld, *factors(i, column))):
            L1[eight((q * 18 + i) * 24 + k, 24 if column else 1), :] = v

    def second_pass(e, i, j, column=False):
        y = flat(e)
        step = 20 * NF if column else NF

        def ld(f, dg, dj):
            return y[eight(((i + 2 + dg) * 20 + j + 2 + dj) * NF + f, step), :]

        def mid(q, dg, dj):
            return L1[eight((q * 18 + i + 1 + dg) * 24 + j + 1 + dj, 24 if column else 1), :]

        sink = keep if e == 0 else finish
        for f, v in enumerate(second_values(ld, mid, *factors(i + 1, column))):
            sink(i, j, f, v, column)

    def whole(e):
        @pl.loop(0, 18)
        def _(i):
            for k in (0, 8, 10):
                first_pass(e, i, k)

        @pl.loop(0, 16)
        def _(i):
            for j in (0, 8):
                second_pass(e, i, j)

    def strips(e):
        @pl.when(active[0])
        def _():
            base_row = jnp.where(on_top, 0, CB)

            @pl.loop(0, 2)
            def _(n):
                for k in (0, 8, 10):
                    first_pass(e, base_row + n, k)

        @pl.when(active[1])
        def _():
            base_col = jnp.where(on_left, 0, CB)

            @pl.loop(0, 6)
            def _(n):
                first_pass(e, jnp.minimum(8 * (n // 2), 10), base_col + lax.rem(n, 2), True)

        @pl.when(active[0])
        def _():
            base_row = jnp.where(on_top, 0, CB - 2)

            @pl.loop(0, 2)
            def _(n):
                for j in (0, 8):
                    second_pass(e, base_row + n, j)

        @pl.when(active[1])
        def _():
            base_col = jnp.where(on_left, 0, CB - 2)

            @pl.loop(0, 4)
            def _(n):
                second_pass(e, 8 * (n // 2), base_col + lax.rem(n, 2), True)

    y_second = flat(1)
    y_first = flat(0)
    out_flat = out.reshape(CB * CB * NF, NR)

    def keep(i, j, f, v, column):
        K1[eight((f * CB + i) * CB + j, CB if column else 1), :] = v
        at = eight(((i + 2) * 20 + j + 2) * NF + f, 20 * NF if column else NF)
        y_second[at, :] = y_first[at, :] + DT * v

    def finish(i, j, f, v, column):
        k1 = K1[eight((f * CB + i) * CB + j, CB if column else 1), :]
        at = eight((i * CB + j) * NF + f, CB * NF if column else NF)
        out_flat[at, :] = np.float32(0.1) * (k1 + v)

    def fetch(k, src, dst):
        copy = pltpu.make_async_copy(src, dst, misc.at[k])
        copy.start()
        return copy

    corner = target_hbm.at[:, pl.ds(0, 128)]
    local = fetch(0, state, Y0.at[pl.ds(2, CB), pl.ds(2, CB)])
    small = [
        fetch(3, angle_hbm, angle),
        fetch(4, corner, near_at),
        fetch(5, base_hbm, base),
        fetch(6, weight_hbm, weight),
        fetch(7, rows, rows_s),
    ]
    greet()
    halo_start(0)
    pass_on()
    tell = pltpu.make_async_remote_copy(
        src_ref=corner, dst_ref=far, send_sem=misc.at[1], recv_sem=misc.at[2],
        device_id=(1 - p, a, c), device_id_type=MESH,
    )
    tell.start()

    for copy in small:
        copy.wait()
    trig[0] = jnp.zeros((16, NR), jnp.float32)
    for i in range(ENTRIES):
        trig[0, i : i + 1, :] = jnp.full((1, NR), angle[0, i], jnp.float32)
    turned = trig[0]
    trig[0] = jnp.cos(turned)
    trig[1] = jnp.sin(turned)

    for i in range(24):
        gi = jnp.minimum(a * CB + i + 3, NTH + 7)
        for k in range(3):
            slopes[k, i : i + 1, :] = jnp.full((1, NR), rows_s[k, gi], jnp.float32)

    tell.wait_recv()
    fetch(8, far, far_at).wait()
    local.wait()
    o_near = loop_place(near_at[0, 0], near_at[1, 0])
    o_far = loop_place(far_at[0, 0], far_at[1, 0])

    for e in range(2):
        halo_wait_recv(e)
        interpolate(e, o_far)
        if e == 0:
            pl.semaphore_wait(heard, LAT - 1)
        for g in range(ENTRIES):
            a_copy(e, g).start()
        whole(e)
        if e == 0:
            second_halo_start(late=False)

        def middle(side):
            a_wait_recv(e, side)
            spread(e, side, o_near)

        side_loop(middle, relays)
        side_loop(lambda side: collect(e, side, o_near), active)
        strips(e)
        if e == 0:
            second_halo_start(late=True)

    tell.wait_send()
    for e in range(2):
        halo_wait_send(e)
        a_wait_send(e)
        side_loop(lambda side: spread_wait_send(e, side), relays)


def loop_place(row, col):
    return jnp.where(
        row < 0,
        2 * col + row + 2,
        jnp.where(
            col >= NPH,
            2 * NPH + 2 * row + col - NPH,
            jnp.where(
                row >= NTH,
                2 * NPH + 2 * NTH + 2 * (NPH - 1 - col) + row - NTH,
                4 * NPH + 2 * NTH + 2 * (NTH - 1 - row) + col + 2,
            ),
        ),
    )


def per_device(state, rim_base, rim_weight, rim_angle, rim_target):
    vmem = pl.BlockSpec(memory_space=pltpu.VMEM)
    anywhere = pl.BlockSpec(memory_space=pl.ANY)
    f32 = jnp.float32
    result = pl.pallas_call(
        kernel,
        out_shape=jax.ShapeDtypeStruct((CB, CB, NF, NR), f32),
        in_specs=[anywhere, vmem] + [anywhere] * 5,
        out_specs=vmem,
        scratch_shapes=[
            pltpu.VMEM((20, 20, NF, NR), f32),
            pltpu.VMEM((20, 20, NF, NR), f32),
            pltpu.VMEM((NF * CB * CB, NR), f32),
            pltpu.VMEM((13 * 18 * 24, NR), f32),
            pltpu.VMEM((2, ENTRIES, NF, NR), f32),
            *[pltpu.VMEM((32, NF, NR), f32)] * 4,
            pltpu.VMEM((2, 2, 34, NF, NR), f32),
            *[pltpu.VMEM((4, 10, NF, NR), f32)] * 4,
            *[pltpu.VMEM((2, 4, NF, NR), f32)] * 4,
            pltpu.VMEM((2, 16, NR), f32),
            pltpu.VMEM((2, 128), jnp.int32),
            pltpu.SMEM((2, ENTRIES), jnp.int32),
            pltpu.SMEM((ENTRIES, 1, 16), f32),
            pltpu.SMEM((1, ENTRIES), f32),
            pltpu.SMEM((2, 128), jnp.int32),
            pltpu.SMEM((2, 128), jnp.int32),
            pltpu.SMEM((3, NTH + 8), f32),
            pltpu.VMEM((3, 24, NR), f32),
            pltpu.SemaphoreType.DMA((2, 8)),
            pltpu.SemaphoreType.DMA((2, 8)),
            pltpu.SemaphoreType.DMA((2,)),
            pltpu.SemaphoreType.DMA((2, 2)),
            pltpu.SemaphoreType.DMA((2, 2, 4)),
            pltpu.SemaphoreType.DMA((2, 2, 4)),
            pltpu.SemaphoreType.DMA((2, 2, 2)),
            pltpu.SemaphoreType.DMA((2, 2, 2)),
            pltpu.SemaphoreType.DMA((9,)),
            pltpu.SemaphoreType.REGULAR,
        ],
        compiler_params=pltpu.CompilerParams(
            collective_id=0, has_side_effects=True, vmem_limit_bytes=56 << 20
        ),
    )(
        jnp.asarray(row_table()),
        jnp.asarray(level_table()),
        state[0],
        rim_base[0].T,
        jnp.transpose(rim_weight, (1, 0, 2)),
        rim_angle,
        rim_target[0].T,
    )
    return result[None]


def solution(mesh):
    return jax.shard_map(
        per_device,
        mesh=mesh,
        in_specs=(
            P("panel", "lat", "lon", None, None),
            P("panel", ("lat", "lon"), None),
            P("panel", ("lat", "lon"), None),
            P("panel", ("lat", "lon")),
            P("panel", None, None),
        ),
        out_specs=P("panel", "lat", "lon", None, None),
        check_vma=False,
    )
```

```python
import math

import jax
import jax.numpy as jnp
import numpy as np
from jax import lax
from jax.experimental import pallas as pl
from jax.experimental.pallas import tpu as pltpu
from jax.sharding import PartitionSpec as P

NTH, NPH, NR, NF, CB = 128, 256, 128, 8, 16
LAT, LON = NTH // CB, NPH // CB
LOOP = 1536
ENTRIES = 12
ETA = np.float32(0.2)
NU = np.float32(0.2)
KAPPA = np.float32(0.3)
LIFT = np.float32(0.5)
DT = np.float32(0.2)
MESH = pl.DeviceIdType.MESH

DTHETA = math.pi / (2 * NTH)
DPHI = 1.5 * math.pi / NPH
H_THETA = np.float32(0.5 / DTHETA)


def row_table():
    g = np.arange(-4, NTH + 4)
    sine = lambda k: np.sin(math.pi / 4 + (k + 0.5) * DTHETA)
    s = sine(g)
    half = 0.5 / DTHETA
    return np.stack([sine(g + 1) * half / s, sine(g - 1) * half / s, 0.5 / DPHI / s]).astype(
        np.float32
    )


def level_table():
    scale = 2.0 * NTH / math.pi
    dr = 0.65 * scale / NR
    r = 0.35 * scale + (np.arange(NR) + 0.5) * dr
    half = 0.5 / dr
    up = np.where(np.arange(NR) < NR - 1, half, 0.0)
    down = np.where(np.arange(NR) > 0, half, 0.0)
    r_up, r_down = np.roll(r, -1), np.roll(r, 1)
    rows = [
        1 / r,
        up * r_up / r,
        down * r_down / r,
        up,
        down,
        up * r_up**2 / r**2,
        down * r_down**2 / r**2,
        0 * r,
    ]
    return np.stack(rows).astype(np.float32)


def above(x):
    return pltpu.roll(x, NR - 1, 1)


def below(x):
    return pltpu.roll(x, 1, 1)


def cross(a, b):
    return (
        a[1] * b[2] - a[2] * b[1],
        a[2] * b[0] - a[0] * b[2],
        a[0] * b[1] - a[1] * b[0],
    )


def kernel(
    rows, levels, state, base_hbm, weight_hbm, angle_hbm, target_hbm,
    out,
    Y0, Y1, K1, L1, V,
    R00, R01, R10, R11, Q, W00, W01, W10, W11, X00, X01, X10, X11,
    ZH, ZV, LZ, trig, far, base, weight, angle, near_at, far_at, rows_s, slopes,
    halo_send, halo_recv, a_send, a_recv, b_send, b_recv, x_send, x_recv, part_send, part_recv, wide_send, wide_recv, misc, heard,
):
    p, a, c = lax.axis_index("panel"), lax.axis_index("lat"), lax.axis_index("lon")
    b = a * LON + c
    Y = (Y0, Y1)
    R = ((R00, R01), (R10, R11))
    W = ((W00, W01), (W10, W11))
    X = ((X00, X01), (X10, X11))

    ri = levels[0:1, :]
    cp, cm = levels[1:2, :], levels[2:3, :]
    dp, dm = levels[3:4, :], levels[4:5, :]
    ep, em = levels[5:6, :], levels[6:7, :]

    steps = [(1, 1), (1, -1), (-1, 1), (-1, -1), (1, 0), (-1, 0), (0, 1), (0, -1)]

    def span(step):
        if step == 0:
            return 0, 2, CB
        return (CB - 2, 0, 2) if step > 0 else (0, CB + 2, 2)

    def halo_copy(e, k, part=None):
        dr, dc = steps[k]
        r0, rd, rn = span(dr)
        c0, cd, cn = span(dc)
        if part is not None:
            first, count = ((0, 2), (2, CB - 4), (CB - 2, 2))[part]
            if dr:
                c0, cd, cn = c0 + first, cd + first, count
            else:
                r0, rd, rn = r0 + first, rd + first, count
        if e == 0:
            src = state.at[pl.ds(r0, rn), pl.ds(c0, cn)]
        else:
            src = Y[1].at[pl.ds(r0 + 2, rn), pl.ds(c0 + 2, cn)]
        return pltpu.make_async_remote_copy(
            src_ref=src,
            dst_ref=Y[e].at[pl.ds(rd, rn), pl.ds(cd, cn)],
            send_sem=halo_send.at[e, k] if part is None else part_send.at[k, part],
            recv_sem=halo_recv.at[e, k] if part is None else part_recv.at[k, part],
            device_id=(p, a + dr, c + dc),
            device_id_type=MESH,
        )

    def exists(dr, dc):
        ok = None
        for pos, d, n in ((a, dr, LAT), (c, dc, LON)):
            if d:
                t = (pos < n - 1) if d > 0 else (pos > 0)
                ok = t if ok is None else jnp.logical_and(ok, t)
        return ok

    def halo_start(e):
        for k, (dr, dc) in enumerate(steps):
            @pl.when(exists(dr, dc))
            def _():
                halo_copy(e, k).start()

    def halo_wait_recv(e):
        for k, (dr, dc) in enumerate(steps):
            @pl.when(exists(-dr, -dc))
            def _():
                halo_copy(e, k).wait_recv()

    def halo_wait_send(e):
        for k, (dr, dc) in enumerate(steps):
            @pl.when(exists(dr, dc))
            def _():
                halo_copy(e, k).wait_send()

    def rim_part(dr, dc, part):
        if part == 1:
            return jnp.bool_(False)
        if dc:
            return on_top if part == 0 else on_bottom
        return on_left if part == 0 else on_right

    def second_halo(sending, act):
        for k, (dr, dc) in enumerate(steps):
            there = exists(dr, dc) if sending else exists(-dr, -dc)
            if dr and dc:
                @pl.when(there)
                def _():
                    act(halo_copy(1, k))
                continue
            for part in range(3):
                @pl.when(jnp.logical_and(there, jnp.logical_not(rim_part(dr, dc, part))))
                def _():
                    act(halo_copy(1, k, part))

    on_top, on_bottom = a == 0, a == LAT - 1
    on_right, on_left = c == LON - 1, c == 0
    active = (jnp.logical_or(on_top, on_bottom), jnp.logical_or(on_right, on_left))
    at_right = c >= LON // 2
    sign = (jnp.where(on_top, 1, -1), jnp.where(at_right, 1, -1))
    rank = (jnp.where(on_top, c, LON - 1 - c), jnp.where(at_right, a, LAT - 1 - a))
    groups = (LON // 4, LAT // 4)
    segment = tuple(lax.rem(u, 4) for u in rank)
    has_next = tuple(u // 4 < n - 1 for u, n in zip(rank, groups))
    has_prev = tuple(u // 4 > 0 for u in rank)
    group = rank[1] // 4
    beside = jnp.logical_and(c >= 2, c < LON - 2)
    relays = (
        active[0],
        jnp.logical_and(
            jnp.logical_or(c < 4, c >= LON - 4),
            segment[1] == jnp.where(beside, 2 - group, 1 + group),
        ),
    )
    member = (
        lax.rem(c, 4) ^ 2,
        2 * jnp.where(at_right, beside, jnp.logical_not(beside)).astype(jnp.int32) + lax.rem(c, 2),
    )
    own_slot = (member[0], jnp.where(relays[1], member[1], -1))

    def along(side, step):
        if side == 0:
            return (p, a, c + sign[0] * step)
        return (p, a + sign[1] * step, jnp.where(at_right, LON - 1, 0))

    def wide_copy(side, way):
        first = (jnp.where(on_top, 0, CB - 4), jnp.where(on_left, 0, CB - 4))[side]
        lands = (jnp.where(on_top, 2, 0), jnp.where(on_left, 2, 0))[side]
        near, far_end = (CB - 4, 0) if way > 0 else (2, CB + 6)
        if side == 0:
            src = state.at[pl.ds(first, 4), pl.ds(near, 2)]
            dst = ZH.at[pl.ds(lands, 4), pl.ds(far_end, 2)]
            dev = (p, a, c + way)
        else:
            src = state.at[pl.ds(near, 2), pl.ds(first, 4)]
            dst = ZV.at[pl.ds(far_end, 2), pl.ds(lands, 4)]
            dev = (p, a + way, c)
        k = 0 if way > 0 else 1
        return pltpu.make_async_remote_copy(
            src_ref=src, dst_ref=dst, send_sem=wide_send.at[side, k],
            recv_sem=wide_recv.at[side, k], device_id=dev, device_id_type=MESH,
        )

    def wide(side, sending, act):
        for way in (1, -1):
            step = way if sending else -way
            there = exists(0, step) if side == 0 else exists(step, 0)

            @pl.when(there)
            def _():
                act(wide_copy(side, way))

    m_src = lax.rem(c, 4)

    def a_copy(e, g):
        half, core = m_src // 2, lax.rem(m_src, 2)
        if g < 4:
            side, dev = 0, (1 - p, 0, 4 * g + (m_src ^ 2))
        elif g < 6:
            n = g - 4
            place = 4 * n + jnp.where(half == 0, 1 + n, 2 - n)
            side, dev = 1, (1 - p, place, LON - 2 - 2 * half + core)
        elif g < 10:
            side, dev = 0, (1 - p, LAT - 1, 4 * (9 - g) + (m_src ^ 2))
        else:
            n = g - 10
            place = 4 * n + jnp.where(half == 1, 1 + n, 2 - n)
            side, dev = 1, (1 - p, LAT - 1 - place, 2 - 2 * half + core)
        return pltpu.make_async_remote_copy(
            src_ref=V.at[e, g],
            dst_ref=R[e][side].at[4 * a + c // 4],
            send_sem=a_send.at[e],
            recv_sem=a_recv.at[e, side],
            device_id=dev,
            device_id_type=MESH,
        )

    def a_wait_send(e):
        pltpu.make_async_remote_copy(
            src_ref=V.at[e],
            dst_ref=R[e][0].at[pl.ds(0, ENTRIES)],
            send_sem=a_send.at[e],
            recv_sem=a_recv.at[e, 0],
            device_id=(1 - p, a, c),
            device_id_type=MESH,
        ).wait_send()

    def a_wait_recv(e, side):
        pltpu.make_async_remote_copy(
            src_ref=R[e][side],
            dst_ref=R[e][side],
            send_sem=a_send.at[e],
            recv_sem=a_recv.at[e, side],
            device_id=(1 - p, a, c),
            device_id_type=MESH,
        ).wait_recv()

    def b_copy(e, side, s, slot, k):
        return pltpu.make_async_remote_copy(
            src_ref=Q.at[e, side, pl.ds(8 * s, 12)],
            dst_ref=W[e][side].at[slot],
            send_sem=b_send.at[e, side, k],
            recv_sem=b_recv.at[e, side, slot],
            device_id=along(side, s - segment[side]),
            device_id_type=MESH,
        )

    def x_copy(e, side, way):
        return pltpu.make_async_remote_copy(
            src_ref=Q.at[e, side, pl.ds(32 if way == 0 else 2, 2)],
            dst_ref=X[e][side].at[way, member[side]],
            send_sem=x_send.at[e, side, way],
            recv_sem=x_recv.at[e, side, way],
            device_id=along(side, (4 if way == 0 else -1) - segment[side]),
            device_id_type=MESH,
        )

    def x_wait_recv(e, side, way):
        pltpu.make_async_remote_copy(
            src_ref=X[e][side].at[way],
            dst_ref=X[e][side].at[way],
            send_sem=x_send.at[e, side, way],
            recv_sem=x_recv.at[e, side, way],
            device_id=along(side, 1),
            device_id_type=MESH,
        ).wait_recv()

    def greet():
        barrier = pltpu.get_barrier_semaphore()

        def hello(dev):
            pl.semaphore_signal(barrier, inc=1, device_id=dev, device_id_type=MESH)

        @pl.loop(0, LON)
        def _(k):
            hello((1 - p, a, k))

        @pl.loop(1, LAT)
        def _(k):
            hello((p, lax.rem(a + k, LAT), c))

        @pl.when(active[0])
        def _():
            @pl.loop(1, LON)
            def _(k):
                hello((p, a, lax.rem(c + k, LON)))

        awaited = jnp.where(active[0], LON + LAT - 1 + LON - 1, LON + LAT - 1)
        for dr, dc in steps:
            if not dc:
                continue
            there = exists(dr, dc)
            awaited += there.astype(jnp.int32)

            @pl.when(there)
            def _():
                hello((p, a + dr, c + dc))

        return lambda: pl.semaphore_wait(barrier, awaited)

    def pass_on():
        @pl.loop(1, LAT)
        def _(k):
            pl.semaphore_signal(
                heard, inc=1, device_id=(p, lax.rem(a + k, LAT), c), device_id_type=MESH
            )

    def flat(e):
        return Y[e].reshape(20 * 20 * NF, NR)

    def interpolate(e, o_far):
        turn = (b + o_far) >> 7
        sub = lax.broadcasted_iota(jnp.int32, (NF, NR), 0)
        first = jnp.logical_or(sub == 1, sub == 4)
        second = jnp.logical_or(sub == 2, sub == 5)
        turned = jnp.logical_or(first, second)

        @pl.loop(0, ENTRIES)
        def _(g):
            i = lax.rem(g - turn + 2 * ENTRIES, ENTRIES)
            r0 = jnp.clip(base[0, i] - a * CB + 1, 1, CB)
            c0 = jnp.clip(base[1, i] - c * CB + 1, 1, CB)
            parts = []
            for x in range(4):
                acc = None
                for y in range(4):
                    term = weight[i, 0, 4 * x + y] * Y[e][r0 + x, c0 + y]
                    acc = term if acc is None else acc + term
                parts.append(acc)
            m = (parts[0] + parts[1]) + (parts[2] + parts[3])
            cosine = trig[0, pl.ds(i, 1), :]
            sine = trig[1, pl.ds(i, 1), :]
            partner = jnp.where(first, -pltpu.roll(m, NF - 1, 0), pltpu.roll(m, 1, 0))
            V[e, g] = jnp.where(turned, cosine * m + sine * partner, m)

    def is_self(side, s):
        here = segment[side] == s
        return here if side == 0 else jnp.logical_and(here, active[1])

    def side_loop(fn, roles):
        for side in range(2):
            @pl.when(roles[side])
            def _():
                fn(side)

    def spread(e, side, o_near):
        shift = (member[side] + o_near) >> 2
        for n in range(36):
            Q[e, side, n] = R[e][side][(n - 2 - shift + LOOP) & 31]
        for way, has in ((0, has_next), (1, has_prev)):
            @pl.when(has[side])
            def _():
                x_copy(e, side, way).start()
        for k in (2, 3, 1, 0):
            s = segment[side] ^ k

            @pl.when(jnp.logical_not(is_self(side, s)))
            def _():
                b_copy(e, side, s, member[side], k).start()

        @pl.when(active[side])
        def _():
            for n in range(12):
                W[e][side][member[side], n] = Q[e, side, 8 * segment[side] + n]

    def spread_wait_send(e, side):
        for k in range(4):
            s = segment[side] ^ k

            @pl.when(jnp.logical_not(is_self(side, s)))
            def _():
                b_copy(e, side, s, member[side], k).wait_send()
        for way, has in ((0, has_next), (1, has_prev)):
            @pl.when(has[side])
            def _():
                x_copy(e, side, way).wait_send()

    def collect(e, side, o_near):
        for s in range(4):
            @pl.when(own_slot[side] != s)
            def _():
                b_copy(e, side, 0, s, 0).wait_recv()
        for way, has, edge in ((0, has_prev, 0), (1, has_next, 3)):
            @pl.when(jnp.logical_and(has[side], segment[side] == edge))
            def _():
                x_wait_recv(e, side, way)

        def place(cell, far_cell):
            for rho in range(4):
                who = (rho - o_near + LOOP) & 3
                for n in range(0 if e == 0 else 1, 12 if e == 0 else 11):
                    value = W[e][side][who, n]
                    if n < 2 or n > 9:
                        way, has, edge = (0, has_prev, 0) if n < 2 else (1, has_next, 3)
                        far_value = jnp.where(has[side], X[e][side][way, who, n if n < 2 else n - 10], 0.0)
                        value = jnp.where(segment[side] == edge, far_value, value)
                    h, o = 2 * n + rho // 2, rho % 2
                    if 1 <= n <= 10:
                        r, q = cell(h - 2, o)
                        Y[e][r, q] = value
                    else:
                        r, q = far_cell(h, o)
                        (ZH, ZV)[side][r, q] = value

        cells = (
            (
                (on_top, lambda h, o: (o, h), lambda h, o: (o, h)),
                (on_bottom, lambda h, o: (18 + o, 19 - h), lambda h, o: (4 + o, 23 - h)),
            ),
            (
                (on_right, lambda h, o: (h, 18 + o), lambda h, o: (h, 4 + o)),
                (on_left, lambda h, o: (19 - h, o), lambda h, o: (23 - h, o)),
            ),
        )[side]
        for on, cell, far_cell in cells:
            @pl.when(on)
            def _():
                place(cell, far_cell)

    def curl(A, ap, am, bb, br, rh):
        a1, a2 = A(1, 0, 0), A(2, 0, 0)
        return (
            ri * ((A(2, 1, 0) * ap - A(2, -1, 0) * am) - (A(1, 0, 1) - A(1, 0, -1)) * bb),
            (A(0, 0, 1) - A(0, 0, -1)) * br - (above(a2) * cp - below(a2) * cm),
            (above(a1) * cp - below(a1) * cm) - (A(0, 1, 0) - A(0, -1, 0)) * rh,
        )

    rh = ri * H_THETA

    def first_values(ld, ap, am, bb, br):
        u = [ld(k, 0, 0) for k in range(3)]
        mag = [ld(3 + k, 0, 0) for k in range(3)]
        w = curl(lambda k, dg, dj: ld(k, dg, dj), ap, am, bb, br, rh)
        cur = curl(lambda k, dg, dj: ld(3 + k, dg, dj), ap, am, bb, br, rh)
        ind = cross(u, mag)
        el = [ind[k] - ETA * cur[k] for k in range(3)]
        t = ld(6, 0, 0)
        grad = [
            above(t) * dp - below(t) * dm,
            (ld(6, 1, 0) - ld(6, -1, 0)) * rh,
            (ld(6, 0, 1) - ld(6, 0, -1)) * br,
        ]
        head = ld(7, 0, 0) + np.float32(0.5) * (u[0] * u[0] + u[1] * u[1] + u[2] * u[2])
        return [*w, *cur, *el, *grad, head]

    def second_values(ld, mid, ap, am, bb, br):
        Wv, J, E, T, H = (lambda k, dg, dj, q=q: mid(q + k, dg, dj) for q in (0, 3, 6, 9, 12))
        cw = curl(Wv, ap, am, bb, br, rh)
        ce = curl(E, ap, am, bb, br, rh)
        u = [ld(k, 0, 0) for k in range(3)]
        mag = [ld(3 + k, 0, 0) for k in range(3)]
        w = [Wv(k, 0, 0) for k in range(3)]
        cur = [J(k, 0, 0) for k in range(3)]
        adv, lor = cross(u, w), cross(cur, mag)
        h = H(0, 0, 0)
        slope = (
            above(h) * dp - below(h) * dm,
            (H(0, 1, 0) - H(0, -1, 0)) * rh,
            (H(0, 0, 1) - H(0, 0, -1)) * br,
        )
        t0 = T(0, 0, 0)
        lap = (above(t0) * ep - below(t0) * em) + ri * (
            (T(1, 1, 0) * ap - T(1, -1, 0) * am) + (T(2, 0, 1) - T(2, 0, -1)) * bb
        )
        div = (above(u[0]) * ep - below(u[0]) * em) + ri * (
            (ld(1, 1, 0) * ap - ld(1, -1, 0) * am) + (ld(2, 0, 1) - ld(2, 0, -1)) * bb
        )
        ru = [adv[k] + lor[k] - slope[k] - NU * cw[k] for k in range(3)]
        ru[0] = ru[0] + LIFT * ld(6, 0, 0)
        rt = KAPPA * lap - (u[0] * t0 + u[1] * T(1, 0, 0) + u[2] * T(2, 0, 0))
        return [*ru, *ce, rt, -div]

    def eight(first, step):
        return pl.ds(first, 8) if step == 1 else pl.ds(first, 8, stride=step)

    def factors(i, column):
        if column:
            ap, am, bb = (slopes[k, pl.ds(i + 3, 8), :] for k in range(3))
        else:
            ap, am, bb = (rows_s[k, a * CB + i + 4] for k in range(3))
        return ap, am, bb, ri * bb

    def block_view(e):
        return (
            flat(e), 20, lambda i, j: (i + 2) * 20 + j + 2,
            L1, 24, lambda q, i, j: (q * 18 + i + 1) * 24 + j + 1,
        )

    def row_view(r0):
        return (
            ZH.reshape(6 * 24 * NF, NR), 24, lambda i, j: (i - r0) * 24 + j + 4,
            LZ, 24, lambda q, i, j: (q * 4 + i - r0 - 1) * 24 + j + 3,
        )

    def column_view(c0):
        return (
            ZV.reshape(24 * 6 * NF, NR), 6, lambda i, j: (i + 4) * 6 + j - c0,
            LZ, 4, lambda q, i, j: (q * 24 + i + 3) * 4 + j - c0 - 1,
        )

    def loader(view, i, j, column):
        cells, width, cell = view[:3]
        step = width * NF if column else NF
        return lambda f, dg, dj: cells[eight(cell(i + dg, j + dj) * NF + f, step), :]

    def first_pass(view, i, j, column=False):
        store, width, place = view[3:]
        values = first_values(loader(view, i, j, column), *factors(i, column))
        for q, v in enumerate(values):
            store[eight(place(q, i, j), width if column else 1), :] = v

    def second_pass(e, view, i, j, column=False):
        store, width, place = view[3:]

        def mid(q, dg, dj):
            return store[eight(place(q, i + dg, j + dj), width if column else 1), :]

        sink = keep if e == 0 else finish
        values = second_values(loader(view, i, j, column), mid, *factors(i, column))
        for f, v in enumerate(values):
            sink(i, j, f, v, column)

    def whole(e):
        view = block_view(e)

        @pl.loop(0, 18)
        def _(n):
            for j in (-1, 7, 9):
                first_pass(view, n - 1, j)

        @pl.loop(0, 16)
        def _(i):
            for j in (0, 8):
                second_pass(e, view, i, j)

    row_edge = jnp.where(on_top, -2, CB - 4)
    column_edge = jnp.where(on_left, -2, CB - 4)

    def wide_strips():
        @pl.when(active[0])
        def _():
            wide(0, False, lambda copy: copy.wait_recv())
            ZH[:, pl.ds(2, 20)] = Y0[pl.ds(row_edge + 2, 6)]
            view = row_view(row_edge)
            for n in range(4):
                for j in (-3, 5, 11):
                    first_pass(view, row_edge + 1 + n, j)
            for n in range(2):
                for j in (-2, 6, 10):
                    second_pass(0, view, row_edge + 2 + n, j)

        @pl.when(active[1])
        def _():
            wide(1, False, lambda copy: copy.wait_recv())
            ZV[pl.ds(2, 20)] = Y0[:, pl.ds(column_edge + 2, 6)]
            view = column_view(column_edge)
            for n in range(4):
                for i in (-3, 5, 11):
                    first_pass(view, i, column_edge + 1 + n, True)
            for n in range(2):
                for i in (-2, 6, 10):
                    second_pass(0, view, i, column_edge + 2 + n, True)

    def strips():
        view = block_view(1)

        @pl.when(active[0])
        def _():
            first = jnp.where(on_top, -1, CB - 1)
            for n in range(2):
                for j in (-1, 7, 9):
                    first_pass(view, first + n, j)

        @pl.when(active[1])
        def _():
            first = jnp.where(on_left, -1, CB - 1)
            for n in range(2):
                for i in (-1, 7, 9):
                    first_pass(view, i, first + n, True)

        @pl.when(active[0])
        def _():
            for n in range(2):
                for j in (0, 8):
                    second_pass(1, view, row_edge + 2 + n, j)

        @pl.when(active[1])
        def _():
            for n in range(2):
                for i in (0, 8):
                    second_pass(1, view, i, column_edge + 2 + n, True)

    y_second = flat(1)
    y_first = flat(0)
    out_flat = out.reshape(CB * CB * NF, NR)

    def keep(i, j, f, v, column):
        K1[eight((f * 20 + i + 2) * 24 + j + 4, 24 if column else 1), :] = v
        at = eight(((i + 2) * 20 + j + 2) * NF + f, 20 * NF if column else NF)
        y_second[at, :] = y_first[at, :] + DT * v

    def finish(i, j, f, v, column):
        k1 = K1[eight((f * 20 + i + 2) * 24 + j + 4, 24 if column else 1), :]
        at = eight((i * CB + j) * NF + f, CB * NF if column else NF)
        out_flat[at, :] = np.float32(0.1) * (k1 + v)

    def fetch(k, src, dst):
        copy = pltpu.make_async_copy(src, dst, misc.at[k])
        copy.start()
        return copy

    hear = greet()
    corner = target_hbm.at[:, pl.ds(0, 128)]
    local = fetch(0, state, Y0.at[pl.ds(2, CB), pl.ds(2, CB)])
    small = [
        fetch(3, angle_hbm, angle),
        fetch(4, corner, near_at),
        fetch(5, base_hbm, base),
        fetch(6, weight_hbm, weight),
        fetch(7, rows, rows_s),
    ]
    hear()
    halo_start(0)
    pass_on()
    tell = pltpu.make_async_remote_copy(
        src_ref=corner, dst_ref=far, send_sem=misc.at[1], recv_sem=misc.at[2],
        device_id=(1 - p, a, c), device_id_type=MESH,
    )
    tell.start()
    side_loop(lambda side: wide(side, True, lambda copy: copy.start()), active)

    for copy in small:
        copy.wait()
    trig[0] = jnp.zeros((16, NR), jnp.float32)
    for i in range(ENTRIES):
        trig[0, i : i + 1, :] = jnp.full((1, NR), angle[0, i], jnp.float32)
    turned = trig[0]
    trig[0] = jnp.cos(turned)
    trig[1] = jnp.sin(turned)

    for i in range(24):
        gi = jnp.minimum(a * CB + i + 1, NTH + 7)
        for k in range(3):
            slopes[k, i : i + 1, :] = jnp.full((1, NR), rows_s[k, gi], jnp.float32)

    tell.wait_recv()
    fetch(8, far, far_at).wait()
    local.wait()
    o_near = loop_place(near_at[0, 0], near_at[1, 0])
    o_far = loop_place(far_at[0, 0], far_at[1, 0])

    for e in range(2):
        if e == 0:
            halo_wait_recv(0)
        else:
            second_halo(False, lambda copy: copy.wait_recv())
        interpolate(e, o_far)
        if e == 0:
            pl.semaphore_wait(heard, LAT - 1)
        for g in range(ENTRIES):
            a_copy(e, g).start()
        whole(e)
        if e == 0:
            second_halo(True, lambda copy: copy.start())

        def middle(side):
            a_wait_recv(e, side)
            spread(e, side, o_near)

        side_loop(middle, relays)
        side_loop(lambda side: collect(e, side, o_near), active)
        if e == 0:
            wide_strips()
        else:
            strips()

    tell.wait_send()
    for e in range(2):
        if e == 0:
            halo_wait_send(0)
            side_loop(lambda side: wide(side, True, lambda copy: copy.wait_send()), active)
        else:
            second_halo(True, lambda copy: copy.wait_send())
        a_wait_send(e)
        side_loop(lambda side: spread_wait_send(e, side), relays)


def loop_place(row, col):
    return jnp.where(
        row < 0,
        2 * col + row + 2,
        jnp.where(
            col >= NPH,
            2 * NPH + 2 * row + col - NPH,
            jnp.where(
                row >= NTH,
                2 * NPH + 2 * NTH + 2 * (NPH - 1 - col) + row - NTH,
                4 * NPH + 2 * NTH + 2 * (NTH - 1 - row) + col + 2,
            ),
        ),
    )


def per_device(state, rim_base, rim_weight, rim_angle, rim_target):
    vmem = pl.BlockSpec(memory_space=pltpu.VMEM)
    anywhere = pl.BlockSpec(memory_space=pl.ANY)
    f32 = jnp.float32
    result = pl.pallas_call(
        kernel,
        out_shape=jax.ShapeDtypeStruct((CB, CB, NF, NR), f32),
        in_specs=[anywhere, vmem] + [anywhere] * 5,
        out_specs=vmem,
        scratch_shapes=[
            pltpu.VMEM((20, 20, NF, NR), f32),
            pltpu.VMEM((20, 20, NF, NR), f32),
            pltpu.VMEM((NF * 20 * 24, NR), f32),
            pltpu.VMEM((13 * 18 * 24, NR), f32),
            pltpu.VMEM((2, ENTRIES, NF, NR), f32),
            *[pltpu.VMEM((32, NF, NR), f32)] * 4,
            pltpu.VMEM((2, 2, 36, NF, NR), f32),
            *[pltpu.VMEM((4, 12, NF, NR), f32)] * 4,
            *[pltpu.VMEM((2, 4, 2, NF, NR), f32)] * 4,
            pltpu.VMEM((6, 24, NF, NR), f32),
            pltpu.VMEM((24, 6, NF, NR), f32),
            pltpu.VMEM((13 * 96 + 8, NR), f32),
            pltpu.VMEM((2, 16, NR), f32),
            pltpu.VMEM((2, 128), jnp.int32),
            pltpu.SMEM((2, ENTRIES), jnp.int32),
            pltpu.SMEM((ENTRIES, 1, 16), f32),
            pltpu.SMEM((1, ENTRIES), f32),
            pltpu.SMEM((2, 128), jnp.int32),
            pltpu.SMEM((2, 128), jnp.int32),
            pltpu.SMEM((3, NTH + 8), f32),
            pltpu.VMEM((3, 24, NR), f32),
            pltpu.SemaphoreType.DMA((2, 8)),
            pltpu.SemaphoreType.DMA((2, 8)),
            pltpu.SemaphoreType.DMA((2,)),
            pltpu.SemaphoreType.DMA((2, 2)),
            pltpu.SemaphoreType.DMA((2, 2, 4)),
            pltpu.SemaphoreType.DMA((2, 2, 4)),
            pltpu.SemaphoreType.DMA((2, 2, 2)),
            pltpu.SemaphoreType.DMA((2, 2, 2)),
            pltpu.SemaphoreType.DMA((8, 3)),
            pltpu.SemaphoreType.DMA((8, 3)),
            pltpu.SemaphoreType.DMA((2, 2)),
            pltpu.SemaphoreType.DMA((2, 2)),
            pltpu.SemaphoreType.DMA((9,)),
            pltpu.SemaphoreType.REGULAR,
        ],
        compiler_params=pltpu.CompilerParams(
            collective_id=0, has_side_effects=True, vmem_limit_bytes=56 << 20
        ),
    )(
        jnp.asarray(row_table()),
        jnp.asarray(level_table()),
        state[0],
        rim_base[0].T,
        jnp.transpose(rim_weight, (1, 0, 2)),
        rim_angle,
        rim_target[0].T,
    )
    return result[None]


def solution(mesh):
    return jax.shard_map(
        per_device,
        mesh=mesh,
        in_specs=(
            P("panel", "lat", "lon", None, None),
            P("panel", ("lat", "lon"), None),
            P("panel", ("lat", "lon"), None),
            P("panel", ("lat", "lon")),
            P("panel", None, None),
        ),
        out_specs=P("panel", "lat", "lon", None, None),
        check_vma=False,
    )
```

```python
import math

import jax
import jax.numpy as jnp
import numpy as np
from jax import lax
from jax.experimental import pallas as pl
from jax.experimental.pallas import tpu as pltpu
from jax.sharding import PartitionSpec as P

NTH, NPH, NR, NF, CB = 128, 256, 128, 8, 16
LAT, LON = NTH // CB, NPH // CB
LOOP = 1536
ENTRIES = 12
ETA = np.float32(0.2)
NU = np.float32(0.2)
KAPPA = np.float32(0.3)
LIFT = np.float32(0.5)
DT = np.float32(0.2)
MESH = pl.DeviceIdType.MESH

DTHETA = math.pi / (2 * NTH)
DPHI = 1.5 * math.pi / NPH
H_THETA = np.float32(0.5 / DTHETA)


def row_table():
    g = np.arange(-4, NTH + 4)
    sine = lambda k: np.sin(math.pi / 4 + (k + 0.5) * DTHETA)
    s = sine(g)
    half = 0.5 / DTHETA
    return np.stack([sine(g + 1) * half / s, sine(g - 1) * half / s, 0.5 / DPHI / s]).astype(
        np.float32
    )


def level_table():
    scale = 2.0 * NTH / math.pi
    dr = 0.65 * scale / NR
    r = 0.35 * scale + (np.arange(NR) + 0.5) * dr
    half = 0.5 / dr
    up = np.where(np.arange(NR) < NR - 1, half, 0.0)
    down = np.where(np.arange(NR) > 0, half, 0.0)
    r_up, r_down = np.roll(r, -1), np.roll(r, 1)
    rows = [
        1 / r,
        up * r_up / r,
        down * r_down / r,
        up,
        down,
        up * r_up**2 / r**2,
        down * r_down**2 / r**2,
        0 * r,
    ]
    return np.stack(rows).astype(np.float32)


def above(x):
    return pltpu.roll(x, NR - 1, 1)


def below(x):
    return pltpu.roll(x, 1, 1)


def cross(a, b):
    return (
        a[1] * b[2] - a[2] * b[1],
        a[2] * b[0] - a[0] * b[2],
        a[0] * b[1] - a[1] * b[0],
    )


def kernel(
    rows, levels, state, base_hbm, weight_hbm, angle_hbm, target_hbm,
    out,
    Y0, Y1, K1, L1, V,
    R00, R01, R10, R11, Q, W00, W01, W10, W11, X00, X01, X10, X11,
    ZH, ZV, LZ, trig, far, base, weight, angle, near_at, far_at, rows_s, levels_s, slopes, O,
    halo_send, halo_recv, a_send, a_recv, b_send, b_recv, x_send, x_recv, part_send, part_recv, wide_send, wide_recv, misc, heard,
):
    p, a, c = lax.axis_index("panel"), lax.axis_index("lat"), lax.axis_index("lon")
    b = a * LON + c
    Y = (Y0, Y1)
    R = ((R00, R01), (R10, R11))
    W = ((W00, W01), (W10, W11))
    X = ((X00, X01), (X10, X11))

    steps = [(1, 1), (1, -1), (-1, 1), (-1, -1), (1, 0), (-1, 0), (0, 1), (0, -1)]

    def span(step):
        if step == 0:
            return 0, 2, CB
        return (CB - 2, 0, 2) if step > 0 else (0, CB + 2, 2)

    def halo_copy(e, k, part=None):
        dr, dc = steps[k]
        r0, rd, rn = span(dr)
        c0, cd, cn = span(dc)
        if part is not None:
            first, count = ((0, 2), (2, CB - 4), (CB - 2, 2))[part]
            if dr:
                c0, cd, cn = c0 + first, cd + first, count
            else:
                r0, rd, rn = r0 + first, rd + first, count
        if e == 0:
            src = state.at[pl.ds(r0, rn), pl.ds(c0, cn)]
        else:
            src = Y[1].at[pl.ds(r0 + 2, rn), pl.ds(c0 + 2, cn)]
        return pltpu.make_async_remote_copy(
            src_ref=src,
            dst_ref=Y[e].at[pl.ds(rd, rn), pl.ds(cd, cn)],
            send_sem=halo_send.at[e, k] if part is None else part_send.at[k, part],
            recv_sem=halo_recv.at[e, k] if part is None else part_recv.at[k, part],
            device_id=(p, a + dr, c + dc),
            device_id_type=MESH,
        )

    def exists(dr, dc):
        ok = None
        for pos, d, n in ((a, dr, LAT), (c, dc, LON)):
            if d:
                t = (pos < n - 1) if d > 0 else (pos > 0)
                ok = t if ok is None else jnp.logical_and(ok, t)
        return ok

    def halo_start(e):
        for k, (dr, dc) in enumerate(steps):
            @pl.when(exists(dr, dc))
            def _():
                halo_copy(e, k).start()

    def halo_wait_recv(e):
        for k, (dr, dc) in enumerate(steps):
            @pl.when(exists(-dr, -dc))
            def _():
                halo_copy(e, k).wait_recv()

    def halo_wait_send(e):
        for k, (dr, dc) in enumerate(steps):
            @pl.when(exists(dr, dc))
            def _():
                halo_copy(e, k).wait_send()

    def rim_part(dr, dc, part):
        if part == 1:
            return jnp.bool_(False)
        if dc:
            return on_top if part == 0 else on_bottom
        return on_left if part == 0 else on_right

    def second_halo(sending, act):
        for k, (dr, dc) in enumerate(steps):
            there = exists(dr, dc) if sending else exists(-dr, -dc)
            if dr and dc:
                @pl.when(there)
                def _():
                    act(halo_copy(1, k))
                continue
            for part in range(3):
                @pl.when(jnp.logical_and(there, jnp.logical_not(rim_part(dr, dc, part))))
                def _():
                    act(halo_copy(1, k, part))

    on_top, on_bottom = a == 0, a == LAT - 1
    on_right, on_left = c == LON - 1, c == 0
    active = (jnp.logical_or(on_top, on_bottom), jnp.logical_or(on_right, on_left))
    at_right = c >= LON // 2
    sign = (jnp.where(on_top, 1, -1), jnp.where(at_right, 1, -1))
    rank = (jnp.where(on_top, c, LON - 1 - c), jnp.where(at_right, a, LAT - 1 - a))
    groups = (LON // 4, LAT // 4)
    segment = tuple(lax.rem(u, 4) for u in rank)
    has_next = tuple(u // 4 < n - 1 for u, n in zip(rank, groups))
    has_prev = tuple(u // 4 > 0 for u in rank)
    relays = (active[0], jnp.logical_or(c < 2, c >= LON - 2))
    member = (
        lax.rem(c, 4) ^ 2,
        2 * lax.rem(segment[1], 2) + lax.rem(c, 2),
    )
    own_slot = member
    to_next = (has_next[0], jnp.logical_and(has_next[1], segment[1] >= 2))
    to_prev = (has_prev[0], jnp.logical_and(has_prev[1], segment[1] < 2))

    def along(side, step):
        if side == 0:
            return (p, a, c + sign[0] * step)
        return (p, a + sign[1] * step, jnp.where(at_right, LON - 1, 0))

    def wide_copy(side, way):
        first = (jnp.where(on_top, 0, CB - 4), jnp.where(on_left, 0, CB - 4))[side]
        lands = (jnp.where(on_top, 2, 0), jnp.where(on_left, 2, 0))[side]
        near, far_end = (CB - 4, 0) if way > 0 else (2, CB + 6)
        if side == 0:
            src = state.at[pl.ds(first, 4), pl.ds(near, 2)]
            dst = ZH.at[pl.ds(lands, 4), pl.ds(far_end, 2)]
            dev = (p, a, c + way)
        else:
            src = state.at[pl.ds(near, 2), pl.ds(first, 4)]
            dst = ZV.at[pl.ds(far_end, 2), pl.ds(lands, 4)]
            dev = (p, a + way, c)
        k = 0 if way > 0 else 1
        return pltpu.make_async_remote_copy(
            src_ref=src, dst_ref=dst, send_sem=wide_send.at[side, k],
            recv_sem=wide_recv.at[side, k], device_id=dev, device_id_type=MESH,
        )

    def wide(side, sending, act):
        for way in (1, -1):
            step = way if sending else -way
            there = exists(0, step) if side == 0 else exists(step, 0)

            @pl.when(there)
            def _():
                act(wide_copy(side, way))

    m_src = lax.rem(c, 4)

    def a_copy(e, g, again=0):
        half, core = m_src // 2, lax.rem(m_src, 2)
        if g < 4:
            side, dev = 0, (1 - p, 0, 4 * g + (m_src ^ 2))
        elif g < 6:
            side, dev = 1, (1 - p, 4 * (g - 4) + 2 * again + half, LON - 2 + core)
        elif g < 10:
            side, dev = 0, (1 - p, LAT - 1, 4 * (9 - g) + (m_src ^ 2))
        else:
            side, dev = 1, (1 - p, LAT - 1 - (4 * (g - 10) + 2 * again + half), core)
        return pltpu.make_async_remote_copy(
            src_ref=V.at[e, g],
            dst_ref=R[e][side].at[4 * a + c // 4],
            send_sem=a_send.at[e, again],
            recv_sem=a_recv.at[e, side],
            device_id=dev,
            device_id_type=MESH,
        )

    column_groups = (4, 5, 10, 11)

    def a_start(e):
        for g in column_groups:
            for again in range(2):
                a_copy(e, g, again).start()
        for g in range(ENTRIES):
            if g not in column_groups:
                a_copy(e, g).start()

    def a_wait_send(e):
        for again, count in ((0, ENTRIES), (1, 4)):
            pltpu.make_async_remote_copy(
                src_ref=V.at[e, pl.ds(0, count)],
                dst_ref=R[e][0].at[pl.ds(0, count)],
                send_sem=a_send.at[e, again],
                recv_sem=a_recv.at[e, 0],
                device_id=(1 - p, a, c),
                device_id_type=MESH,
            ).wait_send()

    def a_wait_recv(e, side):
        pltpu.make_async_remote_copy(
            src_ref=R[e][side],
            dst_ref=R[e][side],
            send_sem=a_send.at[e, 0],
            recv_sem=a_recv.at[e, side],
            device_id=(1 - p, a, c),
            device_id_type=MESH,
        ).wait_recv()

    def b_copy(e, side, s, slot, k):
        first, count = (0, 12) if e == 0 else (1, 10)
        return pltpu.make_async_remote_copy(
            src_ref=Q.at[e, side, pl.ds(8 * s + first, count)],
            dst_ref=W[e][side].at[slot, pl.ds(first, count)],
            send_sem=b_send.at[e, side, k],
            recv_sem=b_recv.at[e, side, slot],
            device_id=along(side, s - segment[side]),
            device_id_type=MESH,
        )

    def x_copy(e, side, way):
        return pltpu.make_async_remote_copy(
            src_ref=Q.at[e, side, pl.ds(32 + e if way == 0 else 2, 2 - e)],
            dst_ref=X[e][side].at[way, member[side], pl.ds(e if way == 0 else 0, 2 - e)],
            send_sem=x_send.at[e, side, way],
            recv_sem=x_recv.at[e, side, way],
            device_id=along(side, (4 if way == 0 else -1) - segment[side]),
            device_id_type=MESH,
        )

    def x_wait_recv(e, side, way):
        pltpu.make_async_remote_copy(
            src_ref=X[e][side].at[way, :, pl.ds(e if way == 0 else 0, 2 - e)],
            dst_ref=X[e][side].at[way, :, pl.ds(e if way == 0 else 0, 2 - e)],
            send_sem=x_send.at[e, side, way],
            recv_sem=x_recv.at[e, side, way],
            device_id=along(side, 1),
            device_id_type=MESH,
        ).wait_recv()

    def greet():
        barrier = pltpu.get_barrier_semaphore()

        def hello(dev):
            pl.semaphore_signal(barrier, inc=1, device_id=dev, device_id_type=MESH)

        @pl.loop(0, LON)
        def _(k):
            hello((1 - p, a, k))

        @pl.loop(1, LAT)
        def _(k):
            hello((p, lax.rem(a + k, LAT), c))

        @pl.when(active[0])
        def _():
            @pl.loop(1, LON)
            def _(k):
                hello((p, a, lax.rem(c + k, LON)))

        awaited = jnp.where(active[0], LON + LAT - 1 + LON - 1, LON + LAT - 1)
        for dr, dc in steps:
            if not dc:
                continue
            there = exists(dr, dc)
            awaited += there.astype(jnp.int32)

            @pl.when(there)
            def _():
                hello((p, a + dr, c + dc))

        return lambda: pl.semaphore_wait(barrier, awaited)

    def pass_on():
        @pl.loop(1, LAT)
        def _(k):
            pl.semaphore_signal(
                heard, inc=1, device_id=(p, lax.rem(a + k, LAT), c), device_id_type=MESH
            )

    def flat(e):
        return Y[e].reshape(20 * 20 * NF, NR)

    def interpolate(e, o_far):
        turn = (b + o_far) >> 7
        sub = lax.broadcasted_iota(jnp.int32, (NF, NR), 0)
        first = jnp.logical_or(sub == 1, sub == 4)
        second = jnp.logical_or(sub == 2, sub == 5)
        turned = jnp.logical_or(first, second)

        @pl.loop(0, ENTRIES)
        def _(g):
            i = lax.rem(g - turn + 2 * ENTRIES, ENTRIES)
            r0 = jnp.clip(base[0, i] - a * CB + 1, 1, CB)
            c0 = jnp.clip(base[1, i] - c * CB + 1, 1, CB)
            parts = []
            for x in range(4):
                acc = None
                for y in range(4):
                    term = weight[i, 0, 4 * x + y] * Y[e][r0 + x, c0 + y]
                    acc = term if acc is None else acc + term
                parts.append(acc)
            m = (parts[0] + parts[1]) + (parts[2] + parts[3])
            cosine = trig[0, pl.ds(i, 1), :]
            sine = trig[1, pl.ds(i, 1), :]
            partner = jnp.where(first, -pltpu.roll(m, NF - 1, 0), pltpu.roll(m, 1, 0))
            V[e, g] = jnp.where(turned, cosine * m + sine * partner, m)

    def is_self(side, s):
        here = segment[side] == s
        return here if side == 0 else jnp.logical_and(here, active[1])

    def side_loop(fn, roles):
        for side in range(2):
            @pl.when(roles[side])
            def _():
                fn(side)

    def spread(e, side, o_near):
        shift = (member[side] + o_near) >> 2
        for n in range(36):
            Q[e, side, n] = R[e][side][(n - 2 - shift + LOOP) & 31]
        for way, has in ((0, to_next), (1, to_prev)):
            @pl.when(has[side])
            def _():
                x_copy(e, side, way).start()
        for k in ((2, 3, 1, 0), (1, 0))[side]:
            s = segment[side] ^ k

            @pl.when(jnp.logical_not(is_self(side, s)))
            def _():
                b_copy(e, side, s, member[side], k).start()

        @pl.when(active[side])
        def _():
            for n in range(12):
                W[e][side][member[side], n] = Q[e, side, 8 * segment[side] + n]

    def spread_wait_send(e, side):
        for k in range((4, 2)[side]):
            s = segment[side] ^ k

            @pl.when(jnp.logical_not(is_self(side, s)))
            def _():
                b_copy(e, side, s, member[side], k).wait_send()
        for way, has in ((0, to_next), (1, to_prev)):
            @pl.when(has[side])
            def _():
                x_copy(e, side, way).wait_send()

    def collect(e, side, o_near):
        for s in range(4):
            @pl.when(own_slot[side] != s)
            def _():
                b_copy(e, side, 0, s, 0).wait_recv()
        for way, has, edge in ((0, has_prev, 0), (1, has_next, 3)):
            @pl.when(jnp.logical_and(has[side], segment[side] == edge))
            def _():
                x_wait_recv(e, side, way)

        def place(cell, far_cell):
            for rho in range(4):
                who = (rho - o_near + LOOP) & 3
                for n in range(0 if e == 0 else 1, 12 if e == 0 else 11):
                    value = W[e][side][who, n]
                    if n < 2 or n > 9:
                        way, has, edge = (0, has_prev, 0) if n < 2 else (1, has_next, 3)
                        far_value = jnp.where(has[side], X[e][side][way, who, n if n < 2 else n - 10], 0.0)
                        value = jnp.where(segment[side] == edge, far_value, value)
                    h, o = 2 * n + rho // 2, rho % 2
                    if 1 <= n <= 10:
                        r, q = cell(h - 2, o)
                        Y[e][r, q] = value
                    else:
                        r, q = far_cell(h, o)
                        (ZH, ZV)[side][r, q] = value

        cells = (
            (
                (on_top, lambda h, o: (o, h), lambda h, o: (o, h)),
                (on_bottom, lambda h, o: (18 + o, 19 - h), lambda h, o: (4 + o, 23 - h)),
            ),
            (
                (on_right, lambda h, o: (h, 18 + o), lambda h, o: (h, 4 + o)),
                (on_left, lambda h, o: (19 - h, o), lambda h, o: (23 - h, o)),
            ),
        )[side]
        for on, cell, far_cell in cells:
            @pl.when(on)
            def _():
                place(cell, far_cell)

    def curl(A, ap, am, bb, br, rh):
        a1, a2 = A(1, 0, 0), A(2, 0, 0)
        return (
            ri * ((A(2, 1, 0) * ap - A(2, -1, 0) * am) - (A(1, 0, 1) - A(1, 0, -1)) * bb),
            (A(0, 0, 1) - A(0, 0, -1)) * br - (above(a2) * cp - below(a2) * cm),
            (above(a1) * cp - below(a1) * cm) - (A(0, 1, 0) - A(0, -1, 0)) * rh,
        )

    def first_values(ld, ap, am, bb, br):
        u = [ld(k, 0, 0) for k in range(3)]
        mag = [ld(3 + k, 0, 0) for k in range(3)]
        w = curl(lambda k, dg, dj: ld(k, dg, dj), ap, am, bb, br, rh)
        cur = curl(lambda k, dg, dj: ld(3 + k, dg, dj), ap, am, bb, br, rh)
        ind = cross(u, mag)
        el = [ind[k] - ETA * cur[k] for k in range(3)]
        t = ld(6, 0, 0)
        grad = [
            above(t) * dp - below(t) * dm,
            (ld(6, 1, 0) - ld(6, -1, 0)) * rh,
            (ld(6, 0, 1) - ld(6, 0, -1)) * br,
        ]
        head = ld(7, 0, 0) + np.float32(0.5) * (u[0] * u[0] + u[1] * u[1] + u[2] * u[2])
        return [*w, *cur, *el, *grad, head]

    def second_values(ld, mid, ap, am, bb, br):
        Wv, J, E, T, H = (lambda k, dg, dj, q=q: mid(q + k, dg, dj) for q in (0, 3, 6, 9, 12))
        cw = curl(Wv, ap, am, bb, br, rh)
        ce = curl(E, ap, am, bb, br, rh)
        u = [ld(k, 0, 0) for k in range(3)]
        mag = [ld(3 + k, 0, 0) for k in range(3)]
        w = [Wv(k, 0, 0) for k in range(3)]
        cur = [J(k, 0, 0) for k in range(3)]
        adv, lor = cross(u, w), cross(cur, mag)
        h = H(0, 0, 0)
        slope = (
            above(h) * dp - below(h) * dm,
            (H(0, 1, 0) - H(0, -1, 0)) * rh,
            (H(0, 0, 1) - H(0, 0, -1)) * br,
        )
        t0 = T(0, 0, 0)
        lap = (above(t0) * ep - below(t0) * em) + ri * (
            (T(1, 1, 0) * ap - T(1, -1, 0) * am) + (T(2, 0, 1) - T(2, 0, -1)) * bb
        )
        div = (above(u[0]) * ep - below(u[0]) * em) + ri * (
            (ld(1, 1, 0) * ap - ld(1, -1, 0) * am) + (ld(2, 0, 1) - ld(2, 0, -1)) * bb
        )
        ru = [adv[k] + lor[k] - slope[k] - NU * cw[k] for k in range(3)]
        ru[0] = ru[0] + LIFT * ld(6, 0, 0)
        rt = KAPPA * lap - (u[0] * t0 + u[1] * T(1, 0, 0) + u[2] * T(2, 0, 0))
        return [*ru, *ce, rt, -div]

    def eight(first, step):
        return pl.ds(first, 8) if step == 1 else pl.ds(first, 8, stride=step)

    def factors(i, column):
        if column:
            ap, am, bb = (slopes[k, pl.ds(i + 3, 8), :] for k in range(3))
        else:
            ap, am, bb = (rows_s[k, a * CB + i + 4] for k in range(3))
        return ap, am, bb, ri * bb

    def block_view(e):
        return (
            flat(e), 20, lambda i, j: (i + 2) * 20 + j + 2,
            L1, 24, lambda q, i, j: (q * 18 + i + 1) * 24 + j + 1,
        )

    def row_view(r0):
        return (
            ZH.reshape(6 * 24 * NF, NR), 24, lambda i, j: (i - r0) * 24 + j + 4,
            LZ, 24, lambda q, i, j: (q * 4 + i - r0 - 1) * 24 + j + 3,
        )

    def column_view(c0):
        return (
            ZV.reshape(24 * 6 * NF, NR), 6, lambda i, j: (i + 4) * 6 + j - c0,
            LZ, 4, lambda q, i, j: (q * 24 + i + 3) * 4 + j - c0 - 1,
        )

    def loader(view, i, j, column):
        cells, width, cell = view[:3]
        step = width * NF if column else NF
        return lambda f, dg, dj: cells[eight(cell(i + dg, j + dj) * NF + f, step), :]

    def first_pass(view, i, j, column=False):
        store, width, place = view[3:]
        values = first_values(loader(view, i, j, column), *factors(i, column))
        for q, v in enumerate(values):
            store[eight(place(q, i, j), width if column else 1), :] = v

    def second_pass(e, view, i, j, column=False):
        store, width, place = view[3:]

        def mid(q, dg, dj):
            return store[eight(place(q, i + dg, j + dj), width if column else 1), :]

        sink = keep if e == 0 else finish
        values = second_values(loader(view, i, j, column), mid, *factors(i, column))
        for f, v in enumerate(values):
            sink(i, j, f, v, column)

    def whole(e):
        view = block_view(e)

        @pl.loop(0, 18)
        def _(n):
            for j in (-1, 7, 9):
                first_pass(view, n - 1, j)

        @pl.loop(0, 16)
        def _(i):
            for j in (0, 8):
                second_pass(e, view, i, j)

    row_edge = jnp.where(on_top, -2, CB - 4)
    column_edge = jnp.where(on_left, -2, CB - 4)

    def wide_strips():
        @pl.when(active[0])
        def _():
            wide(0, False, lambda copy: copy.wait_recv())
            ZH[:, pl.ds(2, 20)] = Y0[pl.ds(row_edge + 2, 6)]
            view = row_view(row_edge)
            for n in range(4):
                for j in (-3, 5, 11):
                    first_pass(view, row_edge + 1 + n, j)
            for n in range(2):
                for j in (-2, 6, 10):
                    second_pass(0, view, row_edge + 2 + n, j)

        @pl.when(active[1])
        def _():
            wide(1, False, lambda copy: copy.wait_recv())
            ZV[pl.ds(2, 20)] = Y0[:, pl.ds(column_edge + 2, 6)]
            view = column_view(column_edge)
            for n in range(4):
                for i in (-3, 5, 11):
                    first_pass(view, i, column_edge + 1 + n, True)
            for n in range(2):
                for i in (-2, 6, 10):
                    second_pass(0, view, i, column_edge + 2 + n, True)

    def strips():
        view = block_view(1)

        @pl.when(active[0])
        def _():
            first = jnp.where(on_top, -1, CB - 1)
            for n in range(2):
                for j in (-1, 7, 9):
                    first_pass(view, first + n, j)

        @pl.when(active[1])
        def _():
            first = jnp.where(on_left, -1, CB - 1)
            for n in range(2):
                for i in (-1, 7, 9):
                    first_pass(view, i, first + n, True)

        @pl.when(active[0])
        def _():
            for n in range(2):
                for j in (0, 8):
                    second_pass(1, view, row_edge + 2 + n, j)

        @pl.when(active[1])
        def _():
            for n in range(2):
                for i in (0, 8):
                    second_pass(1, view, i, column_edge + 2 + n, True)

    y_second = flat(1)
    y_first = flat(0)
    out_flat = O.reshape(CB * CB * NF, NR)

    def keep(i, j, f, v, column):
        K1[eight((f * 20 + i + 2) * 24 + j + 4, 24 if column else 1), :] = v
        at = eight(((i + 2) * 20 + j + 2) * NF + f, 20 * NF if column else NF)
        y_second[at, :] = y_first[at, :] + DT * v

    def finish(i, j, f, v, column):
        k1 = K1[eight((f * 20 + i + 2) * 24 + j + 4, 24 if column else 1), :]
        at = eight((i * CB + j) * NF + f, CB * NF if column else NF)
        out_flat[at, :] = np.float32(0.1) * (k1 + v)

    def fetch(k, src, dst):
        copy = pltpu.make_async_copy(src, dst, misc.at[k])
        copy.start()
        return copy

    inner, two = CB - 4, CB - 2
    parts = (
        (2, inner, 2, inner, None),
        (0, 2, 0, CB, jnp.logical_or(on_top, active[1])),
        (two, 2, 0, CB, jnp.logical_or(on_bottom, active[1])),
        (2, inner, 0, 2, on_left),
        (2, inner, two, 2, on_right),
    )

    def store_copy(k):
        r0, rn, c0, cn, _ = parts[k]
        at = (pl.ds(r0, rn), pl.ds(c0, cn))
        return pltpu.make_async_copy(O.at[at], out.at[at], misc.at[10 + k])

    def store(early):
        for k, (*_, reached) in enumerate(parts):
            if reached is None:
                if early:
                    store_copy(k).start()
                continue

            @pl.when(jnp.logical_not(reached) if early else reached)
            def _():
                store_copy(k).start()

    hear = greet()
    corner = target_hbm.at[:, pl.ds(0, 128)]
    local = fetch(0, state, Y0.at[pl.ds(2, CB), pl.ds(2, CB)])
    small = [
        fetch(3, angle_hbm, angle),
        fetch(4, corner, near_at),
        fetch(5, base_hbm, base),
        fetch(6, weight_hbm, weight),
        fetch(7, rows, rows_s),
        fetch(9, levels, levels_s),
    ]
    hear()
    halo_start(0)
    pass_on()
    tell = pltpu.make_async_remote_copy(
        src_ref=corner, dst_ref=far, send_sem=misc.at[1], recv_sem=misc.at[2],
        device_id=(1 - p, a, c), device_id_type=MESH,
    )
    tell.start()
    side_loop(lambda side: wide(side, True, lambda copy: copy.start()), active)

    for copy in small:
        copy.wait()
    ri = levels_s[0:1, :]
    cp, cm = levels_s[1:2, :], levels_s[2:3, :]
    dp, dm = levels_s[3:4, :], levels_s[4:5, :]
    ep, em = levels_s[5:6, :], levels_s[6:7, :]
    rh = ri * H_THETA
    trig[0] = jnp.zeros((16, NR), jnp.float32)
    for i in range(ENTRIES):
        trig[0, i : i + 1, :] = jnp.full((1, NR), angle[0, i], jnp.float32)
    turned = trig[0]
    trig[0] = jnp.cos(turned)
    trig[1] = jnp.sin(turned)

    for i in range(24):
        gi = jnp.minimum(a * CB + i + 1, NTH + 7)
        for k in range(3):
            slopes[k, i : i + 1, :] = jnp.full((1, NR), rows_s[k, gi], jnp.float32)

    tell.wait_recv()
    fetch(8, far, far_at).wait()
    local.wait()
    o_near = loop_place(near_at[0, 0], near_at[1, 0])
    o_far = loop_place(far_at[0, 0], far_at[1, 0])

    for e in range(2):
        if e == 0:
            halo_wait_recv(0)
        else:
            second_halo(False, lambda copy: copy.wait_recv())
        interpolate(e, o_far)
        if e == 0:
            pl.semaphore_wait(heard, LAT - 1)
        a_start(e)
        whole(e)
        if e == 0:
            second_halo(True, lambda copy: copy.start())
        else:
            store(early=True)

        def middle(side):
            a_wait_recv(e, side)
            spread(e, side, o_near)

        side_loop(middle, relays)
        side_loop(lambda side: collect(e, side, o_near), active)
        if e == 0:
            wide_strips()
        else:
            strips()
            store(early=False)

    tell.wait_send()
    for k in range(len(parts)):
        store_copy(k).wait()
    for e in range(2):
        if e == 0:
            halo_wait_send(0)
            side_loop(lambda side: wide(side, True, lambda copy: copy.wait_send()), active)
        else:
            second_halo(True, lambda copy: copy.wait_send())
        a_wait_send(e)
        side_loop(lambda side: spread_wait_send(e, side), relays)


def loop_place(row, col):
    return jnp.where(
        row < 0,
        2 * col + row + 2,
        jnp.where(
            col >= NPH,
            2 * NPH + 2 * row + col - NPH,
            jnp.where(
                row >= NTH,
                2 * NPH + 2 * NTH + 2 * (NPH - 1 - col) + row - NTH,
                4 * NPH + 2 * NTH + 2 * (NTH - 1 - row) + col + 2,
            ),
        ),
    )


def per_device(state, rim_base, rim_weight, rim_angle, rim_target):
    anywhere = pl.BlockSpec(memory_space=pl.ANY)
    f32 = jnp.float32
    result = pl.pallas_call(
        kernel,
        out_shape=jax.ShapeDtypeStruct((CB, CB, NF, NR), f32),
        in_specs=[anywhere] * 7,
        out_specs=anywhere,
        scratch_shapes=[
            pltpu.VMEM((20, 20, NF, NR), f32),
            pltpu.VMEM((20, 20, NF, NR), f32),
            pltpu.VMEM((NF * 20 * 24, NR), f32),
            pltpu.VMEM((13 * 18 * 24, NR), f32),
            pltpu.VMEM((2, ENTRIES, NF, NR), f32),
            *[pltpu.VMEM((32, NF, NR), f32)] * 4,
            pltpu.VMEM((2, 2, 36, NF, NR), f32),
            *[pltpu.VMEM((4, 12, NF, NR), f32)] * 4,
            *[pltpu.VMEM((2, 4, 2, NF, NR), f32)] * 4,
            pltpu.VMEM((6, 24, NF, NR), f32),
            pltpu.VMEM((24, 6, NF, NR), f32),
            pltpu.VMEM((13 * 96 + 8, NR), f32),
            pltpu.VMEM((2, 16, NR), f32),
            pltpu.VMEM((2, 128), jnp.int32),
            pltpu.SMEM((2, ENTRIES), jnp.int32),
            pltpu.SMEM((ENTRIES, 1, 16), f32),
            pltpu.SMEM((1, ENTRIES), f32),
            pltpu.SMEM((2, 128), jnp.int32),
            pltpu.SMEM((2, 128), jnp.int32),
            pltpu.SMEM((3, NTH + 8), f32),
            pltpu.VMEM((8, NR), f32),
            pltpu.VMEM((3, 24, NR), f32),
            pltpu.VMEM((CB, CB, NF, NR), f32),
            pltpu.SemaphoreType.DMA((2, 8)),
            pltpu.SemaphoreType.DMA((2, 8)),
            pltpu.SemaphoreType.DMA((2, 2)),
            pltpu.SemaphoreType.DMA((2, 2)),
            pltpu.SemaphoreType.DMA((2, 2, 4)),
            pltpu.SemaphoreType.DMA((2, 2, 4)),
            pltpu.SemaphoreType.DMA((2, 2, 2)),
            pltpu.SemaphoreType.DMA((2, 2, 2)),
            pltpu.SemaphoreType.DMA((8, 3)),
            pltpu.SemaphoreType.DMA((8, 3)),
            pltpu.SemaphoreType.DMA((2, 2)),
            pltpu.SemaphoreType.DMA((2, 2)),
            pltpu.SemaphoreType.DMA((15,)),
            pltpu.SemaphoreType.REGULAR,
        ],
        compiler_params=pltpu.CompilerParams(
            collective_id=0, has_side_effects=True, vmem_limit_bytes=56 << 20
        ),
    )(
        jnp.asarray(row_table()),
        jnp.asarray(level_table()),
        state[0],
        rim_base[0].T,
        jnp.transpose(rim_weight, (1, 0, 2)),
        rim_angle,
        rim_target[0].T,
    )
    return result[None]


def solution(mesh):
    return jax.shard_map(
        per_device,
        mesh=mesh,
        in_specs=(
            P("panel", "lat", "lon", None, None),
            P("panel", ("lat", "lon"), None),
            P("panel", ("lat", "lon"), None),
            P("panel", ("lat", "lon")),
            P("panel", None, None),
        ),
        out_specs=P("panel", "lat", "lon", None, None),
        check_vma=False,
    )
```

```python
import math

import jax
import jax.numpy as jnp
import numpy as np
from jax import lax
from jax.experimental import pallas as pl
from jax.experimental.pallas import tpu as pltpu
from jax.sharding import PartitionSpec as P

NTH, NPH, NR, NF, CB = 128, 256, 128, 8, 16
LAT, LON = NTH // CB, NPH // CB
LOOP = 1536
ENTRIES = 12
ETA = np.float32(0.2)
NU = np.float32(0.2)
KAPPA = np.float32(0.3)
LIFT = np.float32(0.5)
DT = np.float32(0.2)
MESH = pl.DeviceIdType.MESH

DTHETA = math.pi / (2 * NTH)
DPHI = 1.5 * math.pi / NPH
H_THETA = np.float32(0.5 / DTHETA)


def row_table():
    g = np.arange(-4, NTH + 4)
    sine = lambda k: np.sin(math.pi / 4 + (k + 0.5) * DTHETA)
    s = sine(g)
    half = 0.5 / DTHETA
    return np.stack([sine(g + 1) * half / s, sine(g - 1) * half / s, 0.5 / DPHI / s]).astype(
        np.float32
    )


def level_table():
    scale = 2.0 * NTH / math.pi
    dr = 0.65 * scale / NR
    r = 0.35 * scale + (np.arange(NR) + 0.5) * dr
    half = 0.5 / dr
    up = np.where(np.arange(NR) < NR - 1, half, 0.0)
    down = np.where(np.arange(NR) > 0, half, 0.0)
    r_up, r_down = np.roll(r, -1), np.roll(r, 1)
    rows = [
        1 / r,
        up * r_up / r,
        down * r_down / r,
        up,
        down,
        up * r_up**2 / r**2,
        down * r_down**2 / r**2,
        0 * r,
    ]
    return np.stack(rows).astype(np.float32)


def above(x):
    return pltpu.roll(x, NR - 1, 1)


def below(x):
    return pltpu.roll(x, 1, 1)


def cross(a, b):
    return (
        a[1] * b[2] - a[2] * b[1],
        a[2] * b[0] - a[0] * b[2],
        a[0] * b[1] - a[1] * b[0],
    )


def kernel(
    rows, levels, state, base_hbm, weight_hbm, angle_hbm, target_hbm,
    out,
    Y0, Y1, K1, L1, V,
    R00, R01, R10, R11, Q, W00, W01, W10, W11, X00, X01, X10, X11,
    ZH, ZV, LZ, trig, far, base, weight, angle, near_at, far_at, rows_s, levels_s, slopes, O,
    halo_send, halo_recv, a_send, a_recv, b_send, b_recv, x_send, x_recv, part_send, part_recv, wide_send, wide_recv, misc, heard,
):
    p, a, c = lax.axis_index("panel"), lax.axis_index("lat"), lax.axis_index("lon")
    b = a * LON + c
    Y = (Y0, Y1)
    R = ((R00, R01), (R10, R11))
    W = ((W00, W01), (W10, W11))
    X = ((X00, X01), (X10, X11))

    steps = [(1, 1), (1, -1), (-1, 1), (-1, -1), (1, 0), (-1, 0), (0, 1), (0, -1)]

    def span(step):
        if step == 0:
            return 0, 2, CB
        return (CB - 2, 0, 2) if step > 0 else (0, CB + 2, 2)

    def halo_copy(e, k, part=None):
        dr, dc = steps[k]
        r0, rd, rn = span(dr)
        c0, cd, cn = span(dc)
        if part is not None:
            first, count = ((0, 2), (2, CB - 4), (CB - 2, 2))[part]
            if dr:
                c0, cd, cn = c0 + first, cd + first, count
            else:
                r0, rd, rn = r0 + first, rd + first, count
        if e == 0:
            src = state.at[pl.ds(r0, rn), pl.ds(c0, cn)]
        else:
            src = Y[1].at[pl.ds(r0 + 2, rn), pl.ds(c0 + 2, cn)]
        return pltpu.make_async_remote_copy(
            src_ref=src,
            dst_ref=Y[e].at[pl.ds(rd, rn), pl.ds(cd, cn)],
            send_sem=halo_send.at[e, k] if part is None else part_send.at[k, part],
            recv_sem=halo_recv.at[e, k] if part is None else part_recv.at[k, part],
            device_id=(p, a + dr, c + dc),
            device_id_type=MESH,
        )

    def exists(dr, dc):
        ok = None
        for pos, d, n in ((a, dr, LAT), (c, dc, LON)):
            if d:
                t = (pos < n - 1) if d > 0 else (pos > 0)
                ok = t if ok is None else jnp.logical_and(ok, t)
        return ok

    def halo_start(e):
        for k, (dr, dc) in enumerate(steps):
            @pl.when(exists(dr, dc))
            def _():
                halo_copy(e, k).start()

    def halo_wait_recv(e):
        for k, (dr, dc) in enumerate(steps):
            @pl.when(exists(-dr, -dc))
            def _():
                halo_copy(e, k).wait_recv()

    def halo_wait_send(e):
        for k, (dr, dc) in enumerate(steps):
            @pl.when(exists(dr, dc))
            def _():
                halo_copy(e, k).wait_send()

    def rim_part(dr, dc, part):
        if part == 1:
            return jnp.bool_(False)
        if dc:
            return on_top if part == 0 else on_bottom
        return on_left if part == 0 else on_right

    def second_halo(sending, act):
        for k, (dr, dc) in enumerate(steps):
            there = exists(dr, dc) if sending else exists(-dr, -dc)
            if dr and dc:
                @pl.when(there)
                def _():
                    act(halo_copy(1, k))
                continue
            for part in range(3):
                @pl.when(jnp.logical_and(there, jnp.logical_not(rim_part(dr, dc, part))))
                def _():
                    act(halo_copy(1, k, part))

    on_top, on_bottom = a == 0, a == LAT - 1
    on_right, on_left = c == LON - 1, c == 0
    active = (jnp.logical_or(on_top, on_bottom), jnp.logical_or(on_right, on_left))
    at_right = c >= LON // 2
    sign = (jnp.where(on_top, 1, -1), jnp.where(at_right, 1, -1))
    rank = (jnp.where(on_top, c, LON - 1 - c), jnp.where(at_right, a, LAT - 1 - a))
    groups = (LON // 4, LAT // 4)
    segment = tuple(lax.rem(u, 4) for u in rank)
    has_next = tuple(u // 4 < n - 1 for u, n in zip(rank, groups))
    has_prev = tuple(u // 4 > 0 for u in rank)
    relays = (active[0], jnp.logical_or(c < 2, c >= LON - 2))
    member = (
        lax.rem(c, 4) ^ 2,
        2 * lax.rem(segment[1], 2) + lax.rem(c, 2),
    )
    own_slot = member
    to_next = (has_next[0], jnp.logical_and(has_next[1], segment[1] >= 2))
    to_prev = (has_prev[0], jnp.logical_and(has_prev[1], segment[1] < 2))

    def along(side, step):
        if side == 0:
            return (p, a, c + sign[0] * step)
        return (p, a + sign[1] * step, jnp.where(at_right, LON - 1, 0))

    def wide_copy(side, way):
        first = (jnp.where(on_top, 0, CB - 4), jnp.where(on_left, 0, CB - 4))[side]
        lands = (jnp.where(on_top, 2, 0), jnp.where(on_left, 2, 0))[side]
        near, far_end = (CB - 4, 0) if way > 0 else (2, CB + 6)
        if side == 0:
            src = state.at[pl.ds(first, 4), pl.ds(near, 2)]
            dst = ZH.at[pl.ds(lands, 4), pl.ds(far_end, 2)]
            dev = (p, a, c + way)
        else:
            src = state.at[pl.ds(near, 2), pl.ds(first, 4)]
            dst = ZV.at[pl.ds(far_end, 2), pl.ds(lands, 4)]
            dev = (p, a + way, c)
        k = 0 if way > 0 else 1
        return pltpu.make_async_remote_copy(
            src_ref=src, dst_ref=dst, send_sem=wide_send.at[side, k],
            recv_sem=wide_recv.at[side, k], device_id=dev, device_id_type=MESH,
        )

    def wide(side, sending, act):
        for way in (1, -1):
            step = way if sending else -way
            there = exists(0, step) if side == 0 else exists(step, 0)

            @pl.when(there)
            def _():
                act(wide_copy(side, way))

    m_src = lax.rem(c, 4)

    def a_copy(e, g, again=0):
        half, core = m_src // 2, lax.rem(m_src, 2)
        if g < 4:
            side, dev = 0, (1 - p, 0, 4 * g + (m_src ^ 2))
        elif g < 6:
            side, dev = 1, (1 - p, 4 * (g - 4) + 2 * again + half, LON - 2 + core)
        elif g < 10:
            side, dev = 0, (1 - p, LAT - 1, 4 * (9 - g) + (m_src ^ 2))
        else:
            side, dev = 1, (1 - p, LAT - 1 - (4 * (g - 10) + 2 * again + half), core)
        return pltpu.make_async_remote_copy(
            src_ref=V.at[e, g],
            dst_ref=R[e][side].at[4 * a + c // 4],
            send_sem=a_send.at[e, again],
            recv_sem=a_recv.at[e, side],
            device_id=dev,
            device_id_type=MESH,
        )

    column_groups = (4, 5, 10, 11)

    def a_wait_send(e):
        for again, count in ((0, ENTRIES), (1, 4)):
            pltpu.make_async_remote_copy(
                src_ref=V.at[e, pl.ds(0, count)],
                dst_ref=R[e][0].at[pl.ds(0, count)],
                send_sem=a_send.at[e, again],
                recv_sem=a_recv.at[e, 0],
                device_id=(1 - p, a, c),
                device_id_type=MESH,
            ).wait_send()

    def a_wait_recv(e, side):
        pltpu.make_async_remote_copy(
            src_ref=R[e][side],
            dst_ref=R[e][side],
            send_sem=a_send.at[e, 0],
            recv_sem=a_recv.at[e, side],
            device_id=(1 - p, a, c),
            device_id_type=MESH,
        ).wait_recv()

    def b_copy(e, side, s, slot, k):
        first, count = (0, 12) if e == 0 else (1, 10)
        return pltpu.make_async_remote_copy(
            src_ref=Q.at[e, side, pl.ds(8 * s + first, count)],
            dst_ref=W[e][side].at[slot, pl.ds(first, count)],
            send_sem=b_send.at[e, side, k],
            recv_sem=b_recv.at[e, side, slot],
            device_id=along(side, s - segment[side]),
            device_id_type=MESH,
        )

    def x_copy(e, side, way):
        return pltpu.make_async_remote_copy(
            src_ref=Q.at[e, side, pl.ds(32 + e if way == 0 else 2, 2 - e)],
            dst_ref=X[e][side].at[way, member[side], pl.ds(e if way == 0 else 0, 2 - e)],
            send_sem=x_send.at[e, side, way],
            recv_sem=x_recv.at[e, side, way],
            device_id=along(side, (4 if way == 0 else -1) - segment[side]),
            device_id_type=MESH,
        )

    def x_wait_recv(e, side, way):
        pltpu.make_async_remote_copy(
            src_ref=X[e][side].at[way, :, pl.ds(e if way == 0 else 0, 2 - e)],
            dst_ref=X[e][side].at[way, :, pl.ds(e if way == 0 else 0, 2 - e)],
            send_sem=x_send.at[e, side, way],
            recv_sem=x_recv.at[e, side, way],
            device_id=along(side, 1),
            device_id_type=MESH,
        ).wait_recv()

    def greet():
        barrier = pltpu.get_barrier_semaphore()

        def hello(dev):
            pl.semaphore_signal(barrier, inc=1, device_id=dev, device_id_type=MESH)

        @pl.loop(0, LON)
        def _(k):
            hello((1 - p, a, k))

        @pl.loop(1, LAT)
        def _(k):
            hello((p, lax.rem(a + k, LAT), c))

        @pl.when(active[0])
        def _():
            @pl.loop(1, LON)
            def _(k):
                hello((p, a, lax.rem(c + k, LON)))

        awaited = jnp.where(active[0], LON + LAT - 1 + LON - 1, LON + LAT - 1)
        for dr, dc in steps:
            if not dc:
                continue
            there = exists(dr, dc)
            awaited += there.astype(jnp.int32)

            @pl.when(there)
            def _():
                hello((p, a + dr, c + dc))

        return lambda: pl.semaphore_wait(barrier, awaited)

    def pass_on():
        @pl.loop(1, LAT)
        def _(k):
            pl.semaphore_signal(
                heard, inc=1, device_id=(p, lax.rem(a + k, LAT), c), device_id_type=MESH
            )

    def flat(e):
        return Y[e].reshape(21 * 20 * NF, NR)

    def interpolate(e, o_far):
        turn = (b + o_far) >> 7
        sub = lax.broadcasted_iota(jnp.int32, (NF, NR), 0)
        first = jnp.logical_or(sub == 1, sub == 4)
        second = jnp.logical_or(sub == 2, sub == 5)
        turned = jnp.logical_or(first, second)

        for g in (*column_groups, 0, 3, 6, 9, 1, 2, 7, 8):
            i = lax.rem(g - turn + 2 * ENTRIES, ENTRIES)
            r0 = jnp.clip(base[0, i] - a * CB + 1, 1, CB)
            c0 = jnp.clip(base[1, i] - c * CB + 1, 1, CB)
            parts = []
            for x in range(4):
                acc = None
                for y in range(4):
                    term = weight[i, 0, 4 * x + y] * Y[e][r0 + x, c0 + y]
                    acc = term if acc is None else acc + term
                parts.append(acc)
            m = (parts[0] + parts[1]) + (parts[2] + parts[3])
            cosine = trig[0, pl.ds(i, 1), :]
            sine = trig[1, pl.ds(i, 1), :]
            partner = jnp.where(first, -pltpu.roll(m, NF - 1, 0), pltpu.roll(m, 1, 0))
            V[e, g] = jnp.where(turned, cosine * m + sine * partner, m)
            for again in range(2 if g in column_groups else 1):
                a_copy(e, g, again).start()

    def is_self(side, s):
        here = segment[side] == s
        return here if side == 0 else jnp.logical_and(here, active[1])

    def side_loop(fn, roles):
        for side in range(2):
            @pl.when(roles[side])
            def _():
                fn(side)

    def spread(e, side, o_near):
        shift = (member[side] + o_near) >> 2
        for n in range(36):
            Q[e, side, n] = R[e][side][(n - 2 - shift + LOOP) & 31]
        for way, has in ((0, to_next), (1, to_prev)):
            @pl.when(has[side])
            def _():
                x_copy(e, side, way).start()
        for k in ((2, 3, 1, 0), (1, 0))[side]:
            s = segment[side] ^ k

            @pl.when(jnp.logical_not(is_self(side, s)))
            def _():
                b_copy(e, side, s, member[side], k).start()

        @pl.when(active[side])
        def _():
            for n in range(12):
                W[e][side][member[side], n] = Q[e, side, 8 * segment[side] + n]

    def spread_wait_send(e, side):
        for k in range((4, 2)[side]):
            s = segment[side] ^ k

            @pl.when(jnp.logical_not(is_self(side, s)))
            def _():
                b_copy(e, side, s, member[side], k).wait_send()
        for way, has in ((0, to_next), (1, to_prev)):
            @pl.when(has[side])
            def _():
                x_copy(e, side, way).wait_send()

    def collect(e, side, o_near):
        for s in range(4):
            @pl.when(own_slot[side] != s)
            def _():
                b_copy(e, side, 0, s, 0).wait_recv()
        for way, has, edge in ((0, has_prev, 0), (1, has_next, 3)):
            @pl.when(jnp.logical_and(has[side], segment[side] == edge))
            def _():
                x_wait_recv(e, side, way)

        def place(cell, far_cell):
            for rho in range(4):
                who = (rho - o_near + LOOP) & 3
                for n in range(0 if e == 0 else 1, 12 if e == 0 else 11):
                    value = W[e][side][who, n]
                    if n < 2 or n > 9:
                        way, has, edge = (0, has_prev, 0) if n < 2 else (1, has_next, 3)
                        far_value = jnp.where(has[side], X[e][side][way, who, n if n < 2 else n - 10], 0.0)
                        value = jnp.where(segment[side] == edge, far_value, value)
                    h, o = 2 * n + rho // 2, rho % 2
                    if 1 <= n <= 10:
                        r, q = cell(h - 2, o)
                        Y[e][r, q] = value
                    else:
                        r, q = far_cell(h, o)
                        (ZH, ZV)[side][r, q] = value

        cells = (
            (
                (on_top, lambda h, o: (o, h), lambda h, o: (o, h)),
                (on_bottom, lambda h, o: (18 + o, 19 - h), lambda h, o: (4 + o, 23 - h)),
            ),
            (
                (on_right, lambda h, o: (h, 18 + o), lambda h, o: (h, 4 + o)),
                (on_left, lambda h, o: (19 - h, o), lambda h, o: (23 - h, o)),
            ),
        )[side]
        for on, cell, far_cell in cells:
            @pl.when(on)
            def _():
                place(cell, far_cell)

    def curl(A, ap, am, bb, br, rh):
        a1, a2 = A(1, 0, 0), A(2, 0, 0)
        return (
            ri * ((A(2, 1, 0) * ap - A(2, -1, 0) * am) - (A(1, 0, 1) - A(1, 0, -1)) * bb),
            (A(0, 0, 1) - A(0, 0, -1)) * br - (above(a2) * cp - below(a2) * cm),
            (above(a1) * cp - below(a1) * cm) - (A(0, 1, 0) - A(0, -1, 0)) * rh,
        )

    def first_values(ld, ap, am, bb, br):
        u = [ld(k, 0, 0) for k in range(3)]
        mag = [ld(3 + k, 0, 0) for k in range(3)]
        w = curl(lambda k, dg, dj: ld(k, dg, dj), ap, am, bb, br, rh)
        cur = curl(lambda k, dg, dj: ld(3 + k, dg, dj), ap, am, bb, br, rh)
        ind = cross(u, mag)
        el = [ind[k] - ETA * cur[k] for k in range(3)]
        t = ld(6, 0, 0)
        grad = [
            above(t) * dp - below(t) * dm,
            (ld(6, 1, 0) - ld(6, -1, 0)) * rh,
            (ld(6, 0, 1) - ld(6, 0, -1)) * br,
        ]
        head = ld(7, 0, 0) + np.float32(0.5) * (u[0] * u[0] + u[1] * u[1] + u[2] * u[2])
        return [*w, *cur, *el, *grad, head]

    def second_values(ld, mid, ap, am, bb, br):
        Wv, J, E, T, H = (lambda k, dg, dj, q=q: mid(q + k, dg, dj) for q in (0, 3, 6, 9, 12))
        cw = curl(Wv, ap, am, bb, br, rh)
        ce = curl(E, ap, am, bb, br, rh)
        u = [ld(k, 0, 0) for k in range(3)]
        mag = [ld(3 + k, 0, 0) for k in range(3)]
        w = [Wv(k, 0, 0) for k in range(3)]
        cur = [J(k, 0, 0) for k in range(3)]
        adv, lor = cross(u, w), cross(cur, mag)
        h = H(0, 0, 0)
        slope = (
            above(h) * dp - below(h) * dm,
            (H(0, 1, 0) - H(0, -1, 0)) * rh,
            (H(0, 0, 1) - H(0, 0, -1)) * br,
        )
        t0 = T(0, 0, 0)
        lap = (above(t0) * ep - below(t0) * em) + ri * (
            (T(1, 1, 0) * ap - T(1, -1, 0) * am) + (T(2, 0, 1) - T(2, 0, -1)) * bb
        )
        div = (above(u[0]) * ep - below(u[0]) * em) + ri * (
            (ld(1, 1, 0) * ap - ld(1, -1, 0) * am) + (ld(2, 0, 1) - ld(2, 0, -1)) * bb
        )
        ru = [adv[k] + lor[k] - slope[k] - NU * cw[k] for k in range(3)]
        ru[0] = ru[0] + LIFT * ld(6, 0, 0)
        rt = KAPPA * lap - (u[0] * t0 + u[1] * T(1, 0, 0) + u[2] * T(2, 0, 0))
        return [*ru, *ce, rt, -div]

    def eight(first, step):
        return pl.ds(first, 8) if step == 1 else pl.ds(first, 8, stride=step)

    def factors(i, column):
        if column:
            ap, am, bb = (slopes[k, pl.ds(i + 3, 8), :] for k in range(3))
        else:
            ap, am, bb = (rows_s[k, a * CB + i + 4] for k in range(3))
        return ap, am, bb, ri * bb

    def block_view(e):
        return (
            flat(e), 20, lambda i, j: (i + 2) * 20 + j + 2,
            L1, 24, lambda q, i, j: (q * 18 + i + 1) * 24 + j + 1,
        )

    def row_view(r0):
        return (
            ZH.reshape(6 * 24 * NF, NR), 24, lambda i, j: (i - r0) * 24 + j + 4,
            LZ, 24, lambda q, i, j: (q * 4 + i - r0 - 1) * 24 + j + 3,
        )

    def column_view(c0):
        return (
            ZV.reshape(25 * 6 * NF, NR), 6, lambda i, j: (i + 4) * 6 + j - c0,
            LZ, 4, lambda q, i, j: (q * 24 + i + 3) * 4 + j - c0 - 1,
        )

    def loader(view, i, j, column):
        cells, width, cell = view[:3]
        step = width * NF if column else NF
        return lambda f, dg, dj: cells[eight(cell(i + dg, j + dj) * NF + f, step), :]

    def first_pass(view, i, j, column=False):
        store, width, place = view[3:]
        values = first_values(loader(view, i, j, column), *factors(i, column))
        for q, v in enumerate(values):
            store[eight(place(q, i, j), width if column else 1), :] = v

    def second_pass(e, view, i, j, column=False):
        store, width, place = view[3:]

        def mid(q, dg, dj):
            return store[eight(place(q, i + dg, j + dj), width if column else 1), :]

        sink = keep if e == 0 else finish
        values = second_values(loader(view, i, j, column), mid, *factors(i, column))
        for f, v in enumerate(values):
            sink(i, j, f, v, column)

    def whole(e):
        view = block_view(e)

        @pl.loop(0, 18)
        def _(n):
            for j in (-1, 7, 9):
                first_pass(view, n - 1, j)

        @pl.loop(0, 16)
        def _(i):
            for j in (0, 8):
                second_pass(e, view, i, j)

    row_edge = jnp.where(on_top, -2, CB - 4)
    column_edge = jnp.where(on_left, -2, CB - 4)

    def wide_strips():
        @pl.when(active[0])
        def _():
            wide(0, False, lambda copy: copy.wait_recv())
            ZH[:, pl.ds(2, 20)] = Y0[pl.ds(row_edge + 2, 6)]
            view = row_view(row_edge)
            for n in range(4):
                for j in (-3, 5, 11):
                    first_pass(view, row_edge + 1 + n, j)
            for n in range(2):
                for j in (-2, 6, 10):
                    second_pass(0, view, row_edge + 2 + n, j)

        @pl.when(active[1])
        def _():
            wide(1, False, lambda copy: copy.wait_recv())
            ZV[pl.ds(2, 20)] = Y0[pl.ds(0, 20), pl.ds(column_edge + 2, 6)]
            view = column_view(column_edge)
            for n in range(4):
                for i in (-3, 5, 11):
                    first_pass(view, i, column_edge + 1 + n, True)
            for n in range(2):
                for i in (-2, 6, 10):
                    second_pass(0, view, i, column_edge + 2 + n, True)

    def strips():
        view = block_view(1)

        @pl.when(active[0])
        def _():
            first = jnp.where(on_top, -1, CB - 1)
            for n in range(2):
                for j in (-1, 7, 9):
                    first_pass(view, first + n, j)

        @pl.when(active[1])
        def _():
            first = jnp.where(on_left, -1, CB - 1)
            for n in range(2):
                for i in (-1, 7, 9):
                    first_pass(view, i, first + n, True)

        @pl.when(active[0])
        def _():
            for n in range(2):
                for j in (0, 8):
                    second_pass(1, view, row_edge + 2 + n, j)

        @pl.when(active[1])
        def _():
            for n in range(2):
                for i in (0, 8):
                    second_pass(1, view, i, column_edge + 2 + n, True)

    y_second = flat(1)
    y_first = flat(0)
    out_flat = O.reshape((CB + 1) * CB * NF, NR)

    def keep(i, j, f, v, column):
        K1[eight((f * 20 + i + 2) * 24 + j + 4, 24 if column else 1), :] = v
        at = eight(((i + 2) * 20 + j + 2) * NF + f, 20 * NF if column else NF)
        y_second[at, :] = y_first[at, :] + DT * v

    def finish(i, j, f, v, column):
        k1 = K1[eight((f * 20 + i + 2) * 24 + j + 4, 24 if column else 1), :]
        at = eight((i * CB + j) * NF + f, CB * NF if column else NF)
        out_flat[at, :] = np.float32(0.1) * (k1 + v)

    def fetch(k, src, dst):
        copy = pltpu.make_async_copy(src, dst, misc.at[k])
        copy.start()
        return copy

    inner, two = CB - 4, CB - 2
    parts = (
        (2, inner, 2, inner, None),
        (0, 2, 0, CB, jnp.logical_or(on_top, active[1])),
        (two, 2, 0, CB, jnp.logical_or(on_bottom, active[1])),
        (2, inner, 0, 2, on_left),
        (2, inner, two, 2, on_right),
    )

    def store_copy(k):
        r0, rn, c0, cn, _ = parts[k]
        at = (pl.ds(r0, rn), pl.ds(c0, cn))
        return pltpu.make_async_copy(O.at[at], out.at[at], misc.at[10 + k])

    def store(early):
        for k, (*_, reached) in enumerate(parts):
            if reached is None:
                if early:
                    store_copy(k).start()
                continue

            @pl.when(jnp.logical_not(reached) if early else reached)
            def _():
                store_copy(k).start()

    hear = greet()
    corner = target_hbm.at[:, pl.ds(0, 128)]
    local = fetch(0, state, Y0.at[pl.ds(2, CB), pl.ds(2, CB)])
    small = [
        fetch(3, angle_hbm, angle),
        fetch(4, corner, near_at),
        fetch(5, base_hbm, base),
        fetch(6, weight_hbm, weight),
        fetch(7, rows, rows_s),
        fetch(9, levels, levels_s),
    ]
    hear()
    halo_start(0)
    pass_on()
    tell = pltpu.make_async_remote_copy(
        src_ref=corner, dst_ref=far, send_sem=misc.at[1], recv_sem=misc.at[2],
        device_id=(1 - p, a, c), device_id_type=MESH,
    )
    tell.start()
    side_loop(lambda side: wide(side, True, lambda copy: copy.start()), active)

    for copy in small:
        copy.wait()
    ri = levels_s[0:1, :]
    cp, cm = levels_s[1:2, :], levels_s[2:3, :]
    dp, dm = levels_s[3:4, :], levels_s[4:5, :]
    ep, em = levels_s[5:6, :], levels_s[6:7, :]
    rh = ri * H_THETA
    trig[0] = jnp.zeros((16, NR), jnp.float32)
    for i in range(ENTRIES):
        trig[0, i : i + 1, :] = jnp.full((1, NR), angle[0, i], jnp.float32)
    turned = trig[0]
    trig[0] = jnp.cos(turned)
    trig[1] = jnp.sin(turned)

    for i in range(24):
        gi = jnp.minimum(a * CB + i + 1, NTH + 7)
        for k in range(3):
            slopes[k, i : i + 1, :] = jnp.full((1, NR), rows_s[k, gi], jnp.float32)

    tell.wait_recv()
    fetch(8, far, far_at).wait()
    local.wait()
    o_near = loop_place(near_at[0, 0], near_at[1, 0])
    o_far = loop_place(far_at[0, 0], far_at[1, 0])

    for e in range(2):
        if e == 0:
            halo_wait_recv(0)
        else:
            second_halo(False, lambda copy: copy.wait_recv())
        if e == 0:
            pl.semaphore_wait(heard, LAT - 1)
        interpolate(e, o_far)
        whole(e)
        if e == 0:
            second_halo(True, lambda copy: copy.start())
        else:
            store(early=True)

        def middle(side):
            a_wait_recv(e, side)
            spread(e, side, o_near)

        side_loop(middle, relays)
        side_loop(lambda side: collect(e, side, o_near), active)
        if e == 0:
            wide_strips()
        else:
            strips()
            store(early=False)

    tell.wait_send()
    for k in range(len(parts)):
        store_copy(k).wait()
    for e in range(2):
        if e == 0:
            halo_wait_send(0)
            side_loop(lambda side: wide(side, True, lambda copy: copy.wait_send()), active)
        else:
            second_halo(True, lambda copy: copy.wait_send())
        a_wait_send(e)
        side_loop(lambda side: spread_wait_send(e, side), relays)


def loop_place(row, col):
    return jnp.where(
        row < 0,
        2 * col + row + 2,
        jnp.where(
            col >= NPH,
            2 * NPH + 2 * row + col - NPH,
            jnp.where(
                row >= NTH,
                2 * NPH + 2 * NTH + 2 * (NPH - 1 - col) + row - NTH,
                4 * NPH + 2 * NTH + 2 * (NTH - 1 - row) + col + 2,
            ),
        ),
    )


def per_device(state, rim_base, rim_weight, rim_angle, rim_target):
    anywhere = pl.BlockSpec(memory_space=pl.ANY)
    f32 = jnp.float32
    result = pl.pallas_call(
        kernel,
        out_shape=jax.ShapeDtypeStruct((CB, CB, NF, NR), f32),
        in_specs=[anywhere] * 7,
        out_specs=anywhere,
        scratch_shapes=[
            pltpu.VMEM((21, 20, NF, NR), f32),
            pltpu.VMEM((21, 20, NF, NR), f32),
            pltpu.VMEM((NF * 20 * 24 + 48, NR), f32),
            pltpu.VMEM((13 * 18 * 24 + 48, NR), f32),
            pltpu.VMEM((2, ENTRIES, NF, NR), f32),
            *[pltpu.VMEM((32, NF, NR), f32)] * 4,
            pltpu.VMEM((2, 2, 36, NF, NR), f32),
            *[pltpu.VMEM((4, 12, NF, NR), f32)] * 4,
            *[pltpu.VMEM((2, 4, 2, NF, NR), f32)] * 4,
            pltpu.VMEM((6, 24, NF, NR), f32),
            pltpu.VMEM((25, 6, NF, NR), f32),
            pltpu.VMEM((13 * 96 + 8, NR), f32),
            pltpu.VMEM((2, 16, NR), f32),
            pltpu.VMEM((2, 128), jnp.int32),
            pltpu.SMEM((2, ENTRIES), jnp.int32),
            pltpu.SMEM((ENTRIES, 1, 16), f32),
            pltpu.SMEM((1, ENTRIES), f32),
            pltpu.SMEM((2, 128), jnp.int32),
            pltpu.SMEM((2, 128), jnp.int32),
            pltpu.SMEM((3, NTH + 8), f32),
            pltpu.VMEM((8, NR), f32),
            pltpu.VMEM((3, 24, NR), f32),
            pltpu.VMEM((CB + 1, CB, NF, NR), f32),
            pltpu.SemaphoreType.DMA((2, 8)),
            pltpu.SemaphoreType.DMA((2, 8)),
            pltpu.SemaphoreType.DMA((2, 2)),
            pltpu.SemaphoreType.DMA((2, 2)),
            pltpu.SemaphoreType.DMA((2, 2, 4)),
            pltpu.SemaphoreType.DMA((2, 2, 4)),
            pltpu.SemaphoreType.DMA((2, 2, 2)),
            pltpu.SemaphoreType.DMA((2, 2, 2)),
            pltpu.SemaphoreType.DMA((8, 3)),
            pltpu.SemaphoreType.DMA((8, 3)),
            pltpu.SemaphoreType.DMA((2, 2)),
            pltpu.SemaphoreType.DMA((2, 2)),
            pltpu.SemaphoreType.DMA((15,)),
            pltpu.SemaphoreType.REGULAR,
        ],
        compiler_params=pltpu.CompilerParams(
            collective_id=0, has_side_effects=True, vmem_limit_bytes=56 << 20
        ),
    )(
        jnp.asarray(row_table()),
        jnp.asarray(level_table()),
        state[0],
        rim_base[0].T,
        jnp.transpose(rim_weight, (1, 0, 2)),
        rim_angle,
        rim_target[0].T,
    )
    return result[None]


def solution(mesh):
    return jax.shard_map(
        per_device,
        mesh=mesh,
        in_specs=(
            P("panel", "lat", "lon", None, None),
            P("panel", ("lat", "lon"), None),
            P("panel", ("lat", "lon"), None),
            P("panel", ("lat", "lon")),
            P("panel", None, None),
        ),
        out_specs=P("panel", "lat", "lon", None, None),
        check_vma=False,
    )
```

```python
import math

import jax
import jax.numpy as jnp
import numpy as np
from jax import lax
from jax.experimental import pallas as pl
from jax.experimental.pallas import tpu as pltpu
from jax.sharding import PartitionSpec as P

NTH, NPH, NR, NF, CB = 128, 256, 128, 8, 16
LAT, LON = NTH // CB, NPH // CB
LOOP = 1536
ENTRIES = 12
ETA = np.float32(0.2)
NU = np.float32(0.2)
KAPPA = np.float32(0.3)
LIFT = np.float32(0.5)
DT = np.float32(0.2)
MESH = pl.DeviceIdType.MESH

DTHETA = math.pi / (2 * NTH)
DPHI = 1.5 * math.pi / NPH
H_THETA = np.float32(0.5 / DTHETA)


def row_table():
    g = np.arange(-4, NTH + 4)
    sine = lambda k: np.sin(math.pi / 4 + (k + 0.5) * DTHETA)
    s = sine(g)
    half = 0.5 / DTHETA
    return np.stack([sine(g + 1) * half / s, sine(g - 1) * half / s, 0.5 / DPHI / s]).astype(
        np.float32
    )


def level_table():
    scale = 2.0 * NTH / math.pi
    dr = 0.65 * scale / NR
    r = 0.35 * scale + (np.arange(NR) + 0.5) * dr
    half = 0.5 / dr
    up = np.where(np.arange(NR) < NR - 1, half, 0.0)
    down = np.where(np.arange(NR) > 0, half, 0.0)
    r_up, r_down = np.roll(r, -1), np.roll(r, 1)
    rows = [
        1 / r,
        up * r_up / r,
        down * r_down / r,
        up,
        down,
        up * r_up**2 / r**2,
        down * r_down**2 / r**2,
        0 * r,
    ]
    return np.stack(rows).astype(np.float32)


def above(x):
    return pltpu.roll(x, NR - 1, 1)


def below(x):
    return pltpu.roll(x, 1, 1)


def cross(a, b):
    return (
        a[1] * b[2] - a[2] * b[1],
        a[2] * b[0] - a[0] * b[2],
        a[0] * b[1] - a[1] * b[0],
    )


def kernel(
    rows, levels, state, base_hbm, weight_hbm, angle_hbm, target_hbm,
    out,
    Y0, Y1, K1, L1, V,
    R00, R01, R10, R11, Q, W00, W01, W10, W11, X00, X01, X10, X11,
    ZH, ZV, LZ, trig, far, base, weight, angle, near_at, far_at, rows_s, levels_s, slopes, O,
    halo_send, halo_recv, a_send, a_recv, b_send, b_recv, x_send, x_recv, part_send, part_recv, wide_send, wide_recv, misc, heard,
):
    p, a, c = lax.axis_index("panel"), lax.axis_index("lat"), lax.axis_index("lon")
    b = a * LON + c
    Y = (Y0, Y1)
    R = ((R00, R01), (R10, R11))
    W = ((W00, W01), (W10, W11))
    X = ((X00, X01), (X10, X11))

    steps = [(1, 0), (-1, 0), (1, 1), (1, -1), (-1, 1), (-1, -1), (0, 1), (0, -1)]

    def span(step):
        if step == 0:
            return 0, 2, CB
        return (CB - 2, 0, 2) if step > 0 else (0, CB + 2, 2)

    def halo_copy(e, k, part=None):
        dr, dc = steps[k]
        r0, rd, rn = span(dr)
        c0, cd, cn = span(dc)
        if part is not None:
            first, count = ((0, 2), (2, CB - 4), (CB - 2, 2))[part]
            if dr:
                c0, cd, cn = c0 + first, cd + first, count
            else:
                r0, rd, rn = r0 + first, rd + first, count
        if e == 0:
            src = state.at[pl.ds(r0, rn), pl.ds(c0, cn)]
        else:
            src = Y[1].at[pl.ds(r0 + 2, rn), pl.ds(c0 + 2, cn)]
        return pltpu.make_async_remote_copy(
            src_ref=src,
            dst_ref=Y[e].at[pl.ds(rd, rn), pl.ds(cd, cn)],
            send_sem=halo_send.at[e, k] if part is None else part_send.at[k, part],
            recv_sem=halo_recv.at[e, k] if part is None else part_recv.at[k, part],
            device_id=(p, a + dr, c + dc),
            device_id_type=MESH,
        )

    def exists(dr, dc):
        ok = None
        for pos, d, n in ((a, dr, LAT), (c, dc, LON)):
            if d:
                t = (pos < n - 1) if d > 0 else (pos > 0)
                ok = t if ok is None else jnp.logical_and(ok, t)
        return ok

    def halo_start(e):
        for k, (dr, dc) in enumerate(steps):
            @pl.when(exists(dr, dc))
            def _():
                halo_copy(e, k).start()

    def halo_wait_recv(e):
        for k, (dr, dc) in enumerate(steps):
            @pl.when(exists(-dr, -dc))
            def _():
                halo_copy(e, k).wait_recv()

    def halo_wait_send(e):
        for k, (dr, dc) in enumerate(steps):
            @pl.when(exists(dr, dc))
            def _():
                halo_copy(e, k).wait_send()

    def rim_part(dr, dc, part):
        if part == 1:
            return jnp.bool_(False)
        if dc:
            return on_top if part == 0 else on_bottom
        return on_left if part == 0 else on_right

    def second_halo(sending, act):
        for k, (dr, dc) in enumerate(steps):
            there = exists(dr, dc) if sending else exists(-dr, -dc)
            if dr and dc:
                @pl.when(there)
                def _():
                    act(halo_copy(1, k))
                continue
            for part in range(3):
                @pl.when(jnp.logical_and(there, jnp.logical_not(rim_part(dr, dc, part))))
                def _():
                    act(halo_copy(1, k, part))

    on_top, on_bottom = a == 0, a == LAT - 1
    on_right, on_left = c == LON - 1, c == 0
    active = (jnp.logical_or(on_top, on_bottom), jnp.logical_or(on_right, on_left))
    at_right = c >= LON // 2
    sign = (jnp.where(on_top, 1, -1), jnp.where(at_right, 1, -1))
    rank = (jnp.where(on_top, c, LON - 1 - c), jnp.where(at_right, a, LAT - 1 - a))
    groups = (LON // 4, LAT // 4)
    segment = tuple(lax.rem(u, 4) for u in rank)
    has_next = tuple(u // 4 < n - 1 for u, n in zip(rank, groups))
    has_prev = tuple(u // 4 > 0 for u in rank)
    relays = (active[0], jnp.logical_or(c < 2, c >= LON - 2))
    member = (
        lax.rem(c, 4) ^ 2,
        2 * lax.rem(segment[1], 2) + lax.rem(c, 2),
    )
    own_slot = member
    to_next = (has_next[0], jnp.logical_and(has_next[1], segment[1] >= 2))
    to_prev = (has_prev[0], jnp.logical_and(has_prev[1], segment[1] < 2))

    def along(side, step):
        if side == 0:
            return (p, a, c + sign[0] * step)
        return (p, a + sign[1] * step, jnp.where(at_right, LON - 1, 0))

    def wide_copy(side, way):
        first = (jnp.where(on_top, 0, CB - 4), jnp.where(on_left, 0, CB - 4))[side]
        lands = (jnp.where(on_top, 2, 0), jnp.where(on_left, 2, 0))[side]
        near, far_end = (CB - 4, 0) if way > 0 else (2, CB + 6)
        if side == 0:
            src = state.at[pl.ds(first, 4), pl.ds(near, 2)]
            dst = ZH.at[pl.ds(lands, 4), pl.ds(far_end, 2)]
            dev = (p, a, c + way)
        else:
            src = state.at[pl.ds(near, 2), pl.ds(first, 4)]
            dst = ZV.at[pl.ds(far_end, 2), pl.ds(lands, 4)]
            dev = (p, a + way, c)
        k = 0 if way > 0 else 1
        return pltpu.make_async_remote_copy(
            src_ref=src, dst_ref=dst, send_sem=wide_send.at[side, k],
            recv_sem=wide_recv.at[side, k], device_id=dev, device_id_type=MESH,
        )

    def wide(side, sending, act):
        for way in (1, -1):
            step = way if sending else -way
            there = exists(0, step) if side == 0 else exists(step, 0)

            @pl.when(there)
            def _():
                act(wide_copy(side, way))

    m_src = lax.rem(c, 4)

    def a_copy(e, g, again=0):
        half, core = m_src // 2, lax.rem(m_src, 2)
        if g < 4:
            side, dev = 0, (1 - p, 0, 4 * g + (m_src ^ 2))
        elif g < 6:
            side, dev = 1, (1 - p, 4 * (g - 4) + 2 * again + half, LON - 2 + core)
        elif g < 10:
            side, dev = 0, (1 - p, LAT - 1, 4 * (9 - g) + (m_src ^ 2))
        else:
            side, dev = 1, (1 - p, LAT - 1 - (4 * (g - 10) + 2 * again + half), core)
        return pltpu.make_async_remote_copy(
            src_ref=V.at[e, g],
            dst_ref=R[e][side].at[4 * a + c // 4],
            send_sem=a_send.at[e, again],
            recv_sem=a_recv.at[e, side],
            device_id=dev,
            device_id_type=MESH,
        )

    column_groups = (4, 5, 10, 11)

    def a_wait_send(e):
        for again, count in ((0, ENTRIES), (1, 4)):
            pltpu.make_async_remote_copy(
                src_ref=V.at[e, pl.ds(0, count)],
                dst_ref=R[e][0].at[pl.ds(0, count)],
                send_sem=a_send.at[e, again],
                recv_sem=a_recv.at[e, 0],
                device_id=(1 - p, a, c),
                device_id_type=MESH,
            ).wait_send()

    def a_wait_recv(e, side):
        pltpu.make_async_remote_copy(
            src_ref=R[e][side],
            dst_ref=R[e][side],
            send_sem=a_send.at[e, 0],
            recv_sem=a_recv.at[e, side],
            device_id=(1 - p, a, c),
            device_id_type=MESH,
        ).wait_recv()

    def b_copy(e, side, s, slot, k):
        first, count = (0, 12) if e == 0 else (1, 10)
        return pltpu.make_async_remote_copy(
            src_ref=Q.at[e, side, pl.ds(8 * s + first, count)],
            dst_ref=W[e][side].at[slot, pl.ds(first, count)],
            send_sem=b_send.at[e, side, k],
            recv_sem=b_recv.at[e, side, slot],
            device_id=along(side, s - segment[side]),
            device_id_type=MESH,
        )

    def x_copy(e, side, way):
        return pltpu.make_async_remote_copy(
            src_ref=Q.at[e, side, pl.ds(32 + e if way == 0 else 2, 2 - e)],
            dst_ref=X[e][side].at[way, member[side], pl.ds(e if way == 0 else 0, 2 - e)],
            send_sem=x_send.at[e, side, way],
            recv_sem=x_recv.at[e, side, way],
            device_id=along(side, (4 if way == 0 else -1) - segment[side]),
            device_id_type=MESH,
        )

    def x_wait_recv(e, side, way):
        pltpu.make_async_remote_copy(
            src_ref=X[e][side].at[way, :, pl.ds(e if way == 0 else 0, 2 - e)],
            dst_ref=X[e][side].at[way, :, pl.ds(e if way == 0 else 0, 2 - e)],
            send_sem=x_send.at[e, side, way],
            recv_sem=x_recv.at[e, side, way],
            device_id=along(side, 1),
            device_id_type=MESH,
        ).wait_recv()

    def greet():
        barrier = pltpu.get_barrier_semaphore()

        def hello(dev):
            pl.semaphore_signal(barrier, inc=1, device_id=dev, device_id_type=MESH)

        @pl.loop(0, LON)
        def _(k):
            hello((1 - p, a, k))

        @pl.loop(1, LAT)
        def _(k):
            hello((p, lax.rem(a + k, LAT), c))

        @pl.when(active[0])
        def _():
            @pl.loop(1, LON)
            def _(k):
                hello((p, a, lax.rem(c + k, LON)))

        awaited = jnp.where(active[0], LON + LAT - 1 + LON - 1, LON + LAT - 1)
        for dr, dc in steps:
            if not dc:
                continue
            there = exists(dr, dc)
            awaited += there.astype(jnp.int32)

            @pl.when(there)
            def _():
                hello((p, a + dr, c + dc))

        return lambda: pl.semaphore_wait(barrier, awaited)

    def pass_on():
        @pl.loop(1, LAT)
        def _(k):
            pl.semaphore_signal(
                heard, inc=1, device_id=(p, lax.rem(a + k, LAT), c), device_id_type=MESH
            )

    def flat(e):
        return Y[e].reshape(21 * 20 * NF, NR)

    def interpolate(e, o_far):
        turn = (b + o_far) >> 7
        sub = lax.broadcasted_iota(jnp.int32, (NF, NR), 0)
        first = jnp.logical_or(sub == 1, sub == 4)
        second = jnp.logical_or(sub == 2, sub == 5)
        turned = jnp.logical_or(first, second)

        for g in (*column_groups, 0, 3, 6, 9, 1, 2, 7, 8):
            i = lax.rem(g - turn + 2 * ENTRIES, ENTRIES)
            r0 = jnp.clip(base[0, i] - a * CB + 1, 1, CB)
            c0 = jnp.clip(base[1, i] - c * CB + 1, 1, CB)
            parts = []
            for x in range(4):
                acc = None
                for y in range(4):
                    term = weight[i, 0, 4 * x + y] * Y[e][r0 + x, c0 + y]
                    acc = term if acc is None else acc + term
                parts.append(acc)
            m = (parts[0] + parts[1]) + (parts[2] + parts[3])
            cosine = trig[0, pl.ds(i, 1), :]
            sine = trig[1, pl.ds(i, 1), :]
            partner = jnp.where(first, -pltpu.roll(m, NF - 1, 0), pltpu.roll(m, 1, 0))
            V[e, g] = jnp.where(turned, cosine * m + sine * partner, m)
            for again in range(2 if g in column_groups else 1):
                a_copy(e, g, again).start()

    def is_self(side, s):
        here = segment[side] == s
        return here if side == 0 else jnp.logical_and(here, active[1])

    def side_loop(fn, roles):
        for side in range(2):
            @pl.when(roles[side])
            def _():
                fn(side)

    def spread(e, side, o_near):
        shift = (member[side] + o_near) >> 2
        for n in range(36):
            Q[e, side, n] = R[e][side][(n - 2 - shift + LOOP) & 31]
        for way, has in ((0, to_next), (1, to_prev)):
            @pl.when(has[side])
            def _():
                x_copy(e, side, way).start()
        for k in ((2, 3, 1, 0), (1, 0))[side]:
            s = segment[side] ^ k

            @pl.when(jnp.logical_not(is_self(side, s)))
            def _():
                b_copy(e, side, s, member[side], k).start()

        @pl.when(active[side])
        def _():
            for n in range(12):
                W[e][side][member[side], n] = Q[e, side, 8 * segment[side] + n]

    def spread_wait_send(e, side):
        for k in range((4, 2)[side]):
            s = segment[side] ^ k

            @pl.when(jnp.logical_not(is_self(side, s)))
            def _():
                b_copy(e, side, s, member[side], k).wait_send()
        for way, has in ((0, to_next), (1, to_prev)):
            @pl.when(has[side])
            def _():
                x_copy(e, side, way).wait_send()

    def collect(e, side, o_near):
        for s in range(4):
            @pl.when(own_slot[side] != s)
            def _():
                b_copy(e, side, 0, s, 0).wait_recv()
        for way, has, edge in ((0, has_prev, 0), (1, has_next, 3)):
            @pl.when(jnp.logical_and(has[side], segment[side] == edge))
            def _():
                x_wait_recv(e, side, way)

        def place(cell, far_cell):
            for rho in range(4):
                who = (rho - o_near + LOOP) & 3
                for n in range(0 if e == 0 else 1, 12 if e == 0 else 11):
                    value = W[e][side][who, n]
                    if n < 2 or n > 9:
                        way, has, edge = (0, has_prev, 0) if n < 2 else (1, has_next, 3)
                        far_value = jnp.where(has[side], X[e][side][way, who, n if n < 2 else n - 10], 0.0)
                        value = jnp.where(segment[side] == edge, far_value, value)
                    h, o = 2 * n + rho // 2, rho % 2
                    if 1 <= n <= 10:
                        r, q = cell(h - 2, o)
                        Y[e][r, q] = value
                    else:
                        r, q = far_cell(h, o)
                        (ZH, ZV)[side][r, q] = value

        cells = (
            (
                (on_top, lambda h, o: (o, h), lambda h, o: (o, h)),
                (on_bottom, lambda h, o: (18 + o, 19 - h), lambda h, o: (4 + o, 23 - h)),
            ),
            (
                (on_right, lambda h, o: (h, 18 + o), lambda h, o: (h, 4 + o)),
                (on_left, lambda h, o: (19 - h, o), lambda h, o: (23 - h, o)),
            ),
        )[side]
        for on, cell, far_cell in cells:
            @pl.when(on)
            def _():
                place(cell, far_cell)

    def curl(A, ap, am, bb, br, rh):
        a1, a2 = A(1, 0, 0), A(2, 0, 0)
        return (
            ri * ((A(2, 1, 0) * ap - A(2, -1, 0) * am) - (A(1, 0, 1) - A(1, 0, -1)) * bb),
            (A(0, 0, 1) - A(0, 0, -1)) * br - (above(a2) * cp - below(a2) * cm),
            (above(a1) * cp - below(a1) * cm) - (A(0, 1, 0) - A(0, -1, 0)) * rh,
        )

    def first_values(ld, ap, am, bb, br):
        u = [ld(k, 0, 0) for k in range(3)]
        mag = [ld(3 + k, 0, 0) for k in range(3)]
        w = curl(lambda k, dg, dj: ld(k, dg, dj), ap, am, bb, br, rh)
        cur = curl(lambda k, dg, dj: ld(3 + k, dg, dj), ap, am, bb, br, rh)
        ind = cross(u, mag)
        el = [ind[k] - ETA * cur[k] for k in range(3)]
        t = ld(6, 0, 0)
        grad = [
            above(t) * dp - below(t) * dm,
            (ld(6, 1, 0) - ld(6, -1, 0)) * rh,
            (ld(6, 0, 1) - ld(6, 0, -1)) * br,
        ]
        head = ld(7, 0, 0) + np.float32(0.5) * (u[0] * u[0] + u[1] * u[1] + u[2] * u[2])
        return [*w, *cur, *el, *grad, head]

    def second_values(ld, mid, ap, am, bb, br):
        Wv, J, E, T, H = (lambda k, dg, dj, q=q: mid(q + k, dg, dj) for q in (0, 3, 6, 9, 12))
        cw = curl(Wv, ap, am, bb, br, rh)
        ce = curl(E, ap, am, bb, br, rh)
        u = [ld(k, 0, 0) for k in range(3)]
        mag = [ld(3 + k, 0, 0) for k in range(3)]
        w = [Wv(k, 0, 0) for k in range(3)]
        cur = [J(k, 0, 0) for k in range(3)]
        adv, lor = cross(u, w), cross(cur, mag)
        h = H(0, 0, 0)
        slope = (
            above(h) * dp - below(h) * dm,
            (H(0, 1, 0) - H(0, -1, 0)) * rh,
            (H(0, 0, 1) - H(0, 0, -1)) * br,
        )
        t0 = T(0, 0, 0)
        lap = (above(t0) * ep - below(t0) * em) + ri * (
            (T(1, 1, 0) * ap - T(1, -1, 0) * am) + (T(2, 0, 1) - T(2, 0, -1)) * bb
        )
        div = (above(u[0]) * ep - below(u[0]) * em) + ri * (
            (ld(1, 1, 0) * ap - ld(1, -1, 0) * am) + (ld(2, 0, 1) - ld(2, 0, -1)) * bb
        )
        ru = [adv[k] + lor[k] - slope[k] - NU * cw[k] for k in range(3)]
        ru[0] = ru[0] + LIFT * ld(6, 0, 0)
        rt = KAPPA * lap - (u[0] * t0 + u[1] * T(1, 0, 0) + u[2] * T(2, 0, 0))
        return [*ru, *ce, rt, -div]

    def eight(first, step):
        return pl.ds(first, 8) if step == 1 else pl.ds(first, 8, stride=step)

    def factors(i, column):
        if column:
            ap, am, bb = (slopes[k, pl.ds(i + 3, 8), :] for k in range(3))
        else:
            ap, am, bb = (rows_s[k, a * CB + i + 4] for k in range(3))
        return ap, am, bb, ri * bb

    def block_view(e):
        return (
            flat(e), 20, lambda i, j: (i + 2) * 20 + j + 2,
            L1, 24, lambda q, i, j: (q * 18 + i + 1) * 24 + j + 1,
        )

    def row_view(r0):
        return (
            ZH.reshape(6 * 24 * NF, NR), 24, lambda i, j: (i - r0) * 24 + j + 4,
            LZ, 24, lambda q, i, j: (q * 4 + i - r0 - 1) * 24 + j + 3,
        )

    def column_view(c0):
        return (
            ZV.reshape(25 * 6 * NF, NR), 6, lambda i, j: (i + 4) * 6 + j - c0,
            LZ, 4, lambda q, i, j: (q * 24 + i + 3) * 4 + j - c0 - 1,
        )

    def loader(view, i, j, column):
        cells, width, cell = view[:3]
        step = width * NF if column else NF
        return lambda f, dg, dj: cells[eight(cell(i + dg, j + dj) * NF + f, step), :]

    def first_pass(view, i, j, column=False):
        store, width, place = view[3:]
        values = first_values(loader(view, i, j, column), *factors(i, column))
        for q, v in enumerate(values):
            store[eight(place(q, i, j), width if column else 1), :] = v

    def second_pass(e, view, i, j, column=False):
        store, width, place = view[3:]

        def mid(q, dg, dj):
            return store[eight(place(q, i + dg, j + dj), width if column else 1), :]

        sink = keep if e == 0 else finish
        values = second_values(loader(view, i, j, column), mid, *factors(i, column))
        for f, v in enumerate(values):
            sink(i, j, f, v, column)

    def whole(e):
        view = block_view(e)

        @pl.loop(0, 18)
        def _(n):
            for j in (-1, 7, 9):
                first_pass(view, n - 1, j)

        @pl.loop(0, 16)
        def _(i):
            for j in (0, 8):
                second_pass(e, view, i, j)

    row_edge = jnp.where(on_top, -2, CB - 4)
    column_edge = jnp.where(on_left, -2, CB - 4)

    def wide_strips():
        @pl.when(active[0])
        def _():
            wide(0, False, lambda copy: copy.wait_recv())
            ZH[:, pl.ds(2, 20)] = Y0[pl.ds(row_edge + 2, 6)]
            view = row_view(row_edge)
            for n in range(4):
                for j in (-3, 5, 11):
                    first_pass(view, row_edge + 1 + n, j)
            for n in range(2):
                for j in (-2, 6, 10):
                    second_pass(0, view, row_edge + 2 + n, j)

        @pl.when(active[1])
        def _():
            wide(1, False, lambda copy: copy.wait_recv())
            ZV[pl.ds(2, 20)] = Y0[pl.ds(0, 20), pl.ds(column_edge + 2, 6)]
            view = column_view(column_edge)
            for n in range(4):
                for i in (-3, 5, 11):
                    first_pass(view, i, column_edge + 1 + n, True)
            for n in range(2):
                for i in (-2, 6, 10):
                    second_pass(0, view, i, column_edge + 2 + n, True)

    def strips():
        view = block_view(1)

        @pl.when(active[0])
        def _():
            first = jnp.where(on_top, -1, CB - 1)
            for n in range(2):
                for j in (-1, 7, 9):
                    first_pass(view, first + n, j)

        @pl.when(active[1])
        def _():
            first = jnp.where(on_left, -1, CB - 1)
            for n in range(2):
                for i in (-1, 7, 9):
                    first_pass(view, i, first + n, True)

        @pl.when(active[0])
        def _():
            for n in range(2):
                for j in (0, 8):
                    second_pass(1, view, row_edge + 2 + n, j)

        @pl.when(active[1])
        def _():
            for n in range(2):
                for i in (0, 8):
                    second_pass(1, view, i, column_edge + 2 + n, True)

    y_second = flat(1)
    y_first = flat(0)
    out_flat = O.reshape((CB + 1) * CB * NF, NR)

    def keep(i, j, f, v, column):
        K1[eight((f * 20 + i + 2) * 24 + j + 4, 24 if column else 1), :] = v
        at = eight(((i + 2) * 20 + j + 2) * NF + f, 20 * NF if column else NF)
        y_second[at, :] = y_first[at, :] + DT * v

    def finish(i, j, f, v, column):
        k1 = K1[eight((f * 20 + i + 2) * 24 + j + 4, 24 if column else 1), :]
        at = eight((i * CB + j) * NF + f, CB * NF if column else NF)
        out_flat[at, :] = np.float32(0.1) * (k1 + v)

    def fetch(k, src, dst):
        copy = pltpu.make_async_copy(src, dst, misc.at[k])
        copy.start()
        return copy

    inner, two = CB - 4, CB - 2
    parts = (
        (2, inner, 2, inner, None),
        (0, 2, 0, CB, jnp.logical_or(on_top, active[1])),
        (two, 2, 0, CB, jnp.logical_or(on_bottom, active[1])),
        (2, inner, 0, 2, on_left),
        (2, inner, two, 2, on_right),
    )

    def store_copy(k):
        r0, rn, c0, cn, _ = parts[k]
        at = (pl.ds(r0, rn), pl.ds(c0, cn))
        return pltpu.make_async_copy(O.at[at], out.at[at], misc.at[10 + k])

    def store(early):
        for k, (*_, reached) in enumerate(parts):
            if reached is None:
                if early:
                    store_copy(k).start()
                continue

            @pl.when(jnp.logical_not(reached) if early else reached)
            def _():
                store_copy(k).start()

    hear = greet()
    corner = target_hbm.at[:, pl.ds(0, 128)]
    local = fetch(0, state, Y0.at[pl.ds(2, CB), pl.ds(2, CB)])
    small = [
        fetch(3, angle_hbm, angle),
        fetch(4, corner, near_at),
        fetch(5, base_hbm, base),
        fetch(6, weight_hbm, weight),
        fetch(7, rows, rows_s),
        fetch(9, levels, levels_s),
    ]
    hear()
    halo_start(0)
    pass_on()
    tell = pltpu.make_async_remote_copy(
        src_ref=corner, dst_ref=far, send_sem=misc.at[1], recv_sem=misc.at[2],
        device_id=(1 - p, a, c), device_id_type=MESH,
    )
    tell.start()
    side_loop(lambda side: wide(side, True, lambda copy: copy.start()), active)

    for copy in small:
        copy.wait()
    ri = levels_s[0:1, :]
    cp, cm = levels_s[1:2, :], levels_s[2:3, :]
    dp, dm = levels_s[3:4, :], levels_s[4:5, :]
    ep, em = levels_s[5:6, :], levels_s[6:7, :]
    rh = ri * H_THETA
    trig[0] = jnp.zeros((16, NR), jnp.float32)
    for i in range(ENTRIES):
        trig[0, i : i + 1, :] = jnp.full((1, NR), angle[0, i], jnp.float32)
    turned = trig[0]
    trig[0] = jnp.cos(turned)
    trig[1] = jnp.sin(turned)

    for i in range(24):
        gi = jnp.minimum(a * CB + i + 1, NTH + 7)
        for k in range(3):
            slopes[k, i : i + 1, :] = jnp.full((1, NR), rows_s[k, gi], jnp.float32)

    tell.wait_recv()
    fetch(8, far, far_at).wait()
    local.wait()
    o_near = loop_place(near_at[0, 0], near_at[1, 0])
    o_far = loop_place(far_at[0, 0], far_at[1, 0])

    for e in range(2):
        if e == 0:
            halo_wait_recv(0)
        else:
            second_halo(False, lambda copy: copy.wait_recv())
        if e == 0:
            pl.semaphore_wait(heard, LAT - 1)
        interpolate(e, o_far)
        whole(e)
        if e == 0:
            second_halo(True, lambda copy: copy.start())
        else:
            store(early=True)

        def middle(side):
            a_wait_recv(e, side)
            spread(e, side, o_near)

        side_loop(middle, relays)
        side_loop(lambda side: collect(e, side, o_near), active)
        if e == 0:
            wide_strips()
        else:
            strips()
            store(early=False)

    tell.wait_send()
    for k in range(len(parts)):
        store_copy(k).wait()
    for e in range(2):
        if e == 0:
            halo_wait_send(0)
            side_loop(lambda side: wide(side, True, lambda copy: copy.wait_send()), active)
        else:
            second_halo(True, lambda copy: copy.wait_send())
        a_wait_send(e)
        side_loop(lambda side: spread_wait_send(e, side), relays)


def loop_place(row, col):
    return jnp.where(
        row < 0,
        2 * col + row + 2,
        jnp.where(
            col >= NPH,
            2 * NPH + 2 * row + col - NPH,
            jnp.where(
                row >= NTH,
                2 * NPH + 2 * NTH + 2 * (NPH - 1 - col) + row - NTH,
                4 * NPH + 2 * NTH + 2 * (NTH - 1 - row) + col + 2,
            ),
        ),
    )


def per_device(state, rim_base, rim_weight, rim_angle, rim_target):
    anywhere = pl.BlockSpec(memory_space=pl.ANY)
    f32 = jnp.float32
    result = pl.pallas_call(
        kernel,
        out_shape=jax.ShapeDtypeStruct((CB, CB, NF, NR), f32),
        in_specs=[anywhere] * 7,
        out_specs=anywhere,
        scratch_shapes=[
            pltpu.VMEM((21, 20, NF, NR), f32),
            pltpu.VMEM((21, 20, NF, NR), f32),
            pltpu.VMEM((NF * 20 * 24 + 48, NR), f32),
            pltpu.VMEM((13 * 18 * 24 + 48, NR), f32),
            pltpu.VMEM((2, ENTRIES, NF, NR), f32),
            *[pltpu.VMEM((32, NF, NR), f32)] * 4,
            pltpu.VMEM((2, 2, 36, NF, NR), f32),
            *[pltpu.VMEM((4, 12, NF, NR), f32)] * 4,
            *[pltpu.VMEM((2, 4, 2, NF, NR), f32)] * 4,
            pltpu.VMEM((6, 24, NF, NR), f32),
            pltpu.VMEM((25, 6, NF, NR), f32),
            pltpu.VMEM((13 * 96 + 8, NR), f32),
            pltpu.VMEM((2, 16, NR), f32),
            pltpu.VMEM((2, 128), jnp.int32),
            pltpu.SMEM((2, ENTRIES), jnp.int32),
            pltpu.SMEM((ENTRIES, 1, 16), f32),
            pltpu.SMEM((1, ENTRIES), f32),
            pltpu.SMEM((2, 128), jnp.int32),
            pltpu.SMEM((2, 128), jnp.int32),
            pltpu.SMEM((3, NTH + 8), f32),
            pltpu.VMEM((8, NR), f32),
            pltpu.VMEM((3, 24, NR), f32),
            pltpu.VMEM((CB + 1, CB, NF, NR), f32),
            pltpu.SemaphoreType.DMA((2, 8)),
            pltpu.SemaphoreType.DMA((2, 8)),
            pltpu.SemaphoreType.DMA((2, 2)),
            pltpu.SemaphoreType.DMA((2, 2)),
            pltpu.SemaphoreType.DMA((2, 2, 4)),
            pltpu.SemaphoreType.DMA((2, 2, 4)),
            pltpu.SemaphoreType.DMA((2, 2, 2)),
            pltpu.SemaphoreType.DMA((2, 2, 2)),
            pltpu.SemaphoreType.DMA((8, 3)),
            pltpu.SemaphoreType.DMA((8, 3)),
            pltpu.SemaphoreType.DMA((2, 2)),
            pltpu.SemaphoreType.DMA((2, 2)),
            pltpu.SemaphoreType.DMA((15,)),
            pltpu.SemaphoreType.REGULAR,
        ],
        compiler_params=pltpu.CompilerParams(
            collective_id=0, has_side_effects=True, vmem_limit_bytes=56 << 20
        ),
    )(
        jnp.asarray(row_table()),
        jnp.asarray(level_table()),
        state[0],
        rim_base[0].T,
        jnp.transpose(rim_weight, (1, 0, 2)),
        rim_angle,
        rim_target[0].T,
    )
    return result[None]


def solution(mesh):
    return jax.shard_map(
        per_device,
        mesh=mesh,
        in_specs=(
            P("panel", "lat", "lon", None, None),
            P("panel", ("lat", "lon"), None),
            P("panel", ("lat", "lon"), None),
            P("panel", ("lat", "lon")),
            P("panel", None, None),
        ),
        out_specs=P("panel", "lat", "lon", None, None),
        check_vma=False,
    )
```

```python
import math

import jax
import jax.numpy as jnp
import numpy as np
from jax import lax
from jax.experimental import pallas as pl
from jax.experimental.pallas import tpu as pltpu
from jax.sharding import PartitionSpec as P

NTH, NPH, NR, NF, CB = 128, 256, 128, 8, 16
LAT, LON = NTH // CB, NPH // CB
LOOP = 1536
ENTRIES = 12
ETA = np.float32(0.2)
NU = np.float32(0.2)
KAPPA = np.float32(0.3)
LIFT = np.float32(0.5)
DT = np.float32(0.2)
MESH = pl.DeviceIdType.MESH

DTHETA = math.pi / (2 * NTH)
DPHI = 1.5 * math.pi / NPH
H_THETA = np.float32(0.5 / DTHETA)


def row_table():
    g = np.arange(-4, NTH + 4)
    sine = lambda k: np.sin(math.pi / 4 + (k + 0.5) * DTHETA)
    s = sine(g)
    half = 0.5 / DTHETA
    return np.stack([sine(g + 1) * half / s, sine(g - 1) * half / s, 0.5 / DPHI / s]).astype(
        np.float32
    )


def level_table():
    scale = 2.0 * NTH / math.pi
    dr = 0.65 * scale / NR
    r = 0.35 * scale + (np.arange(NR) + 0.5) * dr
    half = 0.5 / dr
    up = np.where(np.arange(NR) < NR - 1, half, 0.0)
    down = np.where(np.arange(NR) > 0, half, 0.0)
    r_up, r_down = np.roll(r, -1), np.roll(r, 1)
    rows = [
        1 / r,
        up * r_up / r,
        down * r_down / r,
        up,
        down,
        up * r_up**2 / r**2,
        down * r_down**2 / r**2,
        0 * r,
    ]
    return np.stack(rows).astype(np.float32)


def above(x):
    return pltpu.roll(x, NR - 1, 1)


def below(x):
    return pltpu.roll(x, 1, 1)


def cross(a, b):
    return (
        a[1] * b[2] - a[2] * b[1],
        a[2] * b[0] - a[0] * b[2],
        a[0] * b[1] - a[1] * b[0],
    )


def kernel(
    rows, levels, state, base_hbm, weight_hbm, angle_hbm, target_hbm,
    out,
    Y0, Y1, K1, L1, V,
    R00, R01, R10, R11, Q, W00, W01, W10, W11, X00, X01, X10, X11,
    ZH, ZV, LZ, trig, far, base, weight, angle, near_at, far_at, rows_s, levels_s, slopes, O,
    halo_send, halo_recv, a_send, a_recv, b_send, b_recv, x_send, x_recv, part_send, part_recv, wide_send, wide_recv, misc, heard,
):
    p, a, c = lax.axis_index("panel"), lax.axis_index("lat"), lax.axis_index("lon")
    b = a * LON + c
    Y = (Y0, Y1)
    R = ((R00, R01), (R10, R11))
    W = ((W00, W01), (W10, W11))
    X = ((X00, X01), (X10, X11))

    steps = [(1, 0), (-1, 0), (1, 1), (1, -1), (-1, 1), (-1, -1), (0, 1), (0, -1)]

    def span(step):
        if step == 0:
            return 0, 2, CB
        return (CB - 2, 0, 2) if step > 0 else (0, CB + 2, 2)

    def halo_copy(e, k, part=None):
        dr, dc = steps[k]
        r0, rd, rn = span(dr)
        c0, cd, cn = span(dc)
        if part is not None:
            first, count = ((0, 2), (2, CB - 4), (CB - 2, 2))[part]
            if dr:
                c0, cd, cn = c0 + first, cd + first, count
            else:
                r0, rd, rn = r0 + first, rd + first, count
        if e == 0:
            src = state.at[pl.ds(r0, rn), pl.ds(c0, cn)]
        else:
            src = Y[1].at[pl.ds(r0 + 2, rn), pl.ds(c0 + 2, cn)]
        return pltpu.make_async_remote_copy(
            src_ref=src,
            dst_ref=Y[e].at[pl.ds(rd, rn), pl.ds(cd, cn)],
            send_sem=halo_send.at[e, k] if part is None else part_send.at[k, part],
            recv_sem=halo_recv.at[e, k] if part is None else part_recv.at[k, part],
            device_id=(p, a + dr, c + dc),
            device_id_type=MESH,
        )

    def exists(dr, dc):
        ok = None
        for pos, d, n in ((a, dr, LAT), (c, dc, LON)):
            if d:
                t = (pos < n - 1) if d > 0 else (pos > 0)
                ok = t if ok is None else jnp.logical_and(ok, t)
        return ok

    def halo_start(e):
        for k, (dr, dc) in enumerate(steps):
            @pl.when(exists(dr, dc))
            def _():
                halo_copy(e, k).start()

    def halo_wait_recv(e):
        for k, (dr, dc) in enumerate(steps):
            @pl.when(exists(-dr, -dc))
            def _():
                halo_copy(e, k).wait_recv()

    def halo_wait_send(e):
        for k, (dr, dc) in enumerate(steps):
            @pl.when(exists(dr, dc))
            def _():
                halo_copy(e, k).wait_send()

    def rim_part(dr, dc, part):
        if part == 1:
            return jnp.bool_(False)
        if dc:
            return on_top if part == 0 else on_bottom
        return on_left if part == 0 else on_right

    def second_halo(sending, act):
        for k, (dr, dc) in enumerate(steps):
            there = exists(dr, dc) if sending else exists(-dr, -dc)
            if dr and dc:
                @pl.when(there)
                def _():
                    act(halo_copy(1, k))
                continue
            for part in range(3):
                @pl.when(jnp.logical_and(there, jnp.logical_not(rim_part(dr, dc, part))))
                def _():
                    act(halo_copy(1, k, part))

    on_top, on_bottom = a == 0, a == LAT - 1
    on_right, on_left = c == LON - 1, c == 0
    active = (jnp.logical_or(on_top, on_bottom), jnp.logical_or(on_right, on_left))
    at_right = c >= LON // 2
    sign = (jnp.where(on_top, 1, -1), jnp.where(at_right, 1, -1))
    rank = (jnp.where(on_top, c, LON - 1 - c), jnp.where(at_right, a, LAT - 1 - a))
    groups = (LON // 4, LAT // 4)
    segment = tuple(lax.rem(u, 4) for u in rank)
    has_next = tuple(u // 4 < n - 1 for u, n in zip(rank, groups))
    has_prev = tuple(u // 4 > 0 for u in rank)
    relays = (active[0], jnp.logical_or(c < 2, c >= LON - 2))
    member = (
        lax.rem(c, 4) ^ 2,
        2 * lax.rem(segment[1], 2) + lax.rem(c, 2),
    )
    own_slot = member
    to_next = (has_next[0], jnp.logical_and(has_next[1], segment[1] >= 2))
    to_prev = (has_prev[0], jnp.logical_and(has_prev[1], segment[1] < 2))

    def along(side, step):
        if side == 0:
            return (p, a, c + sign[0] * step)
        return (p, a + sign[1] * step, jnp.where(at_right, LON - 1, 0))

    def wide_copy(side, way):
        first = (jnp.where(on_top, 0, CB - 4), jnp.where(on_left, 0, CB - 4))[side]
        lands = (jnp.where(on_top, 2, 0), jnp.where(on_left, 2, 0))[side]
        near, far_end = (CB - 4, 0) if way > 0 else (2, CB + 6)
        if side == 0:
            src = state.at[pl.ds(first, 4), pl.ds(near, 2)]
            dst = ZH.at[pl.ds(lands, 4), pl.ds(far_end, 2)]
            dev = (p, a, c + way)
        else:
            src = state.at[pl.ds(near, 2), pl.ds(first, 4)]
            dst = ZV.at[pl.ds(far_end, 2), pl.ds(lands, 4)]
            dev = (p, a + way, c)
        k = 0 if way > 0 else 1
        return pltpu.make_async_remote_copy(
            src_ref=src, dst_ref=dst, send_sem=wide_send.at[side, k],
            recv_sem=wide_recv.at[side, k], device_id=dev, device_id_type=MESH,
        )

    def wide(side, sending, act):
        for way in (1, -1):
            step = way if sending else -way
            there = exists(0, step) if side == 0 else exists(step, 0)

            @pl.when(there)
            def _():
                act(wide_copy(side, way))

    m_src = lax.rem(c, 4)

    def a_copy(e, g, again=0):
        half, core = m_src // 2, lax.rem(m_src, 2)
        if g < 4:
            side, dev = 0, (1 - p, 0, 4 * g + (m_src ^ 2))
        elif g < 6:
            side, dev = 1, (1 - p, 4 * (g - 4) + 2 * again + half, LON - 2 + core)
        elif g < 10:
            side, dev = 0, (1 - p, LAT - 1, 4 * (9 - g) + (m_src ^ 2))
        else:
            side, dev = 1, (1 - p, LAT - 1 - (4 * (g - 10) + 2 * again + half), core)
        return pltpu.make_async_remote_copy(
            src_ref=V.at[e, g],
            dst_ref=R[e][side].at[4 * a + c // 4],
            send_sem=a_send.at[e, again],
            recv_sem=a_recv.at[e, side],
            device_id=dev,
            device_id_type=MESH,
        )

    column_groups = (4, 5, 10, 11)

    def a_wait_send(e):
        for again, count in ((0, ENTRIES), (1, 4)):
            pltpu.make_async_remote_copy(
                src_ref=V.at[e, pl.ds(0, count)],
                dst_ref=R[e][0].at[pl.ds(0, count)],
                send_sem=a_send.at[e, again],
                recv_sem=a_recv.at[e, 0],
                device_id=(1 - p, a, c),
                device_id_type=MESH,
            ).wait_send()

    def a_wait_recv(e, side):
        pltpu.make_async_remote_copy(
            src_ref=R[e][side],
            dst_ref=R[e][side],
            send_sem=a_send.at[e, 0],
            recv_sem=a_recv.at[e, side],
            device_id=(1 - p, a, c),
            device_id_type=MESH,
        ).wait_recv()

    def b_copy(e, side, s, slot, k):
        first, count = (0, 12) if e == 0 else (1, 10)
        return pltpu.make_async_remote_copy(
            src_ref=Q.at[e, side, pl.ds(8 * s + first, count)],
            dst_ref=W[e][side].at[slot, pl.ds(first, count)],
            send_sem=b_send.at[e, side, k],
            recv_sem=b_recv.at[e, side, slot],
            device_id=along(side, s - segment[side]),
            device_id_type=MESH,
        )

    def x_copy(e, side, way):
        return pltpu.make_async_remote_copy(
            src_ref=Q.at[e, side, pl.ds(32 + e if way == 0 else 2, 2 - e)],
            dst_ref=X[e][side].at[way, member[side], pl.ds(e if way == 0 else 0, 2 - e)],
            send_sem=x_send.at[e, side, way],
            recv_sem=x_recv.at[e, side, way],
            device_id=along(side, (4 if way == 0 else -1) - segment[side]),
            device_id_type=MESH,
        )

    def x_wait_recv(e, side, way):
        pltpu.make_async_remote_copy(
            src_ref=X[e][side].at[way, :, pl.ds(e if way == 0 else 0, 2 - e)],
            dst_ref=X[e][side].at[way, :, pl.ds(e if way == 0 else 0, 2 - e)],
            send_sem=x_send.at[e, side, way],
            recv_sem=x_recv.at[e, side, way],
            device_id=along(side, 1),
            device_id_type=MESH,
        ).wait_recv()

    def greet():
        barrier = pltpu.get_barrier_semaphore()

        def hello(dev):
            pl.semaphore_signal(barrier, inc=1, device_id=dev, device_id_type=MESH)

        @pl.loop(0, LON)
        def _(k):
            hello((1 - p, a, k))

        @pl.loop(1, LAT)
        def _(k):
            hello((p, lax.rem(a + k, LAT), c))

        @pl.when(active[0])
        def _():
            @pl.loop(1, LON)
            def _(k):
                hello((p, a, lax.rem(c + k, LON)))

        awaited = jnp.where(active[0], LON + LAT - 1 + LON - 1, LON + LAT - 1)
        for dr, dc in steps:
            if not dc:
                continue
            there = exists(dr, dc)
            awaited += there.astype(jnp.int32)

            @pl.when(there)
            def _():
                hello((p, a + dr, c + dc))

        return lambda: pl.semaphore_wait(barrier, awaited)

    def pass_on():
        @pl.loop(1, LAT)
        def _(k):
            pl.semaphore_signal(
                heard, inc=1, device_id=(p, lax.rem(a + k, LAT), c), device_id_type=MESH
            )

    def flat(e):
        return Y[e].reshape(21 * 20 * NF, NR)

    def interpolate(e, o_far):
        turn = (b + o_far) >> 7
        sub = lax.broadcasted_iota(jnp.int32, (NF, NR), 0)
        first = jnp.logical_or(sub == 1, sub == 4)
        second = jnp.logical_or(sub == 2, sub == 5)
        turned = jnp.logical_or(first, second)

        for g in (*column_groups, 0, 3, 6, 9, 1, 2, 7, 8):
            i = lax.rem(g - turn + 2 * ENTRIES, ENTRIES)
            r0 = jnp.clip(base[0, i] - a * CB + 1, 1, CB)
            c0 = jnp.clip(base[1, i] - c * CB + 1, 1, CB)
            parts = []
            for x in range(4):
                acc = None
                for y in range(4):
                    term = weight[i, 0, 4 * x + y] * Y[e][r0 + x, c0 + y]
                    acc = term if acc is None else acc + term
                parts.append(acc)
            m = (parts[0] + parts[1]) + (parts[2] + parts[3])
            cosine = trig[0, pl.ds(i, 1), :]
            sine = trig[1, pl.ds(i, 1), :]
            partner = jnp.where(first, -pltpu.roll(m, NF - 1, 0), pltpu.roll(m, 1, 0))
            V[e, g] = jnp.where(turned, cosine * m + sine * partner, m)
            for again in range(2 if g in column_groups else 1):
                a_copy(e, g, again).start()

    def is_self(side, s):
        here = segment[side] == s
        return here if side == 0 else jnp.logical_and(here, active[1])

    def side_loop(fn, roles):
        for side in range(2):
            @pl.when(roles[side])
            def _():
                fn(side)

    def spread(e, side, o_near):
        shift = (member[side] + o_near) >> 2
        def turn(slots):
            for n in slots:
                Q[e, side, n] = R[e][side][(n - 2 - shift + LOOP) & 31]

        ends = (2, 3, 32, 33)
        turn(ends)
        for way, has in ((0, to_next), (1, to_prev)):
            @pl.when(has[side])
            def _():
                x_copy(e, side, way).start()
        turn([n for n in range(36) if n not in ends])
        for k in ((3, 2, 1, 0), (1, 0))[side]:
            s = segment[side] ^ k

            @pl.when(jnp.logical_not(is_self(side, s)))
            def _():
                b_copy(e, side, s, member[side], k).start()

        @pl.when(active[side])
        def _():
            for n in range(12):
                W[e][side][member[side], n] = Q[e, side, 8 * segment[side] + n]

    def spread_wait_send(e, side):
        for k in range((4, 2)[side]):
            s = segment[side] ^ k

            @pl.when(jnp.logical_not(is_self(side, s)))
            def _():
                b_copy(e, side, s, member[side], k).wait_send()
        for way, has in ((0, to_next), (1, to_prev)):
            @pl.when(has[side])
            def _():
                x_copy(e, side, way).wait_send()

    def collect(e, side, o_near):
        for s in range(4):
            @pl.when(own_slot[side] != s)
            def _():
                b_copy(e, side, 0, s, 0).wait_recv()
        for way, has, edge in ((0, has_prev, 0), (1, has_next, 3)):
            @pl.when(jnp.logical_and(has[side], segment[side] == edge))
            def _():
                x_wait_recv(e, side, way)

        def place(cell, far_cell):
            for rho in range(4):
                who = (rho - o_near + LOOP) & 3
                for n in range(0 if e == 0 else 1, 12 if e == 0 else 11):
                    value = W[e][side][who, n]
                    if n < 2 or n > 9:
                        way, has, edge = (0, has_prev, 0) if n < 2 else (1, has_next, 3)
                        far_value = jnp.where(has[side], X[e][side][way, who, n if n < 2 else n - 10], 0.0)
                        value = jnp.where(segment[side] == edge, far_value, value)
                    h, o = 2 * n + rho // 2, rho % 2
                    if 1 <= n <= 10:
                        r, q = cell(h - 2, o)
                        Y[e][r, q] = value
                    else:
                        r, q = far_cell(h, o)
                        (ZH, ZV)[side][r, q] = value

        cells = (
            (
                (on_top, lambda h, o: (o, h), lambda h, o: (o, h)),
                (on_bottom, lambda h, o: (18 + o, 19 - h), lambda h, o: (4 + o, 23 - h)),
            ),
            (
                (on_right, lambda h, o: (h, 18 + o), lambda h, o: (h, 4 + o)),
                (on_left, lambda h, o: (19 - h, o), lambda h, o: (23 - h, o)),
            ),
        )[side]
        for on, cell, far_cell in cells:
            @pl.when(on)
            def _():
                place(cell, far_cell)

    def curl(A, ap, am, bb, br, rh):
        a1, a2 = A(1, 0, 0), A(2, 0, 0)
        return (
            ri * ((A(2, 1, 0) * ap - A(2, -1, 0) * am) - (A(1, 0, 1) - A(1, 0, -1)) * bb),
            (A(0, 0, 1) - A(0, 0, -1)) * br - (above(a2) * cp - below(a2) * cm),
            (above(a1) * cp - below(a1) * cm) - (A(0, 1, 0) - A(0, -1, 0)) * rh,
        )

    def first_values(ld, ap, am, bb, br):
        u = [ld(k, 0, 0) for k in range(3)]
        mag = [ld(3 + k, 0, 0) for k in range(3)]
        w = curl(lambda k, dg, dj: ld(k, dg, dj), ap, am, bb, br, rh)
        cur = curl(lambda k, dg, dj: ld(3 + k, dg, dj), ap, am, bb, br, rh)
        ind = cross(u, mag)
        el = [ind[k] - ETA * cur[k] for k in range(3)]
        t = ld(6, 0, 0)
        grad = [
            above(t) * dp - below(t) * dm,
            (ld(6, 1, 0) - ld(6, -1, 0)) * rh,
            (ld(6, 0, 1) - ld(6, 0, -1)) * br,
        ]
        head = ld(7, 0, 0) + np.float32(0.5) * (u[0] * u[0] + u[1] * u[1] + u[2] * u[2])
        return [*w, *cur, *el, *grad, head]

    def second_values(ld, mid, ap, am, bb, br):
        Wv, J, E, T, H = (lambda k, dg, dj, q=q: mid(q + k, dg, dj) for q in (0, 3, 6, 9, 12))
        cw = curl(Wv, ap, am, bb, br, rh)
        ce = curl(E, ap, am, bb, br, rh)
        u = [ld(k, 0, 0) for k in range(3)]
        mag = [ld(3 + k, 0, 0) for k in range(3)]
        w = [Wv(k, 0, 0) for k in range(3)]
        cur = [J(k, 0, 0) for k in range(3)]
        adv, lor = cross(u, w), cross(cur, mag)
        h = H(0, 0, 0)
        slope = (
            above(h) * dp - below(h) * dm,
            (H(0, 1, 0) - H(0, -1, 0)) * rh,
            (H(0, 0, 1) - H(0, 0, -1)) * br,
        )
        t0 = T(0, 0, 0)
        lap = (above(t0) * ep - below(t0) * em) + ri * (
            (T(1, 1, 0) * ap - T(1, -1, 0) * am) + (T(2, 0, 1) - T(2, 0, -1)) * bb
        )
        div = (above(u[0]) * ep - below(u[0]) * em) + ri * (
            (ld(1, 1, 0) * ap - ld(1, -1, 0) * am) + (ld(2, 0, 1) - ld(2, 0, -1)) * bb
        )
        ru = [adv[k] + lor[k] - slope[k] - NU * cw[k] for k in range(3)]
        ru[0] = ru[0] + LIFT * ld(6, 0, 0)
        rt = KAPPA * lap - (u[0] * t0 + u[1] * T(1, 0, 0) + u[2] * T(2, 0, 0))
        return [*ru, *ce, rt, -div]

    def eight(first, step):
        return pl.ds(first, 8) if step == 1 else pl.ds(first, 8, stride=step)

    def factors(i, column):
        if column:
            ap, am, bb = (slopes[k, pl.ds(i + 3, 8), :] for k in range(3))
        else:
            ap, am, bb = (rows_s[k, a * CB + i + 4] for k in range(3))
        return ap, am, bb, ri * bb

    def block_view(e):
        return (
            flat(e), 20, lambda i, j: (i + 2) * 20 + j + 2,
            L1, 24, lambda q, i, j: (q * 18 + i + 1) * 24 + j + 1,
        )

    def row_view(r0):
        return (
            ZH.reshape(6 * 24 * NF, NR), 24, lambda i, j: (i - r0) * 24 + j + 4,
            LZ, 24, lambda q, i, j: (q * 4 + i - r0 - 1) * 24 + j + 3,
        )

    def column_view(c0):
        return (
            ZV.reshape(25 * 6 * NF, NR), 6, lambda i, j: (i + 4) * 6 + j - c0,
            LZ, 4, lambda q, i, j: (q * 24 + i + 3) * 4 + j - c0 - 1,
        )

    def loader(view, i, j, column):
        cells, width, cell = view[:3]
        step = width * NF if column else NF
        return lambda f, dg, dj: cells[eight(cell(i + dg, j + dj) * NF + f, step), :]

    def first_pass(view, i, j, column=False):
        store, width, place = view[3:]
        values = first_values(loader(view, i, j, column), *factors(i, column))
        for q, v in enumerate(values):
            store[eight(place(q, i, j), width if column else 1), :] = v

    def second_pass(e, view, i, j, column=False):
        store, width, place = view[3:]

        def mid(q, dg, dj):
            return store[eight(place(q, i + dg, j + dj), width if column else 1), :]

        sink = keep if e == 0 else finish
        values = second_values(loader(view, i, j, column), mid, *factors(i, column))
        for f, v in enumerate(values):
            sink(i, j, f, v, column)

    def whole(e):
        view = block_view(e)

        @pl.loop(0, 18)
        def _(n):
            for j in (-1, 7, 9):
                first_pass(view, n - 1, j)

        @pl.loop(0, 16)
        def _(i):
            for j in (0, 8):
                second_pass(e, view, i, j)

    row_edge = jnp.where(on_top, -2, CB - 4)
    column_edge = jnp.where(on_left, -2, CB - 4)

    def wide_strips():
        @pl.when(active[0])
        def _():
            wide(0, False, lambda copy: copy.wait_recv())
            ZH[:, pl.ds(2, 20)] = Y0[pl.ds(row_edge + 2, 6)]
            view = row_view(row_edge)
            for n in range(4):
                for j in (-3, 5, 11):
                    first_pass(view, row_edge + 1 + n, j)
            for n in range(2):
                for j in (-2, 6, 10):
                    second_pass(0, view, row_edge + 2 + n, j)

        @pl.when(active[1])
        def _():
            wide(1, False, lambda copy: copy.wait_recv())
            ZV[pl.ds(2, 20)] = Y0[pl.ds(0, 20), pl.ds(column_edge + 2, 6)]
            view = column_view(column_edge)
            for n in range(4):
                for i in (-3, 5, 11):
                    first_pass(view, i, column_edge + 1 + n, True)
            for n in range(2):
                for i in (-2, 6, 10):
                    second_pass(0, view, i, column_edge + 2 + n, True)

    def strips():
        view = block_view(1)

        @pl.when(active[0])
        def _():
            first = jnp.where(on_top, -1, CB - 1)
            for n in range(2):
                for j in (-1, 7, 9):
                    first_pass(view, first + n, j)

        @pl.when(active[1])
        def _():
            first = jnp.where(on_left, -1, CB - 1)
            for n in range(2):
                for i in (-1, 7, 9):
                    first_pass(view, i, first + n, True)

        @pl.when(active[0])
        def _():
            for n in range(2):
                for j in (0, 8):
                    second_pass(1, view, row_edge + 2 + n, j)

        @pl.when(active[1])
        def _():
            for n in range(2):
                for i in (0, 8):
                    second_pass(1, view, i, column_edge + 2 + n, True)

    y_second = flat(1)
    y_first = flat(0)
    out_flat = O.reshape((CB + 1) * CB * NF, NR)

    def keep(i, j, f, v, column):
        K1[eight((f * 20 + i + 2) * 24 + j + 4, 24 if column else 1), :] = v
        at = eight(((i + 2) * 20 + j + 2) * NF + f, 20 * NF if column else NF)
        y_second[at, :] = y_first[at, :] + DT * v

    def finish(i, j, f, v, column):
        k1 = K1[eight((f * 20 + i + 2) * 24 + j + 4, 24 if column else 1), :]
        at = eight((i * CB + j) * NF + f, CB * NF if column else NF)
        out_flat[at, :] = np.float32(0.1) * (k1 + v)

    def fetch(k, src, dst):
        copy = pltpu.make_async_copy(src, dst, misc.at[k])
        copy.start()
        return copy

    inner, two = CB - 4, CB - 2
    parts = (
        (2, inner, 2, inner, None),
        (0, 2, 0, CB, jnp.logical_or(on_top, active[1])),
        (two, 2, 0, CB, jnp.logical_or(on_bottom, active[1])),
        (2, inner, 0, 2, on_left),
        (2, inner, two, 2, on_right),
    )

    def store_copy(k):
        r0, rn, c0, cn, _ = parts[k]
        at = (pl.ds(r0, rn), pl.ds(c0, cn))
        return pltpu.make_async_copy(O.at[at], out.at[at], misc.at[10 + k])

    def store(early):
        for k, (*_, reached) in enumerate(parts):
            if reached is None:
                if early:
                    store_copy(k).start()
                continue

            @pl.when(jnp.logical_not(reached) if early else reached)
            def _():
                store_copy(k).start()

    hear = greet()
    corner = target_hbm.at[:, pl.ds(0, 128)]
    local = fetch(0, state, Y0.at[pl.ds(2, CB), pl.ds(2, CB)])
    small = [
        fetch(3, angle_hbm, angle),
        fetch(4, corner, near_at),
        fetch(5, base_hbm, base),
        fetch(6, weight_hbm, weight),
        fetch(7, rows, rows_s),
        fetch(9, levels, levels_s),
    ]
    hear()
    halo_start(0)
    pass_on()
    tell = pltpu.make_async_remote_copy(
        src_ref=corner, dst_ref=far, send_sem=misc.at[1], recv_sem=misc.at[2],
        device_id=(1 - p, a, c), device_id_type=MESH,
    )
    tell.start()
    side_loop(lambda side: wide(side, True, lambda copy: copy.start()), active)

    for copy in small:
        copy.wait()
    ri = levels_s[0:1, :]
    cp, cm = levels_s[1:2, :], levels_s[2:3, :]
    dp, dm = levels_s[3:4, :], levels_s[4:5, :]
    ep, em = levels_s[5:6, :], levels_s[6:7, :]
    rh = ri * H_THETA
    trig[0] = jnp.zeros((16, NR), jnp.float32)
    for i in range(ENTRIES):
        trig[0, i : i + 1, :] = jnp.full((1, NR), angle[0, i], jnp.float32)
    turned = trig[0]
    trig[0] = jnp.cos(turned)
    trig[1] = jnp.sin(turned)

    for i in range(24):
        gi = jnp.minimum(a * CB + i + 1, NTH + 7)
        for k in range(3):
            slopes[k, i : i + 1, :] = jnp.full((1, NR), rows_s[k, gi], jnp.float32)

    tell.wait_recv()
    fetch(8, far, far_at).wait()
    local.wait()
    o_near = loop_place(near_at[0, 0], near_at[1, 0])
    o_far = loop_place(far_at[0, 0], far_at[1, 0])

    for e in range(2):
        if e == 0:
            halo_wait_recv(0)
        else:
            second_halo(False, lambda copy: copy.wait_recv())
        if e == 0:
            pl.semaphore_wait(heard, LAT - 1)
        interpolate(e, o_far)
        whole(e)
        if e == 0:
            second_halo(True, lambda copy: copy.start())
        else:
            store(early=True)

        def middle(side):
            a_wait_recv(e, side)
            spread(e, side, o_near)

        side_loop(middle, relays)
        side_loop(lambda side: collect(e, side, o_near), active)
        if e == 0:
            wide_strips()
        else:
            strips()
            store(early=False)

    tell.wait_send()
    for k in range(len(parts)):
        store_copy(k).wait()
    for e in range(2):
        if e == 0:
            halo_wait_send(0)
            side_loop(lambda side: wide(side, True, lambda copy: copy.wait_send()), active)
        else:
            second_halo(True, lambda copy: copy.wait_send())
        a_wait_send(e)
        side_loop(lambda side: spread_wait_send(e, side), relays)


def loop_place(row, col):
    return jnp.where(
        row < 0,
        2 * col + row + 2,
        jnp.where(
            col >= NPH,
            2 * NPH + 2 * row + col - NPH,
            jnp.where(
                row >= NTH,
                2 * NPH + 2 * NTH + 2 * (NPH - 1 - col) + row - NTH,
                4 * NPH + 2 * NTH + 2 * (NTH - 1 - row) + col + 2,
            ),
        ),
    )


def per_device(state, rim_base, rim_weight, rim_angle, rim_target):
    anywhere = pl.BlockSpec(memory_space=pl.ANY)
    f32 = jnp.float32
    result = pl.pallas_call(
        kernel,
        out_shape=jax.ShapeDtypeStruct((CB, CB, NF, NR), f32),
        in_specs=[anywhere] * 7,
        out_specs=anywhere,
        scratch_shapes=[
            pltpu.VMEM((21, 20, NF, NR), f32),
            pltpu.VMEM((21, 20, NF, NR), f32),
            pltpu.VMEM((NF * 20 * 24 + 48, NR), f32),
            pltpu.VMEM((13 * 18 * 24 + 48, NR), f32),
            pltpu.VMEM((2, ENTRIES, NF, NR), f32),
            *[pltpu.VMEM((32, NF, NR), f32)] * 4,
            pltpu.VMEM((2, 2, 36, NF, NR), f32),
            *[pltpu.VMEM((4, 12, NF, NR), f32)] * 4,
            *[pltpu.VMEM((2, 4, 2, NF, NR), f32)] * 4,
            pltpu.VMEM((6, 24, NF, NR), f32),
            pltpu.VMEM((25, 6, NF, NR), f32),
            pltpu.VMEM((13 * 96 + 8, NR), f32),
            pltpu.VMEM((2, 16, NR), f32),
            pltpu.VMEM((2, 128), jnp.int32),
            pltpu.SMEM((2, ENTRIES), jnp.int32),
            pltpu.SMEM((ENTRIES, 1, 16), f32),
            pltpu.SMEM((1, ENTRIES), f32),
            pltpu.SMEM((2, 128), jnp.int32),
            pltpu.SMEM((2, 128), jnp.int32),
            pltpu.SMEM((3, NTH + 8), f32),
            pltpu.VMEM((8, NR), f32),
            pltpu.VMEM((3, 24, NR), f32),
            pltpu.VMEM((CB + 1, CB, NF, NR), f32),
            pltpu.SemaphoreType.DMA((2, 8)),
            pltpu.SemaphoreType.DMA((2, 8)),
            pltpu.SemaphoreType.DMA((2, 2)),
            pltpu.SemaphoreType.DMA((2, 2)),
            pltpu.SemaphoreType.DMA((2, 2, 4)),
            pltpu.SemaphoreType.DMA((2, 2, 4)),
            pltpu.SemaphoreType.DMA((2, 2, 2)),
            pltpu.SemaphoreType.DMA((2, 2, 2)),
            pltpu.SemaphoreType.DMA((8, 3)),
            pltpu.SemaphoreType.DMA((8, 3)),
            pltpu.SemaphoreType.DMA((2, 2)),
            pltpu.SemaphoreType.DMA((2, 2)),
            pltpu.SemaphoreType.DMA((15,)),
            pltpu.SemaphoreType.REGULAR,
        ],
        compiler_params=pltpu.CompilerParams(
            collective_id=0, has_side_effects=True, vmem_limit_bytes=56 << 20
        ),
    )(
        jnp.asarray(row_table()),
        jnp.asarray(level_table()),
        state[0],
        rim_base[0].T,
        jnp.transpose(rim_weight, (1, 0, 2)),
        rim_angle,
        rim_target[0].T,
    )
    return result[None]


def solution(mesh):
    return jax.shard_map(
        per_device,
        mesh=mesh,
        in_specs=(
            P("panel", "lat", "lon", None, None),
            P("panel", ("lat", "lon"), None),
            P("panel", ("lat", "lon"), None),
            P("panel", ("lat", "lon")),
            P("panel", None, None),
        ),
        out_specs=P("panel", "lat", "lon", None, None),
        check_vma=False,
    )
```
